128 devices in a mesh: section: 2 (over z_hi), dp: 4 (over x), tensor: 16 (over z_lo, y, core).
Axes of the slice: x: 4, y: 4, z: 4 (z_hi: 2, z_lo: 2; z = z_hi * 2 + z_lo), core: 2. Of those that a mesh axis runs over, the one named last changes fastest.
Arguments:
- inputs: bfloat16 [2, 512, 8, 1024], P(None, 'tensor', 'dp'), may hold values from -6 to 6
- lengths: int32 [2, 8], P(None, 'dp'), may hold values from 64 to 512, as said below
- cotangent: bfloat16 [2, 512, 8, 1024], P(None, 'tensor', 'dp'), may hold values from -6 to 6
- w_qkv: bfloat16 [2, 1024, 3, 1024], P('section', None, None, 'tensor'), may hold values from -0.1875 to 0.1875
- b_qv: float32 [2, 2, 1024], P('section', None, 'tensor'), may hold values from -3 to 3
- w_out: bfloat16 [2, 1024, 1024], P('section', 'tensor'), may hold values from -3 to 3
- w_up: bfloat16 [2, 1024, 4096], P('section', None, 'tensor'), may hold values from -0.1875 to 0.1875
- b_up: float32 [2, 4096], P('section', 'tensor'), may hold values from -3 to 3
- w_down: bfloat16 [2, 4096, 1024], P('section', 'tensor'), may hold values from -0.09375 to 0.09375
- norm_gains: float32 [2, 2, 1024], P('section'), may hold values from 0.5 to 1.5
- norm_shifts: float32 [2, 2, 1024], P('section'), may hold values from -3 to 3
- out_bias: float32 [2, 2, 1024], P('section'), may hold values from -3 to 3
Outputs:
- layer_out: bfloat16 [2, 2, 512, 8, 1024], P('section', None, 'tensor', 'dp')
- input_grad: float32 [2, 2, 512, 8, 1024], P('section', None, 'tensor', 'dp')
- grad_qkv: float32 [2, 1024, 3, 1024], P('section', None, None, 'tensor')
- grad_qv: float32 [2, 2, 1024], P('section', None, 'tensor')
- grad_out: float32 [2, 1024, 1024], P('section', 'tensor')
- grad_up: float32 [2, 1024, 4096], P('section', None, 'tensor')
- grad_up_bias: float32 [2, 4096], P('section', 'tensor')
- grad_down: float32 [2, 4096, 1024], P('section', 'tensor')
- grad_gains: float32 [2, 2, 1024], P('section')
- grad_shifts: float32 [2, 2, 1024], P('section')
- grad_out_bias: float32 [2, 2, 1024], P('section')
The draws below stay inside these ranges and needn't reach their ends.
Inputs may be any that keep to these rules, and one draw needn't show every extreme that they name: `lengths`: valid positions of each sequence, counted from its start. For each index of dp one of its sequences, in one micro-batch drawn from the seed, has all 512.
All inputs are finite; a program needn't handle non-finite values.
Results may differ from the reference program's by a relative error of at most 0.04.
Values may be sent and summed in bfloat16 or wider, within the bound.
A program may use at most 128 MiB of HBM per device.

```python
import jax
import jax.numpy as jnp
from jax import lax

D = 1024
HEAD = 64
FF = 4096
LEN = 512
MICRO = 2
SEQ_DEV = 2
BATCH = 8
LAYERS = 2


def draw_lengths(key, part):
    key = jax.random.fold_in(key, 7)
    span_key, pick_key = jax.random.split(key)
    span_draw = jax.random.randint(span_key, (MICRO, BATCH), LEN // 8, LEN + 1)
    blocks = BATCH // SEQ_DEV
    picked = jax.random.randint(pick_key, (blocks,), 0, MICRO * SEQ_DEV)
    micro_pos = lax.broadcasted_iota(jnp.int32, (MICRO, BATCH), 0)
    seq_pos = lax.broadcasted_iota(jnp.int32, (MICRO, BATCH), 1)
    chosen = jnp.take(picked, seq_pos // SEQ_DEV)
    full_hit = (micro_pos == chosen // SEQ_DEV) & (seq_pos % SEQ_DEV == chosen % SEQ_DEV)
    return jnp.where(full_hit, LEN, span_draw).astype(jnp.int32)


def shard_levels(key, dims, shards, low, largest):
    factor_of = 1.0
    for dim, parts in shards:
        draws = jax.random.uniform(jax.random.fold_in(jax.random.fold_in(key, 6), dim), (parts,), jnp.float32, low / len(shards), largest / len(shards))
        factor_of = factor_of * jnp.repeat(jnp.exp(draws), dims[dim] // parts).reshape((-1,) + (1,) * (len(dims) - 1 - dim))
    return factor_of


def bell_draw(rng, extent, scale, reach, cuts=(), kind=jnp.bfloat16):
    result = jax.random.normal(rng, extent, jnp.float32) * scale
    if len(cuts) > 0:
        result = shard_levels(rng, extent, cuts, -0.22, 0.18) * result
    return jnp.clip(result, min=-reach, max=reach).astype(kind)


def setup_inputs(seed: int = 0) -> dict:
    key_of = jax.random.split(jax.random.key(seed), 13)
    inputs = bell_draw(key_of[0], (MICRO, LEN, BATCH, D), 1.0, 6.0, ((1, 16), (2, 4)))
    lengths = draw_lengths(jax.random.fold_in(key_of[12], 71), 0)
    cotangent = bell_draw(key_of[2], (MICRO, LEN, BATCH, D), 1.0, 6.0, ((1, 16), (2, 4)))
    w_qkv = bell_draw(key_of[3], (LAYERS, D, 3, D), D ** -0.5, 0.1875, ((0, 2), (3, 16)))
    b_qv = bell_draw(key_of[4], (LAYERS, 2, D), 0.5, 3.0, ((0, 2), (2, 16)), jnp.float32)
    w_out = bell_draw(key_of[5], (LAYERS, D, D), (max(1, 2 * D // LEN)) ** -0.5, 3.0, ((0, 2), (1, 16)))
    w_up = bell_draw(key_of[6], (LAYERS, D, FF), D ** -0.5, 0.1875, ((0, 2), (2, 16)))
    b_up = bell_draw(key_of[7], (LAYERS, FF), 0.5, 3.0, ((0, 2), (1, 16)), jnp.float32)
    w_down = bell_draw(key_of[8], (LAYERS, FF, D), FF ** -0.5, 0.09375, ((0, 2), (1, 16)))
    norm_gains = jnp.clip(1.0 + 0.1 * jax.random.normal(key_of[9], (LAYERS, 2, D), jnp.float32), 0.5, 1.5)
    norm_shifts = bell_draw(key_of[10], (LAYERS, 2, D), 0.5, 3.0, ((0, 2),), jnp.float32)
    out_bias = bell_draw(key_of[11], (LAYERS, 2, D), 0.5, 3.0, ((0, 2),), jnp.float32)
    return dict(inputs=inputs, lengths=lengths, cotangent=cotangent, w_qkv=w_qkv, b_qv=b_qv, w_out=w_out, w_up=w_up, b_up=b_up, w_down=w_down, norm_gains=norm_gains, norm_shifts=norm_shifts, out_bias=out_bias)


EPSILON = 1e-12
MASKED = -1e+30
HIGHEST_PRECISION = lax.Precision.HIGHEST

@jax.custom_vjp
def low(v):
    return lax.optimization_barrier(v.astype(jnp.bfloat16)).astype(jnp.float32)

@jax.custom_vjp
def low_back(v):
    return v

def low_keep(v):
    return (low(v), None)

def low_pass(kept, grad):
    return (grad,)

def back_keep(v):
    return (v, None)

def back_low(kept, grad):
    return (low(grad),)
low.defvjp(low_keep, low_pass)
low_back.defvjp(back_keep, back_low)

def normalize(token_rows, gain, shift):
    center = lax.optimization_barrier(jnp.mean(token_rows, axis=-1, keepdims=True))
    centred = token_rows - center
    spread = lax.optimization_barrier(jnp.mean(centred * centred, axis=-1, keepdims=True))
    return centred * lax.rsqrt(spread + EPSILON) * gain + shift

def block_layer(token_rows, seq_lens, w_qkv, b_qv, w_out, w_up, b_up, w_down, norm_gains, norm_shifts, out_bias):
    token_count, seq_count = (token_rows.shape[0], token_rows.shape[1])
    projected = jnp.einsum('tbd,dch->tbch', token_rows, w_qkv, precision=HIGHEST_PRECISION)
    bias_rows = jnp.stack([b_qv[0], jnp.zeros_like(b_qv[0]), b_qv[1]])
    head_split = low(low_back(projected + bias_rows)).reshape(token_count, seq_count, 3, -1, HEAD)
    query_heads = head_split[:, :, 0]
    key_heads = head_split[:, :, 1]
    value_heads = head_split[:, :, 2]
    logits = jnp.einsum('tbhe,ubhe->bhtu', query_heads, key_heads, precision=HIGHEST_PRECISION) * HEAD ** (-0.5)
    positions = jnp.arange(token_count, dtype=jnp.int32)
    is_valid = positions[None, :] < seq_lens[:, None]
    logits = low_back(jnp.where(is_valid[:, None, None, :], logits, MASKED))
    row_max = lax.optimization_barrier(jnp.max(logits, axis=-1, keepdims=True))
    exp_terms = jnp.exp(logits - row_max)
    prob_low = low(exp_terms / lax.optimization_barrier(jnp.sum(exp_terms, axis=-1, keepdims=True)))
    mixed = jnp.einsum('bhtu,ubhe->tbhe', prob_low, value_heads, precision=HIGHEST_PRECISION)
    mixed = low(low_back(mixed.reshape(token_count, seq_count, -1)))
    attended = low_back(jnp.einsum('tbh,hd->tbd', mixed, w_out, precision=HIGHEST_PRECISION))
    first_sum = token_rows + attended + out_bias[0]
    middle_norm = normalize(first_sum, norm_gains[0], norm_shifts[0])
    pre_act = low_back(jnp.einsum('tbd,df->tbf', low(middle_norm), w_up, precision=HIGHEST_PRECISION) + b_up)
    hidden = low(jax.nn.gelu(pre_act, approximate=False))
    fed_rows = low_back(jnp.einsum('tbf,fd->tbd', hidden, w_down, precision=HIGHEST_PRECISION))
    second_sum = middle_norm + fed_rows + out_bias[1]
    return normalize(second_sum, norm_gains[1], norm_shifts[1])

def reference(inputs, lengths, cotangent, w_qkv, b_qv, w_out, w_up, b_up, w_down, norm_gains, norm_shifts, out_bias):
    micro_count, token_count, seq_count, feature_count = inputs.shape

    def flatten(array):
        moved = jnp.transpose(array, (1, 0, 2, 3))
        return moved.reshape(token_count, micro_count * seq_count, feature_count).astype(jnp.float32)

    def unflatten(array):
        return jnp.transpose(array.reshape(token_count, micro_count, seq_count, feature_count), (1, 0, 2, 3))
    token_rows = flatten(inputs)
    seq_lens = lengths.reshape(micro_count * seq_count).astype(jnp.int32)
    params = tuple((param.astype(jnp.float32) for param in (w_qkv, b_qv, w_out, w_up, b_up, w_down, norm_gains, norm_shifts, out_bias)))
    layer_total = w_qkv.shape[0]
    extras = jnp.zeros((layer_total - 1, token_count, micro_count * seq_count, feature_count), jnp.float32)

    def forward(start_rows, layer_params, extra_terms):
        hidden_state = start_rows
        layer_outs = []
        for layer_index in range(layer_total):
            if layer_index > 0:
                hidden_state = low_back(low(hidden_state)) + extra_terms[layer_index - 1]
            hidden_state = block_layer(hidden_state, seq_lens, *[param[layer_index] for param in layer_params])
            layer_outs.append(hidden_state)
        return jnp.stack(layer_outs)
    layer_outs, pullback = jax.vjp(forward, token_rows, params, extras)
    output_cot = jnp.zeros_like(layer_outs).at[layer_total - 1].set(flatten(cotangent))
    grad_rows, grad_params, grad_extras = pullback(output_cot)
    layer_out = jnp.stack([unflatten(layer_outs[index]) for index in range(layer_total)]).astype(jnp.bfloat16)
    all_grads = jnp.concatenate([grad_rows[None], grad_extras], axis=0)
    input_grad = jnp.stack([unflatten(all_grads[index]) for index in range(layer_total)])
    return (layer_out, input_grad, grad_params[0], grad_params[1], grad_params[2], grad_params[3], grad_params[4], grad_params[5], grad_params[6], grad_params[7], grad_params[8])
```

```python
import jax
import jax.numpy as jnp
from jax import lax
from jax.experimental import pallas as pl
from jax.experimental.pallas import tpu as pltpu
from jax.sharding import PartitionSpec as P

EPSILON = 1e-12
MASKED = -1e30
F32 = jnp.float32
BF16 = jnp.bfloat16
MESH = pl.DeviceIdType.MESH
INV_SQRT2 = 0.7071067811865476
INV_SQRT_2PI = 0.3989422804014327
SCALE = 0.125

PIECES_A = ((0, 64), (64, 64), (128, 64), (192, 64))
PIECES_F = ((256, 128), (384, 128), (512, 128), (640, 128))


def nt(a, b):
    return lax.dot_general(a, b, (((1,), (1,)), ((), ())), preferred_element_type=F32)


def nn(a, b):
    return lax.dot_general(a, b, (((1,), (0,)), ((), ())), preferred_element_type=F32)


def standardize(rows):
    center = jnp.mean(rows, axis=-1, keepdims=True)
    centred = rows - center
    spread = jnp.mean(centred * centred, axis=-1, keepdims=True)
    inv = lax.rsqrt(spread + EPSILON)
    return centred * inv, inv


def standardize_back(grad_out, gain, unit, inv):
    scaled = grad_out * gain
    return inv * (
        scaled
        - jnp.mean(scaled, axis=-1, keepdims=True)
        - unit * jnp.mean(scaled * unit, axis=-1, keepdims=True)
    )


def kernel(
    xs, cs, wb, sv, valid,
    lout, igout, gout, smout,
    W, SW, XF, YF, GF, GO, CT, PB, PT, PR, AT, HT, GD, GZT, GPT, GKT, GVT,
    N1, N2, S1, S2, Y1, GR, GY, OWN,
    PART, SIB, SUM, RIN, G, PIN, XIN, FIN, XIF, XIA,
    LO, IG, SM, SMC, SM1, SMY, SM2, SMZ, SM3, SMX,
    ag_s, ag_r, sb_s, sb_r, rs_s, rs_r, in_s, in_r, loc, w_sp, w_sc, w_sf, w_r,
    gp_s, gp_r, gc_s, gc_r, xr_s, xr_r, xg_s, xg_r, lo_s, lo_r, ig_s, ig_r,
    sc_s, sc_r, sy_s, sy_r, sz_s, sz_r, sx_s, sx_r,
):
    zh = lax.axis_index("section")
    x = lax.axis_index("dp")
    t = lax.axis_index("tensor")
    zl = t // 8
    y = (t % 8) // 2
    c = t % 2
    d = t % 8
    z = 2 * zh + zl

    def dev(zh_=None, x_=None, zl_=None, y_=None, c_=None):
        zh_ = zh if zh_ is None else zh_
        x_ = x if x_ is None else x_
        zl_ = zl if zl_ is None else zl_
        y_ = y if y_ is None else y_
        c_ = c if c_ is None else c_
        return (zh_, x_, zl_ * 8 + y_ * 2 + c_)

    def yd(r):
        return dev(y_=lax.rem(y + r, 4))

    def xd(r):
        return dev(x_=lax.rem(x + r, 4))

    sibling = dev(c_=1 - c)
    partner = dev(zl_=1 - zl)
    cross = dev(zh_=1 - zh, zl_=1 - zl)
    far = dev(zh_=1 - zh)

    def rc(src, dst, ssem, rsem, where):
        return pltpu.make_async_remote_copy(
            src_ref=src, dst_ref=dst, send_sem=ssem, recv_sem=rsem, device_id=where, device_id_type=MESH
        )

    def arrived(dst, rsem):
        rc(dst, dst, rsem, rsem, sibling).wait_recv()

    barrier = pltpu.get_barrier_semaphore()
    greeted = [sibling, yd(1), yd(2), yd(3), xd(1), xd(2), xd(3), partner, cross, far]
    for other in greeted:
        pl.semaphore_signal(barrier, inc=1, device_id=other, device_id_type=MESH)
    pl.semaphore_wait(barrier, len(greeted))

    def slot(full, l, yy, cc, half=None):
        if half is None:
            return full.at[l, pl.ds(pl.multiple_of(yy * 128 + cc * 64, 64), 64)]
        return full.at[l, pl.ds(pl.multiple_of(yy * 128 + cc * 64 + half * 32, 32), 32)]

    def ring_ag_start(own, where, s_s, s_r):
        copies = [
            rc(own(0), own(0), s_s(0), s_r(0), where(1)),
            rc(own(1), own(1), s_s(3), s_r(3), where(3)),
            rc(own(1), own(1), s_s(1), s_r(1), where(1)),
            rc(own(0), own(0), s_s(2), s_r(2), where(3)),
        ]
        for cp in copies:
            cp.start()
        return copies

    def ring_ag_finish(slot_of, where, s_s, s_r, landed):
        copies = []
        arrived(slot_of(3, 0), s_r(0))
        cp = rc(slot_of(3, 0), slot_of(3, 0), s_s(4), s_r(4), where(1))
        cp.start()
        copies.append(cp)
        landed(0, 3, 0)
        arrived(slot_of(1, 1), s_r(3))
        cp = rc(slot_of(1, 1), slot_of(1, 1), s_s(5), s_r(5), where(3))
        cp.start()
        copies.append(cp)
        landed(3, 1, 1)
        for k, r, h in ((1, 3, 1), (2, 1, 0), (4, 2, 0), (5, 2, 1)):
            arrived(slot_of(r, h), s_r(k))
            landed(k, r, h)
        return copies

    def gather(full, l, k):
        def at(r, half):
            return slot(full, l, lax.rem(y + r, 4), c, half)

        def s_s(i):
            return ag_s.at[l, k, i]

        def s_r(i):
            return ag_r.at[l, k, i]

        copies = ring_ag_start(lambda half: at(0, half), yd, s_s, s_r)
        mine = slot(full, l, y, c)
        cp = rc(mine, mine, s_s(6), s_r(6), sibling)
        cp.start()
        copies.append(cp)

        def landed(i, r, half):
            got = at(r, half)
            cp = rc(got, got, s_s(7 + i), s_r(7 + i), sibling)
            cp.start()
            copies.append(cp)

        copies += ring_ag_finish(at, yd, s_s, s_r, landed)
        arrived(slot(full, l, y, 1 - c), s_r(6))
        for i, r, half in ((0, 3, 0), (3, 1, 1), (1, 3, 1), (2, 1, 0), (4, 2, 0), (5, 2, 1)):
            arrived(slot(full, l, lax.rem(y + r, 4), 1 - c, half), s_r(7 + i))
        for cp in copies:
            cp.wait_send()

    def rs_two(part, inbox, where, s_s, s_r, h):
        a = rc(part.at[pl.ds(0, h)], inbox.at[0], s_s(0), s_r(0), where(1))
        b = rc(part.at[pl.ds(h, h)], inbox.at[1], s_s(1), s_r(1), where(3))
        a.start()
        b.start()
        return [a, b]

    def rs_forward(one, three, inbox, where, s_s, s_r, h):
        arrived(inbox.at[0], s_r(0))
        one[0:h, :] = (one[0:h, :].astype(F32) + inbox[0].astype(F32)).astype(BF16)
        a = rc(one.at[pl.ds(0, h)], inbox.at[4], s_s(4), s_r(4), where(1))
        a.start()
        arrived(inbox.at[1], s_r(1))
        three[h:, :] = (three[h:, :].astype(F32) + inbox[1].astype(F32)).astype(BF16)
        b = rc(three.at[pl.ds(h, h)], inbox.at[5], s_s(5), s_r(5), where(3))
        b.start()
        return [a, b]

    def rs_last(inbox, s_r):
        for i in (2, 3, 4, 5):
            arrived(inbox.at[i], s_r(i))
        low = inbox[3].astype(F32) + inbox[4].astype(F32)
        high = inbox[2].astype(F32) + inbox[5].astype(F32)
        return jnp.concatenate([low, high], axis=0)

    def scatter(l, k, chunk, window):
        def s_s(i):
            return rs_s.at[l, k, i]

        def s_r(i):
            return rs_r.at[l, k, i]

        copies = []

        def make(r):
            yy = lax.rem(y + r, 4)
            PART[r] = chunk(yy).astype(BF16)
            theirs = PART.at[r, pl.ds(pl.multiple_of((1 - c) * 64, 64), 64)]
            cp = rc(theirs, SIB.at[r], sb_s.at[l, k, r], sb_r.at[l, k, r], sibling)
            cp.start()
            copies.append(cp)

        def both(r):
            arrived(SIB.at[r], sb_r.at[l, k, r])
            mine = PART[r, pl.ds(pl.multiple_of(c * 64, 64), 64), :]
            return mine.astype(F32) + SIB[r].astype(F32)

        make(2)
        make(1)
        SUM[2] = both(2).astype(BF16)
        copies.extend(rs_two(SUM.at[2], RIN, yd, s_s, s_r, 32))
        make(3)
        SUM[1] = both(1).astype(BF16)
        cp = rc(SUM.at[1, pl.ds(32, 32)], RIN.at[2], s_s(2), s_r(2), yd(1))
        cp.start()
        copies.append(cp)
        make(0)
        SUM[3] = both(3).astype(BF16)
        cp = rc(SUM.at[3, pl.ds(0, 32)], RIN.at[3], s_s(3), s_r(3), yd(3))
        cp.start()
        copies.append(cp)
        copies.extend(rs_forward(SUM.at[1], SUM.at[3], RIN, yd, s_s, s_r, 32))
        OWN[...] = both(0)
        window()
        total = OWN[...] + rs_last(RIN, s_r)
        for cp in copies:
            cp.wait_send()
        return total

    def rows_of(ref, base, size):
        return ref.at[pl.ds(base, size)]

    def own_copies(i, where, sems):
        if i == 8:
            return rc(sv, SW.at[z], sems.at[i], w_r.at[zh, zl, i], where)
        base, size = (PIECES_A + PIECES_F)[i]
        return rc(
            rows_of(wb, base, size), W.at[zh, zl, pl.ds(base, size)], sems.at[i], w_r.at[zh, zl, i], where
        )

    order_own = (8, 0, 1, 2, 3, 4, 5, 6, 7)

    def send_own():
        for i in order_own:
            own_copies(i, cross, w_sc).start()
            own_copies(i, partner, w_sp).start()

    def w_at(l, b, i):
        if i == 8:
            return SW.at[2 * l + b]
        base, size = (PIECES_A + PIECES_F)[i]
        return W.at[l, b, pl.ds(base, size)]

    def pass_on(l, pieces):
        @pl.when(zh != l)
        def _():
            for i in pieces:
                got = w_at(l, 1 - zl, i)
                arrived(got, w_r.at[l, 1 - zl, i])
                rc(got, got, w_sf.at[i], w_r.at[l, 1 - zl, i], partner).start()

    def weights_here(l, pieces):
        other = jnp.where(zh == l, 1 - zl, zl)
        for i in pieces:
            arrived(w_at(l, other, i), w_r.at[l, other, i])

    mine_rows = pl.ds(pl.multiple_of(d * 64 + zl * 32, 32), 32)
    x_copy = rc(xs.at[1 - zl], XF.at[0, mine_rows], in_s.at[0], in_r.at[0], partner)
    x_copy.start()
    c_copy = rc(cs.at[1 - zl], CT.at[zl], in_s.at[1], in_r.at[1], partner)

    @pl.when(zh == 0)
    def _():
        send_own()

    c_copy.start()
    w_local = pltpu.make_async_copy(wb, W.at[zh, zl], loc)
    w_local.start()
    SW[z] = sv[...]
    XF[0, mine_rows, :] = xs[zl]
    CT[zl] = cs[zl]
    arrived(XF.at[0, pl.ds(pl.multiple_of(d * 64 + (1 - zl) * 32, 32), 32)], in_r.at[0])
    w_local.wait()

    def spread_out(rows, buf, out, s_s, s_r, l):
        buf[l] = rows.reshape(2, 32, 1024)
        for b in range(2):
            @pl.when((2 * l + b) == z)
            def _(b=b):
                out[z] = buf[l, b]

            @pl.when((2 * l + b) != z)
            def _(b=b):
                rc(buf.at[l, b], out.at[z], s_s.at[l, b], s_r.at[z], dev(zh_=l, zl_=b)).start()

    def spread_wait(buf, out, s_s, s_r):
        for k in range(1, 4):
            zz = lax.rem(z + k, 4)
            arrived(out.at[zz], s_r.at[zz])
        for l in range(2):
            for b in range(2):
                @pl.when((2 * l + b) != z)
                def _(l=l, b=b):
                    rc(buf.at[l, b], buf.at[l, b], s_s.at[l, b], s_r.at[z], sibling).wait_send()

    def row_of(l, i):
        return SW[2 * l, pl.ds(i, 1), :]

    own_rows = pl.ds(pl.multiple_of(d * 64, 64), 64)

    def out_weights(l):
        return jnp.concatenate([W[l, 0, 192:256, :], W[l, 1, 192:256, :]], axis=0)

    def qkv_weights(l):
        return jnp.concatenate([W[l, 0, 0:192, :], W[l, 1, 0:192, :]], axis=0)

    def lanes(yy):
        return pl.ds(pl.multiple_of(yy * 128, 128), 128)

    def forward_layer(l, carry):
        gather(XF, l, 0)

        @pl.when(l == 0)
        def _():
            pass_on(0, (8, 0, 1, 2, 3))

            @pl.when(zh == 1)
            def _():
                send_own()

        weights_here(l, (8, 0, 1, 2, 3))
        qv_bias = SW[2 * l, 7:8, 0:384] + SW[2 * l + 1, 7:8, 0:384]
        proj = (nt(XF[l], qkv_weights(l)) + qv_bias).astype(BF16)
        PB[l] = proj
        PT[l] = proj.T

        def attend(yy):
            cols = lanes(yy)
            for h in range(2):
                base = h * 192
                scores = nn(PB[l, :, base + 64 : base + 128], PT[l, base : base + 64, cols]) * SCALE
                scores = jnp.where(valid[...] > 0.5, scores, MASKED)
                terms = jnp.exp(scores - jnp.max(scores, axis=0, keepdims=True))
                probs = terms * (1.0 / jnp.sum(terms, axis=0, keepdims=True))
                PR[l, h, yy] = probs
                mixed = nn(PT[l, base + 128 : base + 192, :], probs.astype(BF16))
                AT[l, h * 64 : h * 64 + 64, cols] = mixed.astype(BF16)
            return nn(AT[l, :, cols].T, out_weights(l))

        attended = scatter(l, 0, attend, lambda: pass_on(l, (4, 5, 6, 7)))
        unit, inv = standardize(XF[l, own_rows, :].astype(F32) + attended + row_of(l, 4))
        N1[l] = unit
        S1[l] = jnp.broadcast_to(inv, (64, 128))
        middle = unit * row_of(l, 0) + row_of(l, 2)
        Y1[...] = middle
        YF[l, own_rows, :] = middle.astype(BF16)
        gather(YF, l, 1)
        weights_here(l, (4, 5, 6, 7))
        up_bias = SW[2 * l, 6:7, 0:512] + SW[2 * l + 1, 6:7, 0:512]

        def feed(yy):
            rows = YF[l, lanes(yy), :]
            total = None
            for b in range(2):
                pre = nt(rows, W[l, b, 256:512, :]) + up_bias[:, b * 256 : b * 256 + 256]
                cdf = 0.5 * (1.0 + lax.erf(pre * INV_SQRT2))
                hidden = (pre * cdf).astype(BF16)
                GD[l, yy, :, b * 256 : b * 256 + 256] = cdf + pre * (INV_SQRT_2PI * jnp.exp(-0.5 * pre * pre))
                HT[l, b * 256 : b * 256 + 256, lanes(yy)] = hidden.T
                piece = nn(hidden, W[l, b, 512:768, :])
                total = piece if total is None else total + piece
            return total

        def feed_window():
            @pl.when(l == 0)
            def _():
                pass_on(1, (8, 0, 1, 2, 3))

        fed = scatter(l, 1, feed, feed_window)
        unit, inv = standardize(Y1[...] + fed + row_of(l, 5))
        N2[l] = unit
        S2[l] = jnp.broadcast_to(inv, (64, 128))
        result = (unit * row_of(l, 1) + row_of(l, 3)).astype(BF16)

        @pl.when(l == 0)
        def _():
            XF[1, own_rows, :] = result

        spread_out(result, LO, lout, lo_s, lo_r, l)
        return carry

    lax.fori_loop(0, 2, forward_layer, 0)

    arrived(CT.at[1 - zl], in_r.at[1])
    GY[...] = CT[...].reshape(64, 1024).astype(F32)
    SM[...] = jnp.zeros_like(SM)

    A_ROWS, F_ROWS = (0, 256), (256, 512)
    pieces = (A_ROWS, F_ROWS)

    def partner_copy(l, p):
        base, size = pieces[p]
        sel = jnp.where(zh == l, 1 - zl, zl)
        return rc(
            G.at[l, sel, pl.ds(base, size)], PIN.at[l, pl.ds(base, size)], gp_s.at[l, p], gp_r.at[l, p], partner
        )

    def cross_copy(l, p):
        base, size = pieces[p]
        return rc(G.at[l, 1 - zl, pl.ds(base, size)], XIN.at[pl.ds(base, size)], gc_s.at[p], gc_r.at[p], cross)

    def combine(l, p):
        base, size = pieces[p]

        @pl.when(zh != l)
        def _():
            arrived(PIN.at[l, pl.ds(base, size)], gp_r.at[l, p])

            @pl.loop(0, size // 64)
            def _(i):
                rows = pl.ds(pl.multiple_of(base + i * 64, 64), 64)
                G[l, 1 - zl, rows, :] = (G[l, 1 - zl, rows, :].astype(F32) + PIN[l, rows, :].astype(F32)).astype(BF16)

            cross_copy(l, p).start()

    def backward_layer(step, carry):
        l = 1 - step
        grad = GY[...]
        unit = N2[l]
        grad_second = standardize_back(grad, row_of(l, 1), unit, S2[l, :, 0:1])
        SM[l, 1:2, :] = jnp.sum(grad * unit, axis=0, keepdims=True)
        SM[l, 3:4, :] = jnp.sum(grad, axis=0, keepdims=True)
        SM[l, 5:6, :] = jnp.sum(grad_second, axis=0, keepdims=True)
        GR[...] = grad_second
        GF[l, own_rows, :] = grad_second.astype(BF16)
        gather(GF, l, 2)

        def feed_back(yy):
            rows = GF[l, lanes(yy), :]
            total = None
            for b in range(2):
                grad_pre = (nt(rows, W[l, b, 512:768, :]) * GD[l, yy, :, b * 256 : b * 256 + 256]).astype(BF16)
                SM[l, 6:7, b * 256 : b * 256 + 256] += jnp.sum(grad_pre.astype(F32), axis=0, keepdims=True)
                GZT[b * 256 : b * 256 + 256, lanes(yy)] = grad_pre.T
                piece = nn(grad_pre, W[l, b, 256:512, :])
                total = piece if total is None else total + piece
            return total

        def feed_grads():
            @pl.loop(0, 2)
            def _(b):
                rows = pl.ds(pl.multiple_of(b * 256, 256), 256)
                G[l, b, 256:512, :] = nn(GZT[rows, :], YF[l]).astype(BF16)
                G[l, b, 512:768, :] = nn(HT[l, rows, :], GF[l]).astype(BF16)

            partner_copy(l, 1).start()

            @pl.when(l == 0)
            def _():
                combine(1, 0)

        grad_middle = GR[...] + scatter(l, 2, feed_back, feed_grads)
        unit = N1[l]
        grad_first = standardize_back(grad_middle, row_of(l, 0), unit, S1[l, :, 0:1])
        SM[l, 0:1, :] = jnp.sum(grad_middle * unit, axis=0, keepdims=True)
        SM[l, 2:3, :] = jnp.sum(grad_middle, axis=0, keepdims=True)
        SM[l, 4:5, :] = jnp.sum(grad_first, axis=0, keepdims=True)
        GR[...] = grad_first
        GO[l, own_rows, :] = grad_first.astype(BF16)
        gather(GO, l, 3)

        GKT[...] = jnp.zeros_like(GKT)
        GVT[...] = jnp.zeros_like(GVT)

        @pl.loop(0, 4)
        def _(yy):
            cols = lanes(yy)
            grad_mixed = nt(GO[l, cols, :], out_weights(l)).astype(BF16)
            mixed_t = grad_mixed.T
            for h in range(2):
                base = h * 192
                half = mixed_t[h * 64 : h * 64 + 64, :]
                probs = PR[l, h, yy]
                grad_prob = nn(PB[l, :, base + 128 : base + 192], half)
                inner = jnp.sum(probs * grad_prob, axis=0, keepdims=True)
                grad_score = (probs * (grad_prob - inner)).astype(BF16)
                GPT[base : base + 64, cols] = (
                    nn(PT[l, base + 64 : base + 128, :], grad_score) * SCALE
                ).astype(BF16)
                GKT[h] += nt(PT[l, base : base + 64, cols], grad_score)
                GVT[h] += nt(half, probs.astype(BF16))

        for h in range(2):
            base = h * 192
            GPT[base + 64 : base + 128, :] = (GKT[h] * SCALE).astype(BF16)
            GPT[base + 128 : base + 192, :] = GVT[h].astype(BF16)

        def project_back(yy):
            grad_proj = GPT[:, lanes(yy)].T
            SM[l, 7:8, 0:384] += jnp.sum(grad_proj.astype(F32), axis=0, keepdims=True)
            return nn(grad_proj, qkv_weights(l))

        def attend_grads():
            @pl.loop(0, 2)
            def _(b):
                G[l, b, 0:192, :] = nn(GPT[pl.ds(pl.multiple_of(b * 192, 64), 192), :], XF[l]).astype(BF16)
                G[l, b, 192:256, :] = nn(AT[l, pl.ds(pl.multiple_of(b * 64, 64), 64), :], GO[l]).astype(BF16)

            partner_copy(l, 0).start()
            combine(l, 1)

        grad_input = (GR[...] + scatter(l, 3, project_back, attend_grads)).astype(BF16)
        GY[...] = grad_input.astype(F32)
        spread_out(grad_input, IG, igout, ig_s, ig_r, l)
        return carry

    lax.fori_loop(0, 2, backward_layer, 0)

    combine(0, 0)
    row = lax.broadcasted_iota(jnp.int32, (2, 8, 1024), 1)
    cp_c = rc(SM, SMC, sc_s, sc_r, sibling)
    cp_c.start()

    def own_sum(p):
        base, size = pieces[p]
        arrived(PIN.at[zh, pl.ds(base, size)], gp_r.at[zh, p])
        arrived(XIN.at[pl.ds(base, size)], gc_r.at[p])

        @pl.loop(0, size // 64)
        def _(i):
            rows = pl.ds(pl.multiple_of(base + i * 64, 64), 64)
            FIN[rows, :] = (
                G[zh, zl, rows, :].astype(F32) + PIN[zh, rows, :].astype(F32) + XIN[rows, :].astype(F32)
            ).astype(BF16)

    def x_rows(ref, p, r):
        base, size = pieces[p]
        n = size // 4
        return ref.at[pl.ds(pl.multiple_of(base + lax.rem(x + r, 4) * n, n), n)]

    xi = (XIA, XIF)
    done = []

    def x_start(p):
        n = pieces[p][1] // 4
        h = n // 2
        done.extend(rs_two(x_rows(FIN, p, 2), xi[p], xd, lambda i: xr_s.at[p, i], lambda i: xr_r.at[p, i], h))
        a = rc(x_rows(FIN, p, 1).at[pl.ds(h, h)], xi[p].at[2], xr_s.at[p, 2], xr_r.at[p, 2], xd(1))
        b = rc(x_rows(FIN, p, 3).at[pl.ds(0, h)], xi[p].at[3], xr_s.at[p, 3], xr_r.at[p, 3], xd(3))
        a.start()
        b.start()
        done.extend([a, b])

    def x_forward(p):
        h = pieces[p][1] // 8
        done.extend(
            rs_forward(
                x_rows(FIN, p, 1), x_rows(FIN, p, 3), xi[p], xd,
                lambda i: xr_s.at[p, i], lambda i: xr_r.at[p, i], h,
            )
        )

    def x_slot(p):
        base, size = pieces[p]
        n, h = size // 4, size // 8

        def at(r, half):
            start = pl.multiple_of(base + lax.rem(x + r, 4) * n + half * h, h)
            return gout.at[pl.ds(start, h)]

        return at

    def x_last(p):
        base, size = pieces[p]
        n = size // 4
        rows = pl.ds(pl.multiple_of(base + x * n, n), n)
        gout[rows, :] = (FIN[rows, :].astype(F32) + rs_last(xi[p], lambda i: xr_r.at[p, i])).astype(BF16)
        at = x_slot(p)
        done.extend(ring_ag_start(lambda half: at(0, half), xd, lambda i: xg_s.at[p, i], lambda i: xg_r.at[p, i]))

    def x_gather(p):
        done.extend(
            ring_ag_finish(x_slot(p), xd, lambda i: xg_s.at[p, i], lambda i: xg_r.at[p, i], lambda k, r, h: None)
        )

    own_sum(1)
    x_start(1)

    arrived(SMC, sc_r)
    cp_c.wait_send()
    SM1[...] = jnp.where(row < 6, SM[...] + SMC[...], SM[...])
    SMY[y] = SM1[...]
    for r in range(1, 4):
        cp = rc(SM1, SMY.at[y], sy_s.at[r], sy_r.at[r], yd(r))
        cp.start()
        done.append(cp)

    x_forward(1)
    for r in range(1, 4):
        arrived(SMY.at[lax.rem(y + 4 - r, 4)], sy_r.at[r])
    SM2[...] = jnp.where(row < 6, (SMY[0] + SMY[1]) + (SMY[2] + SMY[3]), SM1[...])
    SMZ[z] = SM2[zh]
    for k, where, lz in ((0, partner, zh), (1, cross, 1 - zh), (2, far, 1 - zh)):
        cp = rc(SM2.at[lz], SMZ.at[z], sz_s.at[k], sz_r.at[k], where)
        cp.start()
        done.append(cp)

    own_sum(0)
    x_start(0)
    x_last(1)
    x_forward(0)
    for k, zz in ((0, 2 * zh + 1 - zl), (1, 2 * (1 - zh) + 1 - zl), (2, 2 * (1 - zh) + zl)):
        arrived(SMZ.at[zz], sz_r.at[k])
    SM3[...] = (SMZ[0] + SMZ[1]) + (SMZ[2] + SMZ[3])
    SMX[x] = SM3[...]
    for r in range(1, 4):
        cp = rc(SM3, SMX.at[x], sx_s.at[r], sx_r.at[r], xd(r))
        cp.start()
        done.append(cp)
    x_last(0)
    x_gather(1)
    x_gather(0)
    for r in range(1, 4):
        arrived(SMX.at[lax.rem(x + 4 - r, 4)], sx_r.at[r])
    smout[...] = (SMX[0] + SMX[1]) + (SMX[2] + SMX[3])

    spread_wait(LO, lout, lo_s, lo_r)
    spread_wait(IG, igout, ig_s, ig_r)
    x_copy.wait_send()
    c_copy.wait_send()
    for i in order_own:
        own_copies(i, cross, w_sc).wait_send()
        own_copies(i, partner, w_sp).wait_send()
        got = w_at(1 - zh, 1 - zl, i)
        rc(got, got, w_sf.at[i], w_r.at[1 - zh, 1 - zl, i], partner).wait_send()
    for l in range(2):
        for p in range(2):
            partner_copy(l, p).wait_send()
    for p in range(2):
        cross_copy(1 - zh, p).wait_send()
    for cp in done:
        cp.wait_send()


def run_kernel(xs, cs, wb, sv, valid):
    vm = pltpu.VMEM
    dma = pltpu.SemaphoreType.DMA
    scratch = [
        vm((2, 2, 768, 1024), BF16),
        vm((4, 8, 1024), F32),
        vm((2, 512, 1024), BF16),
        vm((2, 512, 1024), BF16),
        vm((2, 512, 1024), BF16),
        vm((2, 512, 1024), BF16),
        vm((2, 32, 1024), BF16),
        vm((2, 512, 384), BF16),
        vm((2, 384, 512), BF16),
        vm((2, 2, 4, 512, 128), F32),
        vm((2, 128, 512), BF16),
        vm((2, 512, 512), BF16),
        vm((2, 4, 128, 512), F32),
        vm((512, 512), BF16),
        vm((384, 512), BF16),
        vm((2, 64, 512), F32),
        vm((2, 64, 512), F32),
        vm((2, 64, 1024), F32),
        vm((2, 64, 1024), F32),
        vm((2, 64, 128), F32),
        vm((2, 64, 128), F32),
        vm((64, 1024), F32),
        vm((64, 1024), F32),
        vm((64, 1024), F32),
        vm((64, 1024), F32),
        vm((4, 128, 1024), BF16),
        vm((4, 64, 1024), BF16),
        vm((4, 64, 1024), BF16),
        vm((6, 32, 1024), BF16),
        vm((2, 2, 768, 1024), BF16),
        vm((2, 768, 1024), BF16),
        vm((768, 1024), BF16),
        vm((768, 1024), BF16),
        vm((6, 64, 1024), BF16),
        vm((6, 32, 1024), BF16),
        vm((2, 2, 32, 1024), BF16),
        vm((2, 2, 32, 1024), BF16),
        vm((2, 8, 1024), F32),
        vm((2, 8, 1024), F32),
        vm((2, 8, 1024), F32),
        vm((4, 2, 8, 1024), F32),
        vm((2, 8, 1024), F32),
        vm((4, 8, 1024), F32),
        vm((8, 1024), F32),
        vm((4, 8, 1024), F32),
        dma((2, 4, 13)),
        dma((2, 4, 13)),
        dma((2, 4, 4)),
        dma((2, 4, 4)),
        dma((2, 4, 6)),
        dma((2, 4, 6)),
        dma((2,)),
        dma((2,)),
        dma(()),
        dma((9,)),
        dma((9,)),
        dma((9,)),
        dma((2, 2, 9)),
        dma((2, 2)),
        dma((2, 2)),
        dma((2,)),
        dma((2,)),
        dma((2, 6)),
        dma((2, 6)),
        dma((2, 6)),
        dma((2, 6)),
        dma((2, 2)),
        dma((4,)),
        dma((2, 2)),
        dma((4,)),
        dma(()),
        dma(()),
        dma((4,)),
        dma((4,)),
        dma((3,)),
        dma((3,)),
        dma((4,)),
        dma((4,)),
    ]
    in_vmem = pl.BlockSpec(memory_space=pltpu.VMEM)
    return pl.pallas_call(
        kernel,
        out_shape=(
            jax.ShapeDtypeStruct((4, 32, 1024), BF16),
            jax.ShapeDtypeStruct((4, 32, 1024), BF16),
            jax.ShapeDtypeStruct((768, 1024), BF16),
            jax.ShapeDtypeStruct((8, 1024), F32),
        ),
        in_specs=[in_vmem, in_vmem, pl.BlockSpec(memory_space=pl.ANY), in_vmem, in_vmem],
        out_specs=(in_vmem,) * 4,
        scratch_shapes=scratch,
        compiler_params=pltpu.CompilerParams(
            collective_id=0, has_side_effects=True, vmem_limit_bytes=60 * 1024 * 1024
        ),
        cost_estimate=pl.CostEstimate(flops=10_000_000_000, bytes_accessed=10_000_000, transcendentals=3_000_000),
    )(xs, cs, wb, sv, valid)


def per_device(
    inputs, lengths, cotangent, w_qkv, b_qv, w_out, w_up, b_up, w_down, norm_gains, norm_shifts, out_bias
):
    zh = lax.axis_index("section")
    zl = lax.axis_index("tensor") // 8
    xs = jnp.transpose(lax.dynamic_index_in_dim(inputs, zh, 0, keepdims=False), (1, 0, 2))
    cs = jnp.transpose(lax.dynamic_index_in_dim(cotangent, zh, 0, keepdims=False), (1, 0, 2))
    wb = jnp.concatenate(
        [jnp.transpose(w_qkv[0], (1, 2, 0)).reshape(192, 1024), w_out[0], w_up[0].T, w_down[0]], axis=0
    )
    zeros = jnp.zeros((64,), F32)
    up_row = lax.dynamic_update_slice(jnp.zeros((1024,), F32), b_up[0], (zl * 256,))
    qv_row = lax.dynamic_update_slice(
        jnp.zeros((1024,), F32), jnp.concatenate([b_qv[0, 0], zeros, b_qv[0, 1]]), (zl * 192,)
    )
    sv = jnp.concatenate([norm_gains[0], norm_shifts[0], out_bias[0], up_row[None], qv_row[None]], axis=0)
    length = lax.dynamic_slice(lengths, (zh, zl), (1, 1))
    r = lax.broadcasted_iota(jnp.int32, (512, 128), 0)
    position = ((r // 32) % 2) * 256 + (r // 64) * 32 + r % 32
    valid = (position < length).astype(F32)

    lout, igout, g, sm = run_kernel(xs, cs, wb, sv, valid)

    def place(blocks):
        return jnp.transpose(blocks.reshape(2, 2, 32, 1024), (0, 2, 1, 3))[None]

    g32 = g.astype(F32)
    grad_qkv = jnp.transpose(g32[0:192].reshape(3, 64, 1024), (2, 0, 1))[None]
    qv = lax.dynamic_slice(sm[7], (zl * 192,), (192,))
    up_bias = lax.dynamic_slice(sm[6], (zl * 256,), (256,))
    return (
        place(lout),
        place(igout).astype(F32),
        grad_qkv,
        jnp.stack([qv[0:64], qv[128:192]])[None],
        g32[192:256][None],
        g32[256:512].T[None],
        up_bias[None],
        g32[512:768][None],
        sm[0:2][None],
        sm[2:4][None],
        sm[4:6][None],
    )


def solution(mesh):
    in_specs = (
        P(None, "tensor", "dp", None),
        P(None, "dp"),
        P(None, "tensor", "dp", None),
        P("section", None, None, "tensor"),
        P("section", None, "tensor"),
        P("section", "tensor", None),
        P("section", None, "tensor"),
        P("section", "tensor"),
        P("section", "tensor", None),
        P("section", None, None),
        P("section", None, None),
        P("section", None, None),
    )
    out_specs = (
        P("section", None, "tensor", "dp", None),
        P("section", None, "tensor", "dp", None),
        P("section", None, None, "tensor"),
        P("section", None, "tensor"),
        P("section", "tensor", None),
        P("section", None, "tensor"),
        P("section", "tensor"),
        P("section", "tensor", None),
        P("section", None, None),
        P("section", None, None),
        P("section", None, None),
    )
    return jax.shard_map(per_device, mesh=mesh, in_specs=in_specs, out_specs=out_specs, check_vma=False)
```

```python
import jax
import jax.numpy as jnp
from jax import lax
from jax.experimental import pallas as pl
from jax.experimental.pallas import tpu as pltpu
from jax.sharding import PartitionSpec as P

EPSILON = 1e-12
MASKED = -1e30
F32 = jnp.float32
BF16 = jnp.bfloat16
MESH = pl.DeviceIdType.MESH
INV_SQRT2 = 0.7071067811865476
INV_SQRT_2PI = 0.3989422804014327
SCALE = 0.125

PIECES = ((0, 256), (256, 512))


def nt(a, b):
    return lax.dot_general(a, b, (((1,), (1,)), ((), ())), preferred_element_type=F32)


def nn(a, b):
    return lax.dot_general(a, b, (((1,), (0,)), ((), ())), preferred_element_type=F32)


def standardize(rows):
    center = jnp.mean(rows, axis=-1, keepdims=True)
    centred = rows - center
    spread = jnp.mean(centred * centred, axis=-1, keepdims=True)
    inv = lax.rsqrt(spread + EPSILON)
    return centred * inv, inv


def standardize_back(grad_out, gain, unit, inv):
    scaled = grad_out * gain
    return inv * (
        scaled
        - jnp.mean(scaled, axis=-1, keepdims=True)
        - unit * jnp.mean(scaled * unit, axis=-1, keepdims=True)
    )


def kernel(
    xs, cs, wb, sv, valid,
    lout, igout, gout, smout,
    W, SW, XF, YF, GF, GO, CT, PB, PT, PR, AT, HT, GD, GZT, GPT, GKT, GVT,
    N1, N2, S1, S2, Y1, GR, GY, OWN,
    PART, SIB, SUM, RIN, G, GXA, GXF, QXA, QXF, ZXA, ZXF,
    LO, IG, SM, SMC, SM1, SMY, SM2, SMZ, SM3, SMX,
    ag_s, ag_r, sb_s, sb_r, rs_s, rs_r, in_s, in_r, loc, w_s, w_r,
    xr_s, xr_r, gz_s, gz_r, xg_s, xg_r, lo_s, lo_r, ig_s, ig_r,
    sc_s, sc_r, sy_s, sy_r, sz_s, sz_r, sx_s, sx_r,
):
    zh = lax.axis_index("section")
    x = lax.axis_index("dp")
    t = lax.axis_index("tensor")
    zl = t // 8
    y = (t % 8) // 2
    c = t % 2
    d = t % 8
    z = 2 * zh + zl

    def dev(zh_=None, x_=None, zl_=None, y_=None, c_=None):
        zh_ = zh if zh_ is None else zh_
        x_ = x if x_ is None else x_
        zl_ = zl if zl_ is None else zl_
        y_ = y if y_ is None else y_
        c_ = c if c_ is None else c_
        return (zh_, x_, zl_ * 8 + y_ * 2 + c_)

    def yd(r):
        return dev(y_=lax.rem(y + r, 4))

    def xd(r):
        return dev(x_=lax.rem(x + r, 4))

    sibling = dev(c_=1 - c)
    partner = dev(zl_=1 - zl)
    cross = dev(zh_=1 - zh, zl_=1 - zl)
    far = dev(zh_=1 - zh)

    def rc(src, dst, ssem, rsem, where):
        return pltpu.make_async_remote_copy(
            src_ref=src, dst_ref=dst, send_sem=ssem, recv_sem=rsem, device_id=where, device_id_type=MESH
        )

    def arrived(dst, rsem):
        rc(dst, dst, rsem, rsem, sibling).wait_recv()

    barrier = pltpu.get_barrier_semaphore()
    greeted = [sibling, yd(1), yd(2), yd(3), xd(1), xd(2), xd(3), partner, cross, far]
    for other in greeted:
        pl.semaphore_signal(barrier, inc=1, device_id=other, device_id_type=MESH)
    pl.semaphore_wait(barrier, len(greeted))

    def slot(full, l, yy, cc):
        return full.at[l, pl.ds(pl.multiple_of(yy * 128 + cc * 64, 64), 64)]

    def ag_begin(full, l, k):
        mine = slot(full, l, y, c)
        copies = [rc(mine, mine, ag_s.at[l, k, i], ag_r.at[l, k, i], yd(i)) for i in (1, 3, 2)]
        copies.append(rc(mine, mine, ag_s.at[l, k, 4], ag_r.at[l, k, 4], sibling))
        for cp in copies:
            cp.start()
        return copies

    def from_ring(full, l, k, i, copies):
        got = slot(full, l, lax.rem(y + 4 - i, 4), c)
        arrived(got, ag_r.at[l, k, i])
        cp = rc(got, got, ag_s.at[l, k, 4 + i], ag_r.at[l, k, 4 + i], sibling)
        cp.start()
        copies.append(cp)

    def from_sibling(full, l, k, i):
        arrived(slot(full, l, lax.rem(y + 4 - i, 4), 1 - c), ag_r.at[l, k, 4 + i])

    def gather(full, l, k, use):
        copies = ag_begin(full, l, k)
        from_sibling(full, l, k, 0)
        use(y)
        from_ring(full, l, k, 1, copies)
        from_ring(full, l, k, 3, copies)
        from_sibling(full, l, k, 1)
        use(lax.rem(y + 3, 4))
        from_ring(full, l, k, 2, copies)
        from_sibling(full, l, k, 3)
        use(lax.rem(y + 1, 4))
        from_sibling(full, l, k, 2)
        use(lax.rem(y + 2, 4))
        for cp in copies:
            cp.wait_send()

    def make(l, k, r, chunk, copies):
        PART[r] = chunk(lax.rem(y + r, 4)).astype(BF16)
        theirs = PART.at[r, pl.ds(pl.multiple_of((1 - c) * 64, 64), 64)]
        cp = rc(theirs, SIB.at[r], sb_s.at[l, k, r], sb_r.at[l, k, r], sibling)
        cp.start()
        copies.append(cp)

    def both(l, k, r):
        arrived(SIB.at[r], sb_r.at[l, k, r])
        mine = PART[r, pl.ds(pl.multiple_of(c * 64, 64), 64), :]
        return mine.astype(F32) + SIB[r].astype(F32)

    def push(l, k, r, copies):
        SUM[r] = both(l, k, r).astype(BF16)
        cp = rc(SUM.at[r], RIN.at[r], rs_s.at[l, k, r], rs_r.at[l, k, r], yd(r))
        cp.start()
        copies.append(cp)

    def finish(l, k, copies):
        for r in (1, 3, 2):
            arrived(RIN.at[r], rs_r.at[l, k, r])
        total = OWN[...] + ((RIN[1].astype(F32) + RIN[3].astype(F32)) + RIN[2].astype(F32))
        for cp in copies:
            cp.wait_send()
        return total

    def scatter(l, k, chunk, window):
        copies = []
        make(l, k, 2, chunk, copies)
        make(l, k, 1, chunk, copies)
        push(l, k, 2, copies)
        make(l, k, 3, chunk, copies)
        push(l, k, 1, copies)
        make(l, k, 0, chunk, copies)
        push(l, k, 3, copies)
        OWN[...] = both(l, k, 0)
        window()
        return finish(l, k, copies)

    def gather_scatter(full, l, k, chunk, window):
        copies = ag_begin(full, l, k)
        from_sibling(full, l, k, 0)
        make(l, k, 0, chunk, copies)
        from_ring(full, l, k, 1, copies)
        from_ring(full, l, k, 3, copies)
        from_sibling(full, l, k, 1)
        make(l, k, 3, chunk, copies)
        from_ring(full, l, k, 2, copies)
        from_sibling(full, l, k, 3)
        make(l, k, 1, chunk, copies)
        push(l, k, 3, copies)
        from_sibling(full, l, k, 2)
        make(l, k, 2, chunk, copies)
        push(l, k, 1, copies)
        push(l, k, 2, copies)
        OWN[...] = both(l, k, 0)
        window()
        return finish(l, k, copies)

    others = (far, cross, partner)

    def w_at(l, b, i):
        if i == 2:
            return SW.at[2 * l + b]
        base, size = PIECES[i]
        return W.at[l, b, pl.ds(base, size)]

    def w_copy(i, k):
        src = sv if i == 2 else wb.at[pl.ds(*PIECES[i])]
        return rc(src, w_at(zh, zl, i), w_s.at[k, i], w_r.at[zh, zl, i], others[k])

    def send_own(i):
        for k in range(3):
            w_copy(i, k).start()

    def weights_here(l, i):
        for b in range(2):
            @pl.when((2 * l + b) != z)
            def _(b=b):
                arrived(w_at(l, b, i), w_r.at[l, b, i])

    mine_rows = pl.ds(pl.multiple_of(d * 64 + zl * 32, 32), 32)
    x_copy = rc(xs.at[1 - zl], XF.at[0, mine_rows], in_s.at[0], in_r.at[0], partner)
    x_copy.start()
    c_copy = rc(cs.at[1 - zl], CT.at[zl], in_s.at[1], in_r.at[1], partner)

    @pl.when(zh == 0)
    def _():
        send_own(2)
        send_own(0)
        send_own(1)

    c_copy.start()
    w_local = pltpu.make_async_copy(wb, W.at[zh, zl], loc)
    w_local.start()
    SW[z] = sv[...]
    XF[0, mine_rows, :] = xs[zl]
    CT[zl] = cs[zl]
    arrived(XF.at[0, pl.ds(pl.multiple_of(d * 64 + (1 - zl) * 32, 32), 32)], in_r.at[0])
    w_local.wait()

    def spread_out(rows, buf, out, s_s, s_r, l):
        buf[l] = rows.reshape(2, 32, 1024)
        for b in range(2):
            @pl.when((2 * l + b) == z)
            def _(b=b):
                out[z] = buf[l, b]

            @pl.when((2 * l + b) != z)
            def _(b=b):
                rc(buf.at[l, b], out.at[z], s_s.at[l, b], s_r.at[z], dev(zh_=l, zl_=b)).start()

    def spread_wait(buf, out, s_s, s_r):
        for k in range(1, 4):
            zz = lax.rem(z + k, 4)
            arrived(out.at[zz], s_r.at[zz])
        for l in range(2):
            for b in range(2):
                @pl.when((2 * l + b) != z)
                def _(l=l, b=b):
                    rc(buf.at[l, b], buf.at[l, b], s_s.at[l, b], s_r.at[z], sibling).wait_send()

    def row_of(l, i):
        return SW[2 * l, pl.ds(i, 1), :]

    own_rows = pl.ds(pl.multiple_of(d * 64, 64), 64)

    def out_weights(l):
        return jnp.concatenate([W[l, 0, 192:256, :], W[l, 1, 192:256, :]], axis=0)

    def qkv_weights(l):
        return jnp.concatenate([W[l, 0, 0:192, :], W[l, 1, 0:192, :]], axis=0)

    def lanes(yy):
        return pl.ds(pl.multiple_of(yy * 128, 128), 128)

    def forward_layer(l, carry):
        gather(XF, l, 0, lambda yy: None)
        weights_here(l, 2)
        weights_here(l, 0)

        @pl.when((l == 0) & (zh == 1))
        def _():
            send_own(2)
            send_own(0)

        qv_bias = SW[2 * l, 7:8, 0:384] + SW[2 * l + 1, 7:8, 0:384]
        proj = (nt(XF[l], qkv_weights(l)) + qv_bias).astype(BF16)
        PB[l] = proj
        PT[l] = proj.T

        def attend(yy):
            cols = lanes(yy)
            for h in range(2):
                base = h * 192
                scores = nn(PB[l, :, base + 64 : base + 128], PT[l, base : base + 64, cols]) * SCALE
                scores = jnp.where(valid[...] > 0.5, scores, MASKED)
                terms = jnp.exp(scores - jnp.max(scores, axis=0, keepdims=True))
                probs = terms * (1.0 / jnp.sum(terms, axis=0, keepdims=True))
                PR[l, h, yy] = probs
                mixed = nn(PT[l, base + 128 : base + 192, :], probs.astype(BF16))
                AT[l, h * 64 : h * 64 + 64, cols] = mixed.astype(BF16)
            return nn(AT[l, :, cols].T, out_weights(l))

        attended = scatter(l, 0, attend, lambda: None)
        unit, inv = standardize(XF[l, own_rows, :].astype(F32) + attended + row_of(l, 4))
        N1[l] = unit
        S1[l] = jnp.broadcast_to(inv, (64, 128))
        middle = unit * row_of(l, 0) + row_of(l, 2)
        Y1[...] = middle
        YF[l, own_rows, :] = middle.astype(BF16)
        weights_here(l, 1)

        @pl.when((l == 0) & (zh == 1))
        def _():
            send_own(1)

        up_bias = SW[2 * l, 6:7, 0:512] + SW[2 * l + 1, 6:7, 0:512]

        def feed(yy):
            rows = YF[l, lanes(yy), :]
            total = None
            for b in range(2):
                pre = nt(rows, W[l, b, 256:512, :]) + up_bias[:, b * 256 : b * 256 + 256]
                cdf = 0.5 * (1.0 + lax.erf(pre * INV_SQRT2))
                hidden = (pre * cdf).astype(BF16)
                GD[l, yy, :, b * 256 : b * 256 + 256] = cdf + pre * (INV_SQRT_2PI * jnp.exp(-0.5 * pre * pre))
                HT[l, b * 256 : b * 256 + 256, lanes(yy)] = hidden.T
                piece = nn(hidden, W[l, b, 512:768, :])
                total = piece if total is None else total + piece
            return total

        fed = gather_scatter(YF, l, 1, feed, lambda: None)
        unit, inv = standardize(Y1[...] + fed + row_of(l, 5))
        N2[l] = unit
        S2[l] = jnp.broadcast_to(inv, (64, 128))
        result = (unit * row_of(l, 1) + row_of(l, 3)).astype(BF16)

        @pl.when(l == 0)
        def _():
            XF[1, own_rows, :] = result

        spread_out(result, LO, lout, lo_s, lo_r, l)
        return carry

    lax.fori_loop(0, 2, forward_layer, 0)

    arrived(CT.at[1 - zl], in_r.at[1])
    GY[...] = CT[...].reshape(64, 1024).astype(F32)
    SM[...] = jnp.zeros_like(SM)

    GX, QX, ZX = (GXA, GXF), (QXA, QXF), (ZXA, ZXF)

    def own_part(p, ref, who, *lead):
        base, size = PIECES[p]
        n = size // 4
        return ref.at[(*lead, pl.ds(pl.multiple_of(base + who * n, n), n))]

    def x_copy_of(l, p, b, r):
        src = own_part(p, G, lax.rem(x + r, 4), l, b)
        return rc(src, GX[p].at[l, b, r - 1], xr_s.at[l, p, b, r - 1], xr_r.at[l, p, b, r - 1], xd(r))

    def z_copy_of(l, p, b):
        k = lax.rem(2 * l + b + 4 - z, 4) - 1
        return rc(QX[p].at[l, b], ZX[p].at[k], gz_s.at[l, p, b], gz_r.at[p, k], dev(zh_=l, zl_=b))

    def g_copy_of(p, r):
        mine = own_part(p, gout, x)
        return rc(mine, mine, xg_s.at[p, r - 1], xg_r.at[p, r - 1], xd(r))

    def grad_x(l, p):
        for b in range(2):
            for r in (2, 1, 3):
                x_copy_of(l, p, b, r).start()

    def grad_z(l, p):
        n = PIECES[p][1] // 4
        for b in range(2):
            for r in (1, 3, 2):
                arrived(GX[p].at[l, b, r - 1], xr_r.at[l, p, b, r - 1])
            mine = own_part(p, G, x, l, b)

            @pl.loop(0, n // 32)
            def _(i, b=b, mine=mine):
                rows = pl.ds(pl.multiple_of(i * 32, 32), 32)
                QX[p][l, b, rows, :] = (
                    (mine[rows, :].astype(F32) + GX[p][l, b, 0, rows, :].astype(F32))
                    + (GX[p][l, b, 1, rows, :].astype(F32) + GX[p][l, b, 2, rows, :].astype(F32))
                ).astype(BF16)

            @pl.when((2 * l + b) != z)
            def _(b=b):
                z_copy_of(l, p, b).start()

    def grad_own(p):
        n = PIECES[p][1] // 4
        for k in range(3):
            arrived(ZX[p].at[k], gz_r.at[p, k])
        mine = own_part(p, gout, x)

        @pl.loop(0, n // 32)
        def _(i):
            rows = pl.ds(pl.multiple_of(i * 32, 32), 32)
            mine[rows, :] = (
                (QX[p][zh, zl, rows, :].astype(F32) + ZX[p][0, rows, :].astype(F32))
                + (ZX[p][1, rows, :].astype(F32) + ZX[p][2, rows, :].astype(F32))
            ).astype(BF16)

        for r in (2, 1, 3):
            g_copy_of(p, r).start()

    def grad_done(p):
        for r in (1, 3, 2):
            arrived(own_part(p, gout, lax.rem(x + 4 - r, 4)), xg_r.at[p, r - 1])

    def backward_layer(step, carry):
        l = 1 - step
        grad = GY[...]
        unit = N2[l]
        grad_second = standardize_back(grad, row_of(l, 1), unit, S2[l, :, 0:1])
        SM[l, 1:2, :] = jnp.sum(grad * unit, axis=0, keepdims=True)
        SM[l, 3:4, :] = jnp.sum(grad, axis=0, keepdims=True)
        SM[l, 5:6, :] = jnp.sum(grad_second, axis=0, keepdims=True)
        GR[...] = grad_second
        GF[l, own_rows, :] = grad_second.astype(BF16)
        def feed_back(yy):
            rows = GF[l, lanes(yy), :]
            total = None
            for b in range(2):
                grad_pre = (nt(rows, W[l, b, 512:768, :]) * GD[l, yy, :, b * 256 : b * 256 + 256]).astype(BF16)
                SM[l, 6:7, b * 256 : b * 256 + 256] += jnp.sum(grad_pre.astype(F32), axis=0, keepdims=True)
                GZT[b * 256 : b * 256 + 256, lanes(yy)] = grad_pre.T
                piece = nn(grad_pre, W[l, b, 256:512, :])
                total = piece if total is None else total + piece
            return total

        def feed_grads():
            @pl.loop(0, 2)
            def _(b):
                rows = pl.ds(pl.multiple_of(b * 256, 256), 256)
                G[l, b, 256:512, :] = nn(GZT[rows, :], YF[l]).astype(BF16)
                G[l, b, 512:768, :] = nn(HT[l, rows, :], GF[l]).astype(BF16)

            grad_x(l, 1)

            @pl.when(l == 0)
            def _():
                grad_z(1, 1)
                grad_z(1, 0)

        grad_middle = GR[...] + gather_scatter(GF, l, 2, feed_back, feed_grads)
        unit = N1[l]
        grad_first = standardize_back(grad_middle, row_of(l, 0), unit, S1[l, :, 0:1])
        SM[l, 0:1, :] = jnp.sum(grad_middle * unit, axis=0, keepdims=True)
        SM[l, 2:3, :] = jnp.sum(grad_middle, axis=0, keepdims=True)
        SM[l, 4:5, :] = jnp.sum(grad_first, axis=0, keepdims=True)
        GR[...] = grad_first
        GO[l, own_rows, :] = grad_first.astype(BF16)
        GKT[...] = jnp.zeros_like(GKT)
        GVT[...] = jnp.zeros_like(GVT)

        def attend_back(yy):
            cols = lanes(yy)
            grad_mixed = nt(GO[l, cols, :], out_weights(l)).astype(BF16)
            mixed_t = grad_mixed.T
            for h in range(2):
                base = h * 192
                half = mixed_t[h * 64 : h * 64 + 64, :]
                probs = PR[l, h, yy]
                grad_prob = nn(PB[l, :, base + 128 : base + 192], half)
                inner = jnp.sum(probs * grad_prob, axis=0, keepdims=True)
                grad_score = (probs * (grad_prob - inner)).astype(BF16)
                GPT[base : base + 64, cols] = (
                    nn(PT[l, base + 64 : base + 128, :], grad_score) * SCALE
                ).astype(BF16)
                GKT[h] += nt(PT[l, base : base + 64, cols], grad_score)
                GVT[h] += nt(half, probs.astype(BF16))

        gather(GO, l, 3, attend_back)

        for h in range(2):
            base = h * 192
            GPT[base + 64 : base + 128, :] = (GKT[h] * SCALE).astype(BF16)
            GPT[base + 128 : base + 192, :] = GVT[h].astype(BF16)

        def project_back(yy):
            grad_proj = GPT[:, lanes(yy)].T
            SM[l, 7:8, 0:384] += jnp.sum(grad_proj.astype(F32), axis=0, keepdims=True)
            return nn(grad_proj, qkv_weights(l))

        def attend_grads():
            @pl.loop(0, 2)
            def _(b):
                G[l, b, 0:192, :] = nn(GPT[pl.ds(pl.multiple_of(b * 192, 64), 192), :], XF[l]).astype(BF16)
                G[l, b, 192:256, :] = nn(AT[l, pl.ds(pl.multiple_of(b * 64, 64), 64), :], GO[l]).astype(BF16)

            grad_x(l, 0)

        grad_input = (GR[...] + scatter(l, 3, project_back, attend_grads)).astype(BF16)
        GY[...] = grad_input.astype(F32)
        spread_out(grad_input, IG, igout, ig_s, ig_r, l)
        return carry

    lax.fori_loop(0, 2, backward_layer, 0)

    done = []

    def go(cp):
        cp.start()
        done.append(cp)

    row = lax.broadcasted_iota(jnp.int32, (2, 8, 1024), 1)
    go(rc(SM, SMC, sc_s, sc_r, sibling))
    grad_z(0, 1)
    arrived(SMC, sc_r)
    SM1[...] = jnp.where(row < 6, SM[...] + SMC[...], SM[...])
    SMY[y] = SM1[...]
    for r in range(1, 4):
        go(rc(SM1, SMY.at[y], sy_s.at[r], sy_r.at[r], yd(r)))
    grad_z(0, 0)
    for r in range(1, 4):
        arrived(SMY.at[lax.rem(y + 4 - r, 4)], sy_r.at[r])
    SM2[...] = jnp.where(row < 6, (SMY[0] + SMY[1]) + (SMY[2] + SMY[3]), SM1[...])
    SMZ[z] = SM2[zh]
    for k, where, lz in ((0, partner, zh), (1, cross, 1 - zh), (2, far, 1 - zh)):
        go(rc(SM2.at[lz], SMZ.at[z], sz_s.at[k], sz_r.at[k], where))
    grad_own(1)
    for k, zz in ((0, 2 * zh + 1 - zl), (1, 2 * (1 - zh) + 1 - zl), (2, 2 * (1 - zh) + zl)):
        arrived(SMZ.at[zz], sz_r.at[k])
    SM3[...] = (SMZ[0] + SMZ[1]) + (SMZ[2] + SMZ[3])
    SMX[x] = SM3[...]
    for r in range(1, 4):
        go(rc(SM3, SMX.at[x], sx_s.at[r], sx_r.at[r], xd(r)))
    grad_own(0)
    for r in range(1, 4):
        arrived(SMX.at[lax.rem(x + 4 - r, 4)], sx_r.at[r])
    smout[...] = (SMX[0] + SMX[1]) + (SMX[2] + SMX[3])
    spread_wait(LO, lout, lo_s, lo_r)
    spread_wait(IG, igout, ig_s, ig_r)
    grad_done(1)
    grad_done(0)

    x_copy.wait_send()
    c_copy.wait_send()
    for i in range(3):
        for k in range(3):
            w_copy(i, k).wait_send()
    for p in range(2):
        for l in range(2):
            for b in range(2):
                for r in range(1, 4):
                    x_copy_of(l, p, b, r).wait_send()

                @pl.when((2 * l + b) != z)
                def _(l=l, b=b, p=p):
                    z_copy_of(l, p, b).wait_send()
        for r in range(1, 4):
            g_copy_of(p, r).wait_send()
    for cp in done:
        cp.wait_send()


def run_kernel(xs, cs, wb, sv, valid):
    vm = pltpu.VMEM
    dma = pltpu.SemaphoreType.DMA
    scratch = [
        vm((2, 2, 768, 1024), BF16),
        vm((4, 8, 1024), F32),
        vm((2, 512, 1024), BF16),
        vm((2, 512, 1024), BF16),
        vm((2, 512, 1024), BF16),
        vm((2, 512, 1024), BF16),
        vm((2, 32, 1024), BF16),
        vm((2, 512, 384), BF16),
        vm((2, 384, 512), BF16),
        vm((2, 2, 4, 512, 128), F32),
        vm((2, 128, 512), BF16),
        vm((2, 512, 512), BF16),
        vm((2, 4, 128, 512), F32),
        vm((512, 512), BF16),
        vm((384, 512), BF16),
        vm((2, 64, 512), F32),
        vm((2, 64, 512), F32),
        vm((2, 64, 1024), F32),
        vm((2, 64, 1024), F32),
        vm((2, 64, 128), F32),
        vm((2, 64, 128), F32),
        vm((64, 1024), F32),
        vm((64, 1024), F32),
        vm((64, 1024), F32),
        vm((64, 1024), F32),
        vm((4, 128, 1024), BF16),
        vm((4, 64, 1024), BF16),
        vm((4, 64, 1024), BF16),
        vm((4, 64, 1024), BF16),
        vm((2, 2, 768, 1024), BF16),
        vm((2, 2, 3, 64, 1024), BF16),
        vm((2, 2, 3, 128, 1024), BF16),
        vm((2, 2, 64, 1024), BF16),
        vm((2, 2, 128, 1024), BF16),
        vm((3, 64, 1024), BF16),
        vm((3, 128, 1024), BF16),
        vm((2, 2, 32, 1024), BF16),
        vm((2, 2, 32, 1024), BF16),
        vm((2, 8, 1024), F32),
        vm((2, 8, 1024), F32),
        vm((2, 8, 1024), F32),
        vm((4, 2, 8, 1024), F32),
        vm((2, 8, 1024), F32),
        vm((4, 8, 1024), F32),
        vm((8, 1024), F32),
        vm((4, 8, 1024), F32),
        dma((2, 4, 8)),
        dma((2, 4, 8)),
        dma((2, 4, 4)),
        dma((2, 4, 4)),
        dma((2, 4, 4)),
        dma((2, 4, 4)),
        dma((2,)),
        dma((2,)),
        dma(()),
        dma((3, 3)),
        dma((2, 2, 3)),
        dma((2, 2, 2, 3)),
        dma((2, 2, 2, 3)),
        dma((2, 2, 2)),
        dma((2, 3)),
        dma((2, 3)),
        dma((2, 3)),
        dma((2, 2)),
        dma((4,)),
        dma((2, 2)),
        dma((4,)),
        dma(()),
        dma(()),
        dma((4,)),
        dma((4,)),
        dma((3,)),
        dma((3,)),
        dma((4,)),
        dma((4,)),
    ]
    in_vmem = pl.BlockSpec(memory_space=pltpu.VMEM)
    return pl.pallas_call(
        kernel,
        out_shape=(
            jax.ShapeDtypeStruct((4, 32, 1024), BF16),
            jax.ShapeDtypeStruct((4, 32, 1024), BF16),
            jax.ShapeDtypeStruct((768, 1024), BF16),
            jax.ShapeDtypeStruct((8, 1024), F32),
        ),
        in_specs=[in_vmem, in_vmem, pl.BlockSpec(memory_space=pl.ANY), in_vmem, in_vmem],
        out_specs=(in_vmem,) * 4,
        scratch_shapes=scratch,
        compiler_params=pltpu.CompilerParams(
            collective_id=0, has_side_effects=True, vmem_limit_bytes=60 * 1024 * 1024
        ),
        cost_estimate=pl.CostEstimate(flops=10_000_000_000, bytes_accessed=10_000_000, transcendentals=3_000_000),
    )(xs, cs, wb, sv, valid)


def per_device(
    inputs, lengths, cotangent, w_qkv, b_qv, w_out, w_up, b_up, w_down, norm_gains, norm_shifts, out_bias
):
    zh = lax.axis_index("section")
    zl = lax.axis_index("tensor") // 8
    xs = jnp.transpose(lax.dynamic_index_in_dim(inputs, zh, 0, keepdims=False), (1, 0, 2))
    cs = jnp.transpose(lax.dynamic_index_in_dim(cotangent, zh, 0, keepdims=False), (1, 0, 2))
    wb = jnp.concatenate(
        [jnp.transpose(w_qkv[0], (1, 2, 0)).reshape(192, 1024), w_out[0], w_up[0].T, w_down[0]], axis=0
    )
    zeros = jnp.zeros((64,), F32)
    up_row = lax.dynamic_update_slice(jnp.zeros((1024,), F32), b_up[0], (zl * 256,))
    qv_row = lax.dynamic_update_slice(
        jnp.zeros((1024,), F32), jnp.concatenate([b_qv[0, 0], zeros, b_qv[0, 1]]), (zl * 192,)
    )
    sv = jnp.concatenate([norm_gains[0], norm_shifts[0], out_bias[0], up_row[None], qv_row[None]], axis=0)
    length = lax.dynamic_slice(lengths, (zh, zl), (1, 1))
    r = lax.broadcasted_iota(jnp.int32, (512, 128), 0)
    position = ((r // 32) % 2) * 256 + (r // 64) * 32 + r % 32
    valid = (position < length).astype(F32)

    lout, igout, g, sm = run_kernel(xs, cs, wb, sv, valid)

    def place(blocks):
        return jnp.transpose(blocks.reshape(2, 2, 32, 1024), (0, 2, 1, 3))[None]

    g32 = g.astype(F32)
    grad_qkv = jnp.transpose(g32[0:192].reshape(3, 64, 1024), (2, 0, 1))[None]
    qv = lax.dynamic_slice(sm[7], (zl * 192,), (192,))
    up_bias = lax.dynamic_slice(sm[6], (zl * 256,), (256,))
    return (
        place(lout),
        place(igout).astype(F32),
        grad_qkv,
        jnp.stack([qv[0:64], qv[128:192]])[None],
        g32[192:256][None],
        g32[256:512].T[None],
        up_bias[None],
        g32[512:768][None],
        sm[0:2][None],
        sm[2:4][None],
        sm[4:6][None],
    )


def solution(mesh):
    in_specs = (
        P(None, "tensor", "dp", None),
        P(None, "dp"),
        P(None, "tensor", "dp", None),
        P("section", None, None, "tensor"),
        P("section", None, "tensor"),
        P("section", "tensor", None),
        P("section", None, "tensor"),
        P("section", "tensor"),
        P("section", "tensor", None),
        P("section", None, None),
        P("section", None, None),
        P("section", None, None),
    )
    out_specs = (
        P("section", None, "tensor", "dp", None),
        P("section", None, "tensor", "dp", None),
        P("section", None, None, "tensor"),
        P("section", None, "tensor"),
        P("section", "tensor", None),
        P("section", None, "tensor"),
        P("section", "tensor"),
        P("section", "tensor", None),
        P("section", None, None),
        P("section", None, None),
        P("section", None, None),
    )
    return jax.shard_map(per_device, mesh=mesh, in_specs=in_specs, out_specs=out_specs, check_vma=False)
```

```python
import jax
import jax.numpy as jnp
from jax import lax
from jax.experimental import pallas as pl
from jax.experimental.pallas import tpu as pltpu
from jax.sharding import PartitionSpec as P

EPSILON = 1e-12
MASKED = -1e30
F32 = jnp.float32
BF16 = jnp.bfloat16
MESH = pl.DeviceIdType.MESH
INV_SQRT2 = 0.7071067811865476
INV_SQRT_2PI = 0.3989422804014327
SCALE = 0.125

PIECES = ((0, 256), (256, 512))
ALONG_Z = ((0, 128), (256, 192))
QUARTERED = ((128, 128), (448, 320))


def nt(a, b):
    return lax.dot_general(a, b, (((1,), (1,)), ((), ())), preferred_element_type=F32)


def nn(a, b):
    return lax.dot_general(a, b, (((1,), (0,)), ((), ())), preferred_element_type=F32)


def standardize(rows):
    center = jnp.mean(rows, axis=-1, keepdims=True)
    centred = rows - center
    spread = jnp.mean(centred * centred, axis=-1, keepdims=True)
    inv = lax.rsqrt(spread + EPSILON)
    return centred * inv, inv


def standardize_back(grad_out, gain, unit, inv):
    scaled = grad_out * gain
    return inv * (
        scaled
        - jnp.mean(scaled, axis=-1, keepdims=True)
        - unit * jnp.mean(scaled * unit, axis=-1, keepdims=True)
    )


def kernel(
    xs, cs, qkv_in, out_in, up_in, down_in, gains_in, shifts_in, bias_in, b_up_in, b_qv_in, len_in,
    lout, igout, g_a, g_up, g_down, smout,
    valid, sv, gout,
    W, SW, XF, YF, GF, GO, CT, PB, PT, PR, AT, HT, GD, GZT, GPT, GKT, GVT,
    N1, N2, S1, S2, Y1, GR, GY, OWN,
    PART, SIB, SUM, RIN, G, GXA, GXF, QXA, QXF, ZXA, ZXF,
    LO, IG, SM, SMC, SM1, SMY, SM2, SMZ, SM3, SMX,
    ag_s, ag_r, sb_s, sb_r, rs_s, rs_r, in_s, in_r, loc, sv_s, sv_r, wz_s, wz_r, wq_s, wq_r, wx_s, wx_r,
    xr_s, xr_r, gz_s, gz_r, xg_s, xg_r, lo_s, lo_r, ig_s, ig_r,
    sc_s, sc_r, sy_s, sy_r, sz_s, sz_r, sx_s, sx_r,
):
    zh = lax.axis_index("section")
    x = lax.axis_index("dp")
    t = lax.axis_index("tensor")
    zl = t // 8
    y = (t % 8) // 2
    c = t % 2
    d = t % 8
    z = 2 * zh + zl

    def dev(zh_=None, x_=None, zl_=None, y_=None, c_=None):
        zh_ = zh if zh_ is None else zh_
        x_ = x if x_ is None else x_
        zl_ = zl if zl_ is None else zl_
        y_ = y if y_ is None else y_
        c_ = c if c_ is None else c_
        return (zh_, x_, zl_ * 8 + y_ * 2 + c_)

    def yd(r):
        return dev(y_=lax.rem(y + r, 4))

    def xd(r):
        return dev(x_=lax.rem(x + r, 4))

    sibling = dev(c_=1 - c)
    partner = dev(zl_=1 - zl)
    cross = dev(zh_=1 - zh, zl_=1 - zl)
    far = dev(zh_=1 - zh)

    def rc(src, dst, ssem, rsem, where):
        return pltpu.make_async_remote_copy(
            src_ref=src, dst_ref=dst, send_sem=ssem, recv_sem=rsem, device_id=where, device_id_type=MESH
        )

    def arrived(dst, rsem):
        rc(dst, dst, rsem, rsem, sibling).wait_recv()

    barrier = pltpu.get_barrier_semaphore()
    greeted = [sibling, yd(1), yd(2), yd(3), xd(1), xd(2), xd(3), partner, cross, far]
    for other in greeted:
        pl.semaphore_signal(barrier, inc=1, device_id=other, device_id_type=MESH)
    pl.semaphore_wait(barrier, len(greeted))

    def slot(full, l, yy, cc):
        return full.at[l, pl.ds(pl.multiple_of(yy * 128 + cc * 64, 64), 64)]

    def ag_begin(full, l, k):
        mine = slot(full, l, y, c)
        copies = [rc(mine, mine, ag_s.at[l, k, i], ag_r.at[l, k, i], yd(i)) for i in (1, 3, 2)]
        copies.append(rc(mine, mine, ag_s.at[l, k, 4], ag_r.at[l, k, 4], sibling))
        for cp in copies:
            cp.start()
        return copies

    def from_ring(full, l, k, i, copies):
        got = slot(full, l, lax.rem(y + 4 - i, 4), c)
        arrived(got, ag_r.at[l, k, i])
        cp = rc(got, got, ag_s.at[l, k, 4 + i], ag_r.at[l, k, 4 + i], sibling)
        cp.start()
        copies.append(cp)

    def from_sibling(full, l, k, i):
        arrived(slot(full, l, lax.rem(y + 4 - i, 4), 1 - c), ag_r.at[l, k, 4 + i])

    def gather(full, l, k, use):
        copies = ag_begin(full, l, k)
        from_sibling(full, l, k, 0)
        use(y)
        from_ring(full, l, k, 1, copies)
        from_ring(full, l, k, 3, copies)
        from_sibling(full, l, k, 1)
        use(lax.rem(y + 3, 4))
        from_ring(full, l, k, 2, copies)
        from_sibling(full, l, k, 3)
        use(lax.rem(y + 1, 4))
        from_sibling(full, l, k, 2)
        use(lax.rem(y + 2, 4))
        for cp in copies:
            cp.wait_send()

    def make(l, k, r, chunk, copies):
        PART[r] = chunk(lax.rem(y + r, 4)).astype(BF16)
        theirs = PART.at[r, pl.ds(pl.multiple_of((1 - c) * 64, 64), 64)]
        cp = rc(theirs, SIB.at[r], sb_s.at[l, k, r], sb_r.at[l, k, r], sibling)
        cp.start()
        copies.append(cp)

    def both(l, k, r):
        arrived(SIB.at[r], sb_r.at[l, k, r])
        mine = PART[r, pl.ds(pl.multiple_of(c * 64, 64), 64), :]
        return mine.astype(F32) + SIB[r].astype(F32)

    def push(l, k, r, copies):
        SUM[r] = both(l, k, r).astype(BF16)
        cp = rc(SUM.at[r], RIN.at[r], rs_s.at[l, k, r], rs_r.at[l, k, r], yd(r))
        cp.start()
        copies.append(cp)

    def finish(l, k, copies):
        for r in (1, 3, 2):
            arrived(RIN.at[r], rs_r.at[l, k, r])
        total = OWN[...] + ((RIN[1].astype(F32) + RIN[3].astype(F32)) + RIN[2].astype(F32))
        for cp in copies:
            cp.wait_send()
        return total

    def scatter(l, k, chunk, window):
        copies = []
        make(l, k, 2, chunk, copies)
        make(l, k, 1, chunk, copies)
        push(l, k, 2, copies)
        make(l, k, 3, chunk, copies)
        push(l, k, 1, copies)
        make(l, k, 0, chunk, copies)
        push(l, k, 3, copies)
        OWN[...] = both(l, k, 0)
        window()
        return finish(l, k, copies)

    def gather_scatter(full, l, k, chunk, window):
        copies = ag_begin(full, l, k)
        from_sibling(full, l, k, 0)
        make(l, k, 0, chunk, copies)
        from_ring(full, l, k, 1, copies)
        from_ring(full, l, k, 3, copies)
        from_sibling(full, l, k, 1)
        make(l, k, 3, chunk, copies)
        from_ring(full, l, k, 2, copies)
        from_sibling(full, l, k, 3)
        make(l, k, 1, chunk, copies)
        push(l, k, 3, copies)
        from_sibling(full, l, k, 2)
        make(l, k, 2, chunk, copies)
        push(l, k, 1, copies)
        push(l, k, 2, copies)
        OWN[...] = both(l, k, 0)
        window()
        return finish(l, k, copies)

    others = (far, cross, partner)

    def sv_copy(k):
        return rc(sv, SW.at[z], sv_s.at[k], sv_r.at[zh, zl], others[k])

    def wz_copy(i, k):
        rows = W.at[zh, zl, pl.ds(*ALONG_Z[i])]
        return rc(rows, rows, wz_s.at[k, i], wz_r.at[zh, zl, i], others[k])

    def quarter(l, b, i, who):
        base, size = QUARTERED[i]
        n = size // 4
        return W.at[l, b, pl.ds(pl.multiple_of(base + who * n, 16), n)]

    def wq_copy(i, k):
        rows = quarter(zh, zl, i, x)
        return rc(rows, rows, wq_s.at[k, i], wq_r.at[zh, zl, i], others[k])

    def wx_copy(l, b, i, r):
        rows = quarter(l, b, i, x)
        return rc(rows, rows, wx_s.at[l, b, i, r - 1], wx_r.at[l, b, i, r - 1], xd(r))

    def send_own(i):
        for k in range(3):
            wq_copy(i, k).start()
        for k in range(3):
            wz_copy(i, k).start()

    def send_vectors():
        for k in range(3):
            sv_copy(k).start()

    def pass_on(l, i):
        for b in range(2):
            @pl.when((2 * l + b) != z)
            def _(b=b):
                arrived(quarter(l, b, i, x), wq_r.at[l, b, i])
                for r in (2, 1, 3):
                    wx_copy(l, b, i, r).start()

    def vectors_here(l):
        for b in range(2):
            @pl.when((2 * l + b) != z)
            def _(b=b):
                arrived(SW.at[2 * l + b], sv_r.at[l, b])

    def weights_here(l, i):
        for b in range(2):
            @pl.when((2 * l + b) != z)
            def _(b=b):
                arrived(W.at[l, b, pl.ds(*ALONG_Z[i])], wz_r.at[l, b, i])
                for r in (1, 3, 2):
                    arrived(quarter(l, b, i, lax.rem(x + 4 - r, 4)), wx_r.at[l, b, i, r - 1])

    mine_rows = pl.ds(pl.multiple_of(d * 64 + zl * 32, 32), 32)
    x_copy = rc(xs.at[1 - zl], XF.at[0, mine_rows], in_s.at[0], in_r.at[0], partner)
    x_copy.start()
    c_copy = rc(cs.at[1 - zl], CT.at[zl], in_s.at[1], in_r.at[1], partner)

    own_block = W.at[zh, zl]
    loads = [
        pltpu.make_async_copy(src, own_block.at[pl.ds(base, size)], loc.at[i])
        for i, (src, base, size) in enumerate(((qkv_in, 0, 192), (out_in, 192, 64), (down_in, 512, 256)))
    ]
    for load in loads:
        load.start()
    c_copy.start()
    XF[0, mine_rows, :] = xs[zl]
    CT[zl] = cs[zl]
    first = zl == 0
    sv[0:2, :] = gains_in[...]
    sv[2:4, :] = shifts_in[...]
    sv[4:6, :] = bias_in[...]
    sv[6:8, :] = jnp.zeros((2, 1024), F32)
    sv[6:7, 0:256] = jnp.where(first, b_up_in[...], 0.0)
    sv[6:7, 256:512] = jnp.where(first, 0.0, b_up_in[...])
    for i, at in ((0, 0), (1, 128)):
        sv[7:8, at : at + 64] = jnp.where(first, b_qv_in[i : i + 1, :], 0.0)
        sv[7:8, at + 192 : at + 256] = jnp.where(first, 0.0, b_qv_in[i : i + 1, :])
    SW[z] = sv[...]
    loads[0].wait()
    loads[1].wait()

    @pl.when(zh == 0)
    def _():
        send_vectors()
        send_own(0)

    own_block[256:512, :] = up_in[...].T
    loads[2].wait()

    @pl.when(zh == 0)
    def _():
        send_own(1)

    r_ = lax.broadcasted_iota(jnp.int32, (512, 128), 0)
    position = lax.rem(r_ // 32, 2) * 256 + (r_ // 64) * 32 + lax.rem(r_, 32)
    valid[...] = jnp.where(position < len_in[zh, zl], 1.0, 0.0)
    arrived(XF.at[0, pl.ds(pl.multiple_of(d * 64 + (1 - zl) * 32, 32), 32)], in_r.at[0])

    def spread_out(rows, buf, out, s_s, s_r, l):
        buf[l] = rows.reshape(2, 32, 1024)
        for b in range(2):
            @pl.when((2 * l + b) == z)
            def _(b=b):
                out[z] = buf[l, b]

            @pl.when((2 * l + b) != z)
            def _(b=b):
                rc(buf.at[l, b], out.at[z], s_s.at[l, b], s_r.at[z], dev(zh_=l, zl_=b)).start()

    def spread_wait(buf, out, s_s, s_r):
        for k in range(1, 4):
            zz = lax.rem(z + k, 4)
            arrived(out.at[zz], s_r.at[zz])
        for l in range(2):
            for b in range(2):
                @pl.when((2 * l + b) != z)
                def _(l=l, b=b):
                    rc(buf.at[l, b], buf.at[l, b], s_s.at[l, b], s_r.at[z], sibling).wait_send()

    def row_of(l, i):
        return SW[2 * l, pl.ds(i, 1), :]

    own_rows = pl.ds(pl.multiple_of(d * 64, 64), 64)

    def out_weights(l):
        return jnp.concatenate([W[l, 0, 192:256, :], W[l, 1, 192:256, :]], axis=0)

    def qkv_weights(l):
        return jnp.concatenate([W[l, 0, 0:192, :], W[l, 1, 0:192, :]], axis=0)

    def lanes(yy):
        return pl.ds(pl.multiple_of(yy * 128, 128), 128)

    def forward_layer(l, carry):
        seen = []

        def between(yy):
            seen.append(yy)
            if len(seen) in (2, 4):
                @pl.when(l == 0)
                def _():
                    pass_on(0, len(seen) // 2 - 1)

        gather(XF, l, 0, between)
        vectors_here(l)
        weights_here(l, 0)

        @pl.when((l == 0) & (zh == 1))
        def _():
            send_vectors()
            send_own(0)
            send_own(1)

        qv_bias = SW[2 * l, 7:8, 0:384] + SW[2 * l + 1, 7:8, 0:384]
        proj = (nt(XF[l], qkv_weights(l)) + qv_bias).astype(BF16)
        PB[l] = proj
        PT[l] = proj.T

        def attend(yy):
            cols = lanes(yy)
            for h in range(2):
                base = h * 192
                scores = nn(PB[l, :, base + 64 : base + 128], PT[l, base : base + 64, cols]) * SCALE
                scores = jnp.where(valid[...] > 0.5, scores, MASKED)
                terms = jnp.exp(scores - jnp.max(scores, axis=0, keepdims=True))
                probs = terms * (1.0 / jnp.sum(terms, axis=0, keepdims=True))
                PR[l, h, yy] = probs
                mixed = nn(PT[l, base + 128 : base + 192, :], probs.astype(BF16))
                AT[l, h * 64 : h * 64 + 64, cols] = mixed.astype(BF16)
            return nn(AT[l, :, cols].T, out_weights(l))

        def attend_window():
            @pl.when(l == 0)
            def _():
                pass_on(1, 0)
                pass_on(1, 1)

        attended = scatter(l, 0, attend, attend_window)
        unit, inv = standardize(XF[l, own_rows, :].astype(F32) + attended + row_of(l, 4))
        N1[l] = unit
        S1[l] = jnp.broadcast_to(inv, (64, 128))
        middle = unit * row_of(l, 0) + row_of(l, 2)
        Y1[...] = middle
        YF[l, own_rows, :] = middle.astype(BF16)
        weights_here(l, 1)

        up_bias = SW[2 * l, 6:7, 0:512] + SW[2 * l + 1, 6:7, 0:512]

        def feed(yy):
            rows = YF[l, lanes(yy), :]
            total = None
            for b in range(2):
                pre = nt(rows, W[l, b, 256:512, :]) + up_bias[:, b * 256 : b * 256 + 256]
                cdf = 0.5 * (1.0 + lax.erf(pre * INV_SQRT2))
                hidden = (pre * cdf).astype(BF16)
                GD[l, yy, :, b * 256 : b * 256 + 256] = cdf + pre * (INV_SQRT_2PI * jnp.exp(-0.5 * pre * pre))
                HT[l, b * 256 : b * 256 + 256, lanes(yy)] = hidden.T
                piece = nn(hidden, W[l, b, 512:768, :])
                total = piece if total is None else total + piece
            return total

        fed = gather_scatter(YF, l, 1, feed, lambda: None)
        unit, inv = standardize(Y1[...] + fed + row_of(l, 5))
        N2[l] = unit
        S2[l] = jnp.broadcast_to(inv, (64, 128))
        result = (unit * row_of(l, 1) + row_of(l, 3)).astype(BF16)

        @pl.when(l == 0)
        def _():
            XF[1, own_rows, :] = result

        spread_out(result, LO, lout, lo_s, lo_r, l)
        return carry

    lax.fori_loop(0, 2, forward_layer, 0)

    arrived(CT.at[1 - zl], in_r.at[1])
    GY[...] = CT[...].reshape(64, 1024).astype(F32)
    SM[...] = jnp.zeros_like(SM)

    GX, QX, ZX = (GXA, GXF), (QXA, QXF), (ZXA, ZXF)

    def own_part(p, ref, who, *lead):
        base, size = PIECES[p]
        n = size // 4
        return ref.at[(*lead, pl.ds(pl.multiple_of(base + who * n, n), n))]

    def x_copy_of(l, p, b, r):
        src = own_part(p, G, lax.rem(x + r, 4), l, b)
        return rc(src, GX[p].at[l, b, r - 1], xr_s.at[l, p, b, r - 1], xr_r.at[l, p, b, r - 1], xd(r))

    def z_copy_of(l, p, b):
        k = lax.rem(2 * l + b + 4 - z, 4) - 1
        return rc(QX[p].at[l, b], ZX[p].at[k], gz_s.at[l, p, b], gz_r.at[p, k], dev(zh_=l, zl_=b))

    def g_copy_of(p, r):
        mine = own_part(p, gout, x)
        return rc(mine, mine, xg_s.at[p, r - 1], xg_r.at[p, r - 1], xd(r))

    def grad_x(l, p):
        for b in range(2):
            for r in (2, 1, 3):
                x_copy_of(l, p, b, r).start()

    def grad_z(l, p):
        n = PIECES[p][1] // 4
        for b in range(2):
            for r in (1, 3, 2):
                arrived(GX[p].at[l, b, r - 1], xr_r.at[l, p, b, r - 1])
            mine = own_part(p, G, x, l, b)

            @pl.loop(0, n // 32)
            def _(i, b=b, mine=mine):
                rows = pl.ds(pl.multiple_of(i * 32, 32), 32)
                QX[p][l, b, rows, :] = (
                    (mine[rows, :].astype(F32) + GX[p][l, b, 0, rows, :].astype(F32))
                    + (GX[p][l, b, 1, rows, :].astype(F32) + GX[p][l, b, 2, rows, :].astype(F32))
                ).astype(BF16)

            @pl.when((2 * l + b) != z)
            def _(b=b):
                z_copy_of(l, p, b).start()

    def grad_own(p):
        n = PIECES[p][1] // 4
        for k in range(3):
            arrived(ZX[p].at[k], gz_r.at[p, k])
        mine = own_part(p, gout, x)

        @pl.loop(0, n // 32)
        def _(i):
            rows = pl.ds(pl.multiple_of(i * 32, 32), 32)
            mine[rows, :] = (
                (QX[p][zh, zl, rows, :].astype(F32) + ZX[p][0, rows, :].astype(F32))
                + (ZX[p][1, rows, :].astype(F32) + ZX[p][2, rows, :].astype(F32))
            ).astype(BF16)

        for r in (2, 1, 3):
            g_copy_of(p, r).start()

    def grad_done(p):
        for r in (1, 3, 2):
            arrived(own_part(p, gout, lax.rem(x + 4 - r, 4)), xg_r.at[p, r - 1])

    def backward_layer(step, carry):
        l = 1 - step
        grad = GY[...]
        unit = N2[l]
        grad_second = standardize_back(grad, row_of(l, 1), unit, S2[l, :, 0:1])
        SM[l, 1:2, :] = jnp.sum(grad * unit, axis=0, keepdims=True)
        SM[l, 3:4, :] = jnp.sum(grad, axis=0, keepdims=True)
        SM[l, 5:6, :] = jnp.sum(grad_second, axis=0, keepdims=True)
        GR[...] = grad_second
        GF[l, own_rows, :] = grad_second.astype(BF16)
        def feed_back(yy):
            rows = GF[l, lanes(yy), :]
            total = None
            for b in range(2):
                grad_pre = (nt(rows, W[l, b, 512:768, :]) * GD[l, yy, :, b * 256 : b * 256 + 256]).astype(BF16)
                SM[l, 6:7, b * 256 : b * 256 + 256] += jnp.sum(grad_pre.astype(F32), axis=0, keepdims=True)
                GZT[b * 256 : b * 256 + 256, lanes(yy)] = grad_pre.T
                piece = nn(grad_pre, W[l, b, 256:512, :])
                total = piece if total is None else total + piece
            return total

        def feed_grads():
            @pl.loop(0, 2)
            def _(b):
                rows = pl.ds(pl.multiple_of(b * 256, 256), 256)
                G[l, b, 256:512, :] = nn(GZT[rows, :], YF[l]).astype(BF16)
                G[l, b, 512:768, :] = nn(HT[l, rows, :], GF[l]).astype(BF16)

            grad_x(l, 1)

            @pl.when(l == 0)
            def _():
                grad_z(1, 1)
                grad_z(1, 0)

        grad_middle = GR[...] + gather_scatter(GF, l, 2, feed_back, feed_grads)
        unit = N1[l]
        grad_first = standardize_back(grad_middle, row_of(l, 0), unit, S1[l, :, 0:1])
        SM[l, 0:1, :] = jnp.sum(grad_middle * unit, axis=0, keepdims=True)
        SM[l, 2:3, :] = jnp.sum(grad_middle, axis=0, keepdims=True)
        SM[l, 4:5, :] = jnp.sum(grad_first, axis=0, keepdims=True)
        GR[...] = grad_first
        GO[l, own_rows, :] = grad_first.astype(BF16)
        GKT[...] = jnp.zeros_like(GKT)
        GVT[...] = jnp.zeros_like(GVT)

        def attend_back(yy):
            cols = lanes(yy)
            grad_mixed = nt(GO[l, cols, :], out_weights(l)).astype(BF16)
            mixed_t = grad_mixed.T
            for h in range(2):
                base = h * 192
                half = mixed_t[h * 64 : h * 64 + 64, :]
                probs = PR[l, h, yy]
                grad_prob = nn(PB[l, :, base + 128 : base + 192], half)
                inner = jnp.sum(probs * grad_prob, axis=0, keepdims=True)
                grad_score = (probs * (grad_prob - inner)).astype(BF16)
                GPT[base : base + 64, cols] = (
                    nn(PT[l, base + 64 : base + 128, :], grad_score) * SCALE
                ).astype(BF16)
                GKT[h] += nt(PT[l, base : base + 64, cols], grad_score)
                GVT[h] += nt(half, probs.astype(BF16))

        gather(GO, l, 3, attend_back)

        for h in range(2):
            base = h * 192
            GPT[base + 64 : base + 128, :] = (GKT[h] * SCALE).astype(BF16)
            GPT[base + 128 : base + 192, :] = GVT[h].astype(BF16)

        def project_back(yy):
            grad_proj = GPT[:, lanes(yy)].T
            SM[l, 7:8, 0:384] += jnp.sum(grad_proj.astype(F32), axis=0, keepdims=True)
            return nn(grad_proj, qkv_weights(l))

        def attend_grads():
            @pl.loop(0, 2)
            def _(b):
                G[l, b, 0:192, :] = nn(GPT[pl.ds(pl.multiple_of(b * 192, 64), 192), :], XF[l]).astype(BF16)
                G[l, b, 192:256, :] = nn(AT[l, pl.ds(pl.multiple_of(b * 64, 64), 64), :], GO[l]).astype(BF16)

            grad_x(l, 0)

        grad_input = (GR[...] + scatter(l, 3, project_back, attend_grads)).astype(BF16)
        GY[...] = grad_input.astype(F32)
        spread_out(grad_input, IG, igout, ig_s, ig_r, l)
        return carry

    lax.fori_loop(0, 2, backward_layer, 0)

    done = []

    def go(cp):
        cp.start()
        done.append(cp)

    row = lax.broadcasted_iota(jnp.int32, (2, 8, 1024), 1)
    go(rc(SM, SMC, sc_s, sc_r, sibling))
    grad_z(0, 1)
    arrived(SMC, sc_r)
    SM1[...] = jnp.where(row < 6, SM[...] + SMC[...], SM[...])
    SMY[y] = SM1[...]
    for r in range(1, 4):
        go(rc(SM1, SMY.at[y], sy_s.at[r], sy_r.at[r], yd(r)))
    grad_z(0, 0)
    for r in range(1, 4):
        arrived(SMY.at[lax.rem(y + 4 - r, 4)], sy_r.at[r])
    SM2[...] = jnp.where(row < 6, (SMY[0] + SMY[1]) + (SMY[2] + SMY[3]), SM1[...])
    SMZ[z] = SM2[zh]
    for k, where, lz in ((0, partner, zh), (1, cross, 1 - zh), (2, far, 1 - zh)):
        go(rc(SM2.at[lz], SMZ.at[z], sz_s.at[k], sz_r.at[k], where))
    grad_own(1)
    for k, zz in ((0, 2 * zh + 1 - zl), (1, 2 * (1 - zh) + 1 - zl), (2, 2 * (1 - zh) + zl)):
        arrived(SMZ.at[zz], sz_r.at[k])
    SM3[...] = (SMZ[0] + SMZ[1]) + (SMZ[2] + SMZ[3])
    SMX[x] = SM3[...]
    for r in range(1, 4):
        go(rc(SM3, SMX.at[x], sx_s.at[r], sx_r.at[r], xd(r)))
    grad_own(0)
    for r in range(1, 4):
        arrived(SMX.at[lax.rem(x + 4 - r, 4)], sx_r.at[r])
    smout[...] = (SMX[0] + SMX[1]) + (SMX[2] + SMX[3])
    spread_wait(LO, lout, lo_s, lo_r)
    spread_wait(IG, igout, ig_s, ig_r)
    grad_done(1)
    g_up[...] = gout[256:512, :].T
    g_down[...] = gout[512:768, :]
    grad_done(0)
    g_a[...] = gout[0:256, :]

    x_copy.wait_send()
    c_copy.wait_send()
    for k in range(3):
        sv_copy(k).wait_send()
        for i in range(2):
            wz_copy(i, k).wait_send()
            wq_copy(i, k).wait_send()
    for l in range(2):
        for b in range(2):
            @pl.when((2 * l + b) != z)
            def _(l=l, b=b):
                for i in range(2):
                    for r in range(1, 4):
                        wx_copy(l, b, i, r).wait_send()
    for p in range(2):
        for l in range(2):
            for b in range(2):
                for r in range(1, 4):
                    x_copy_of(l, p, b, r).wait_send()

                @pl.when((2 * l + b) != z)
                def _(l=l, b=b, p=p):
                    z_copy_of(l, p, b).wait_send()
        for r in range(1, 4):
            g_copy_of(p, r).wait_send()
    for cp in done:
        cp.wait_send()


def run_kernel(*operands):
    vm = pltpu.VMEM
    dma = pltpu.SemaphoreType.DMA
    scratch = [
        vm((512, 128), F32),
        vm((8, 1024), F32),
        vm((768, 1024), BF16),
        vm((2, 2, 768, 1024), BF16),
        vm((4, 8, 1024), F32),
        vm((2, 512, 1024), BF16),
        vm((2, 512, 1024), BF16),
        vm((2, 512, 1024), BF16),
        vm((2, 512, 1024), BF16),
        vm((2, 32, 1024), BF16),
        vm((2, 512, 384), BF16),
        vm((2, 384, 512), BF16),
        vm((2, 2, 4, 512, 128), F32),
        vm((2, 128, 512), BF16),
        vm((2, 512, 512), BF16),
        vm((2, 4, 128, 512), F32),
        vm((512, 512), BF16),
        vm((384, 512), BF16),
        vm((2, 64, 512), F32),
        vm((2, 64, 512), F32),
        vm((2, 64, 1024), F32),
        vm((2, 64, 1024), F32),
        vm((2, 64, 128), F32),
        vm((2, 64, 128), F32),
        vm((64, 1024), F32),
        vm((64, 1024), F32),
        vm((64, 1024), F32),
        vm((64, 1024), F32),
        vm((4, 128, 1024), BF16),
        vm((4, 64, 1024), BF16),
        vm((4, 64, 1024), BF16),
        vm((4, 64, 1024), BF16),
        vm((2, 2, 768, 1024), BF16),
        vm((2, 2, 3, 64, 1024), BF16),
        vm((2, 2, 3, 128, 1024), BF16),
        vm((2, 2, 64, 1024), BF16),
        vm((2, 2, 128, 1024), BF16),
        vm((3, 64, 1024), BF16),
        vm((3, 128, 1024), BF16),
        vm((2, 2, 32, 1024), BF16),
        vm((2, 2, 32, 1024), BF16),
        vm((2, 8, 1024), F32),
        vm((2, 8, 1024), F32),
        vm((2, 8, 1024), F32),
        vm((4, 2, 8, 1024), F32),
        vm((2, 8, 1024), F32),
        vm((4, 8, 1024), F32),
        vm((8, 1024), F32),
        vm((4, 8, 1024), F32),
        dma((2, 4, 8)),
        dma((2, 4, 8)),
        dma((2, 4, 4)),
        dma((2, 4, 4)),
        dma((2, 4, 4)),
        dma((2, 4, 4)),
        dma((2,)),
        dma((2,)),
        dma((3,)),
        dma((3,)),
        dma((2, 2)),
        dma((3, 2)),
        dma((2, 2, 2)),
        dma((3, 2)),
        dma((2, 2, 2)),
        dma((2, 2, 2, 3)),
        dma((2, 2, 2, 3)),
        dma((2, 2, 2, 3)),
        dma((2, 2, 2, 3)),
        dma((2, 2, 2)),
        dma((2, 3)),
        dma((2, 3)),
        dma((2, 3)),
        dma((2, 2)),
        dma((4,)),
        dma((2, 2)),
        dma((4,)),
        dma(()),
        dma(()),
        dma((4,)),
        dma((4,)),
        dma((3,)),
        dma((3,)),
        dma((4,)),
        dma((4,)),
    ]
    in_vmem = pl.BlockSpec(memory_space=pltpu.VMEM)
    hbm = pl.BlockSpec(memory_space=pl.ANY)
    return pl.pallas_call(
        kernel,
        out_shape=(
            jax.ShapeDtypeStruct((4, 32, 1024), BF16),
            jax.ShapeDtypeStruct((4, 32, 1024), BF16),
            jax.ShapeDtypeStruct((256, 1024), BF16),
            jax.ShapeDtypeStruct((1024, 256), BF16),
            jax.ShapeDtypeStruct((256, 1024), BF16),
            jax.ShapeDtypeStruct((8, 1024), F32),
        ),
        in_specs=[in_vmem] * 2 + [hbm] * 2 + [in_vmem, hbm] + [in_vmem] * 5 + [pl.BlockSpec(memory_space=pltpu.SMEM)],
        out_specs=(in_vmem,) * 6,
        scratch_shapes=scratch,
        compiler_params=pltpu.CompilerParams(
            collective_id=0, has_side_effects=True, vmem_limit_bytes=60 * 1024 * 1024
        ),
        cost_estimate=pl.CostEstimate(flops=10_000_000_000, bytes_accessed=10_000_000, transcendentals=3_000_000),
    )(*operands)


def per_device(
    inputs, lengths, cotangent, w_qkv, b_qv, w_out, w_up, b_up, w_down, norm_gains, norm_shifts, out_bias
):
    zh = lax.axis_index("section")
    zl = lax.axis_index("tensor") // 8
    xs = jnp.transpose(lax.dynamic_index_in_dim(inputs, zh, 0, keepdims=False), (1, 0, 2))
    cs = jnp.transpose(lax.dynamic_index_in_dim(cotangent, zh, 0, keepdims=False), (1, 0, 2))
    qkv_rows = jnp.transpose(w_qkv[0], (1, 2, 0)).reshape(192, 1024)
    lout, igout, g_a, g_up, g_down, sm = run_kernel(
        xs, cs, qkv_rows, w_out[0], w_up[0], w_down[0], norm_gains[0], norm_shifts[0], out_bias[0], b_up, b_qv[0], lengths
    )

    def place(blocks):
        return jnp.transpose(blocks.reshape(2, 2, 32, 1024), (0, 2, 1, 3))[None]

    grad_qkv = jnp.transpose(g_a[0:192].astype(F32).reshape(3, 64, 1024), (2, 0, 1))[None]
    qv = lax.dynamic_slice(sm[7], (zl * 192,), (192,))
    up_bias = lax.dynamic_slice(sm[6], (zl * 256,), (256,))
    return (
        place(lout),
        place(igout).astype(F32),
        grad_qkv,
        jnp.stack([qv[0:64], qv[128:192]])[None],
        g_a[192:256].astype(F32)[None],
        g_up.astype(F32)[None],
        up_bias[None],
        g_down.astype(F32)[None],
        sm[0:2][None],
        sm[2:4][None],
        sm[4:6][None],
    )


def solution(mesh):
    in_specs = (
        P(None, "tensor", "dp", None),
        P(None, "dp"),
        P(None, "tensor", "dp", None),
        P("section", None, None, "tensor"),
        P("section", None, "tensor"),
        P("section", "tensor", None),
        P("section", None, "tensor"),
        P("section", "tensor"),
        P("section", "tensor", None),
        P("section", None, None),
        P("section", None, None),
        P("section", None, None),
    )
    out_specs = (
        P("section", None, "tensor", "dp", None),
        P("section", None, "tensor", "dp", None),
        P("section", None, None, "tensor"),
        P("section", None, "tensor"),
        P("section", "tensor", None),
        P("section", None, "tensor"),
        P("section", "tensor"),
        P("section", "tensor", None),
        P("section", None, None),
        P("section", None, None),
        P("section", None, None),
    )
    return jax.shard_map(per_device, mesh=mesh, in_specs=in_specs, out_specs=out_specs, check_vma=False)
```

```python
import jax
import jax.numpy as jnp
from jax import lax
from jax.experimental import pallas as pl
from jax.experimental.pallas import tpu as pltpu
from jax.sharding import PartitionSpec as P

EPSILON = 1e-12
MASKED = -1e30
F32 = jnp.float32
BF16 = jnp.bfloat16
MESH = pl.DeviceIdType.MESH
INV_SQRT2 = 0.7071067811865476
INV_SQRT_2PI = 0.3989422804014327
SCALE = 0.125

PIECES = ((0, 256), (256, 512))
ALONG_Z = ((0, 128), (256, 192))
QUARTERED = ((128, 128), (448, 320))


def nt(a, b):
    return lax.dot_general(a, b, (((1,), (1,)), ((), ())), preferred_element_type=F32)


def nn(a, b):
    return lax.dot_general(a, b, (((1,), (0,)), ((), ())), preferred_element_type=F32)


def standardize(rows):
    center = jnp.mean(rows, axis=-1, keepdims=True)
    centred = rows - center
    spread = jnp.mean(centred * centred, axis=-1, keepdims=True)
    inv = lax.rsqrt(spread + EPSILON)
    return centred * inv, inv


def standardize_back(grad_out, gain, unit, inv):
    scaled = grad_out * gain
    return inv * (
        scaled
        - jnp.mean(scaled, axis=-1, keepdims=True)
        - unit * jnp.mean(scaled * unit, axis=-1, keepdims=True)
    )


def kernel(
    xs, cs, qkv_in, out_in, up_in, down_in, gains_in, shifts_in, bias_in, b_up_in, b_qv_in, len_in,
    lout, igout, gout, smout,
    valid, sv,
    W, SW, XF, YF, GF, GO, CT, PB, PT, PR, AT, HT, GD, CDF, HB, GZT, GPT, GKT, GVT,
    N1, N2, S1, S2, Y1, GR, GY, OWN,
    PART, SIB, SUM, RIN, G, GXA, GXF, QXA, QXF, ZXA, ZXF,
    LO, IG, SM, SMN, SMC, SM1, SMY, SM2, SMZ, SM3, SMX,
    ag_s, ag_r, sb_s, sb_r, rs_s, rs_r, in_s, in_r, loc, sv_s, sv_r, wz_s, wz_r, wq_s, wq_r, wx_s, wx_r,
    xr_s, xr_r, gz_s, gz_r, xg_s, xg_r, lo_s, lo_r, ig_s, ig_r,
    sc_s, sc_r, sy_s, sy_r, sz_s, sz_r, sx_s, sx_r,
):
    zh = lax.axis_index("section")
    x = lax.axis_index("dp")
    t = lax.axis_index("tensor")
    zl = t // 8
    y = (t % 8) // 2
    c = t % 2
    d = t % 8
    z = 2 * zh + zl

    def dev(zh_=None, x_=None, zl_=None, y_=None, c_=None):
        zh_ = zh if zh_ is None else zh_
        x_ = x if x_ is None else x_
        zl_ = zl if zl_ is None else zl_
        y_ = y if y_ is None else y_
        c_ = c if c_ is None else c_
        return (zh_, x_, zl_ * 8 + y_ * 2 + c_)

    def yd(r):
        return dev(y_=lax.rem(y + r, 4))

    def xd(r):
        return dev(x_=lax.rem(x + r, 4))

    sibling = dev(c_=1 - c)
    partner = dev(zl_=1 - zl)
    cross = dev(zh_=1 - zh, zl_=1 - zl)
    far = dev(zh_=1 - zh)

    def rc(src, dst, ssem, rsem, where):
        return pltpu.make_async_remote_copy(
            src_ref=src, dst_ref=dst, send_sem=ssem, recv_sem=rsem, device_id=where, device_id_type=MESH
        )

    def arrived(dst, rsem):
        rc(dst, dst, rsem, rsem, sibling).wait_recv()

    barrier = pltpu.get_barrier_semaphore()
    greeted = [sibling, yd(1), yd(2), yd(3), xd(1), xd(2), xd(3), partner, cross, far]
    for other in greeted:
        pl.semaphore_signal(barrier, inc=1, device_id=other, device_id_type=MESH)
    pl.semaphore_wait(barrier, len(greeted))

    def slot(full, l, yy, cc):
        return full.at[l, pl.ds(pl.multiple_of(yy * 128 + cc * 64, 64), 64)]

    def ag_begin(full, l, k):
        mine = slot(full, l, y, c)
        copies = [rc(mine, mine, ag_s.at[l, k, i], ag_r.at[l, k, i], yd(i)) for i in (1, 3, 2)]
        copies.append(rc(mine, mine, ag_s.at[l, k, 4], ag_r.at[l, k, 4], sibling))
        for cp in copies:
            cp.start()
        return copies

    def from_ring(full, l, k, i, copies):
        got = slot(full, l, lax.rem(y + 4 - i, 4), c)
        arrived(got, ag_r.at[l, k, i])
        cp = rc(got, got, ag_s.at[l, k, 4 + i], ag_r.at[l, k, 4 + i], sibling)
        cp.start()
        copies.append(cp)

    def from_sibling(full, l, k, i):
        arrived(slot(full, l, lax.rem(y + 4 - i, 4), 1 - c), ag_r.at[l, k, 4 + i])

    def gather(full, l, k, use):
        copies = ag_begin(full, l, k)
        from_sibling(full, l, k, 0)
        use(y)
        from_ring(full, l, k, 1, copies)
        from_ring(full, l, k, 3, copies)
        from_sibling(full, l, k, 1)
        use(lax.rem(y + 3, 4))
        from_ring(full, l, k, 2, copies)
        from_sibling(full, l, k, 3)
        use(lax.rem(y + 1, 4))
        from_sibling(full, l, k, 2)
        use(lax.rem(y + 2, 4))
        return copies

    def make(l, k, r, chunk, copies):
        PART[r] = chunk(lax.rem(y + r, 4)).astype(BF16)
        theirs = PART.at[r, pl.ds(pl.multiple_of((1 - c) * 64, 64), 64)]
        cp = rc(theirs, SIB.at[r], sb_s.at[l, k, r], sb_r.at[l, k, r], sibling)
        cp.start()
        copies.append(cp)

    def both(l, k, r):
        arrived(SIB.at[r], sb_r.at[l, k, r])
        mine = PART[r, pl.ds(pl.multiple_of(c * 64, 64), 64), :]
        return mine.astype(F32) + SIB[r].astype(F32)

    def push(l, k, r, pushes):
        SUM[r] = both(l, k, r).astype(BF16)
        cp = rc(SUM.at[r], RIN.at[r], rs_s.at[l, k, r], rs_r.at[l, k, r], yd(r))
        cp.start()
        pushes.append(cp)

    def finish(l, k, copies, pushes):
        for cp in copies:
            cp.wait_send()
        for r in (1, 3, 2):
            arrived(RIN.at[r], rs_r.at[l, k, r])
        total = OWN[...] + ((RIN[1].astype(F32) + RIN[3].astype(F32)) + RIN[2].astype(F32))
        for cp in pushes:
            cp.wait_send()
        return total

    def scatter(l, k, chunk, window, copies, midway=lambda: None):
        pushes = []
        make(l, k, 2, chunk, copies)
        make(l, k, 1, chunk, copies)
        push(l, k, 2, pushes)
        make(l, k, 3, chunk, copies)
        push(l, k, 1, pushes)
        midway()
        make(l, k, 0, chunk, copies)
        push(l, k, 3, pushes)
        OWN[...] = both(l, k, 0)
        window()
        return finish(l, k, copies, pushes)

    def gather_scatter(full, l, k, chunk, window):
        mine = slot(full, l, y, c)
        pushes = []

        def to_ring(i):
            return rc(mine, mine, ag_s.at[l, k, i], ag_r.at[l, k, i], yd(i))

        copies = [rc(mine, mine, ag_s.at[l, k, 4], ag_r.at[l, k, 4], sibling), to_ring(1), to_ring(3)]
        for cp in copies:
            cp.start()
        from_sibling(full, l, k, 0)
        make(l, k, 0, chunk, copies)
        cp = to_ring(2)
        cp.start()
        copies.append(cp)
        from_ring(full, l, k, 1, copies)
        from_ring(full, l, k, 3, copies)
        from_sibling(full, l, k, 1)
        make(l, k, 3, chunk, copies)
        from_sibling(full, l, k, 3)
        make(l, k, 1, chunk, copies)
        push(l, k, 3, pushes)
        push(l, k, 1, pushes)
        from_ring(full, l, k, 2, copies)
        from_sibling(full, l, k, 2)
        make(l, k, 2, chunk, copies)
        push(l, k, 2, pushes)
        OWN[...] = both(l, k, 0)
        window()
        return finish(l, k, copies, pushes)

    others = (far, cross, partner)

    def sv_copy(k):
        return rc(sv, SW.at[z], sv_s.at[k], sv_r.at[zh, zl], others[k])

    def wz_copy(i, k):
        rows = W.at[zh, zl, pl.ds(*ALONG_Z[i])]
        return rc(rows, rows, wz_s.at[k, i], wz_r.at[zh, zl, i], others[k])

    def quarter(l, b, i, who):
        base, size = QUARTERED[i]
        n = size // 4
        return W.at[l, b, pl.ds(pl.multiple_of(base + who * n, 16), n)]

    def wq_copy(i, k):
        rows = quarter(zh, zl, i, x)
        return rc(rows, rows, wq_s.at[k, i], wq_r.at[zh, zl, i], others[k])

    def wx_copy(l, b, i, r):
        rows = quarter(l, b, i, x)
        return rc(rows, rows, wx_s.at[l, b, i, r - 1], wx_r.at[l, b, i, r - 1], xd(r))

    def send_quarter(i):
        for k in range(3):
            wq_copy(i, k).start()

    def send_rest(i):
        for k in range(3):
            wz_copy(i, k).start()

    def send_vectors():
        for k in range(3):
            sv_copy(k).start()

    def pass_on(l, i):
        for b in range(2):
            @pl.when((2 * l + b) != z)
            def _(b=b):
                arrived(quarter(l, b, i, x), wq_r.at[l, b, i])
                for r in (2, 1, 3):
                    wx_copy(l, b, i, r).start()

    def vectors_here(l):
        for b in range(2):
            @pl.when((2 * l + b) != z)
            def _(b=b):
                arrived(SW.at[2 * l + b], sv_r.at[l, b])

    def weights_here(l, i):
        for b in range(2):
            @pl.when((2 * l + b) != z)
            def _(b=b):
                arrived(W.at[l, b, pl.ds(*ALONG_Z[i])], wz_r.at[l, b, i])
                for r in (1, 3, 2):
                    arrived(quarter(l, b, i, lax.rem(x + 4 - r, 4)), wx_r.at[l, b, i, r - 1])

    mine_rows = pl.ds(pl.multiple_of(d * 64 + zl * 32, 32), 32)
    x_copy = rc(xs.at[1 - zl], XF.at[0, mine_rows], in_s.at[0], in_r.at[0], partner)
    x_copy.start()
    c_copy = rc(cs.at[1 - zl], CT.at[zl], in_s.at[1], in_r.at[1], partner)

    own_block = W.at[zh, zl]
    loads = [
        pltpu.make_async_copy(src, own_block.at[pl.ds(base, size)], loc.at[i])
        for i, (src, base, size) in enumerate(((qkv_in, 0, 192), (out_in, 192, 64), (down_in, 512, 256)))
    ]
    for load in loads:
        load.start()
    c_copy.start()
    XF[0, mine_rows, :] = xs[zl]
    CT[zl] = cs[zl]
    first = zl == 0
    sv[0:2, :] = gains_in[...]
    sv[2:4, :] = shifts_in[...]
    sv[4:6, :] = bias_in[...]
    sv[6:8, :] = jnp.zeros((2, 1024), F32)
    sv[6:7, 0:256] = jnp.where(first, b_up_in[...], 0.0)
    sv[6:7, 256:512] = jnp.where(first, 0.0, b_up_in[...])
    for i, at in ((0, 0), (1, 128)):
        sv[7:8, at : at + 64] = jnp.where(first, b_qv_in[i : i + 1, :], 0.0)
        sv[7:8, at + 192 : at + 256] = jnp.where(first, 0.0, b_qv_in[i : i + 1, :])
    SW[z] = sv[...]
    loads[0].wait()
    loads[1].wait()

    @pl.when(zh == 0)
    def _():
        send_vectors()
        send_quarter(0)
        send_rest(0)

    own_block[256:512, :] = up_in[...].T
    loads[2].wait()
    r_ = lax.broadcasted_iota(jnp.int32, (512, 128), 0)
    position = lax.rem(r_ // 32, 2) * 256 + (r_ // 64) * 32 + lax.rem(r_, 32)
    valid[...] = jnp.where(position < len_in[zh, zl], 1.0, 0.0)
    arrived(XF.at[0, pl.ds(pl.multiple_of(d * 64 + (1 - zl) * 32, 32), 32)], in_r.at[0])

    def spread_out(rows, buf, out, s_s, s_r, l):
        buf[l] = rows.reshape(2, 32, 1024)
        for b in range(2):
            @pl.when((2 * l + b) == z)
            def _(b=b):
                out[z] = buf[l, b]

            @pl.when((2 * l + b) != z)
            def _(b=b):
                rc(buf.at[l, b], out.at[z], s_s.at[l, b], s_r.at[z], dev(zh_=l, zl_=b)).start()

    def spread_wait(buf, out, s_s, s_r):
        for k in range(1, 4):
            zz = lax.rem(z + k, 4)
            arrived(out.at[zz], s_r.at[zz])
        for l in range(2):
            for b in range(2):
                @pl.when((2 * l + b) != z)
                def _(l=l, b=b):
                    rc(buf.at[l, b], buf.at[l, b], s_s.at[l, b], s_r.at[z], sibling).wait_send()

    def row_of(l, i):
        return SW[2 * l, pl.ds(i, 1), :]

    own_rows = pl.ds(pl.multiple_of(d * 64, 64), 64)

    def out_weights(l):
        return jnp.concatenate([W[l, 0, 192:256, :], W[l, 1, 192:256, :]], axis=0)

    def qkv_weights(l):
        return jnp.concatenate([W[l, 0, 0:192, :], W[l, 1, 0:192, :]], axis=0)

    def lanes(yy):
        return pl.ds(pl.multiple_of(yy * 128, 128), 128)

    def forward_layer(l, carry):
        seen = []

        def between(yy):
            seen.append(yy)
            if len(seen) == 2:
                @pl.when((l == 0) & (zh == 0))
                def _():
                    send_quarter(1)

                @pl.when(l == 0)
                def _():
                    pass_on(0, 0)

        x_copies = gather(XF, l, 0, between)

        @pl.when((l == 0) & (zh == 0))
        def _():
            send_rest(1)

        vectors_here(l)
        weights_here(l, 0)
        qv_bias = SW[2 * l, 7:8, 0:384] + SW[2 * l + 1, 7:8, 0:384]
        proj = (nt(XF[l], qkv_weights(l)) + qv_bias).astype(BF16)
        PB[l] = proj
        PT[l] = proj.T


        def attend(yy):
            cols = lanes(yy)
            for h in range(2):
                base = h * 192
                scores = nn(PB[l, :, base + 64 : base + 128], PT[l, base : base + 64, cols]) * SCALE
                scores = jnp.where(valid[...] > 0.5, scores, MASKED)
                terms = jnp.exp(scores - jnp.max(scores, axis=0, keepdims=True))
                probs = terms * (1.0 / jnp.sum(terms, axis=0, keepdims=True))
                PR[l, h, yy] = probs
                mixed = nn(PT[l, base + 128 : base + 192, :], probs.astype(BF16))
                AT[l, h * 64 : h * 64 + 64, cols] = mixed.astype(BF16)
            return nn(AT[l, :, cols].T, out_weights(l))

        def attend_midway():
            @pl.when(l == 0)
            def _():
                pass_on(0, 1)

        def attend_window():
            @pl.when((l == 0) & (zh == 1))
            def _():
                send_vectors()
                send_quarter(0)
                send_rest(0)
                send_quarter(1)

        attended = scatter(l, 0, attend, attend_window, x_copies, attend_midway)
        unit, inv = standardize(XF[l, own_rows, :].astype(F32) + attended + row_of(l, 4))
        N1[l] = unit
        S1[l] = jnp.broadcast_to(inv, (64, 128))
        middle = unit * row_of(l, 0) + row_of(l, 2)
        Y1[...] = middle
        YF[l, own_rows, :] = middle.astype(BF16)
        weights_here(l, 1)

        up_bias = SW[2 * l, 6:7, 0:512] + SW[2 * l + 1, 6:7, 0:512]

        def feed(yy):
            rows = YF[l, lanes(yy), :]
            total = None
            for b in range(2):
                pre = nt(rows, W[l, b, 256:512, :]) + up_bias[:, b * 256 : b * 256 + 256]
                cdf = 0.5 * (1.0 + lax.erf(pre * INV_SQRT2))
                hidden = (pre * cdf).astype(BF16)
                cols = pl.ds(b * 256, 256)
                GD[l, yy, :, cols] = pre
                CDF[yy, :, cols] = cdf
                HB[yy, :, cols] = hidden
                piece = nn(hidden, W[l, b, 512:768, :])
                total = piece if total is None else total + piece
            return total

        def feed_window():
            @pl.loop(0, 4)
            def _(yy):
                HT[l, :, lanes(yy)] = HB[yy].T
                pre = GD[l, yy]
                GD[l, yy] = CDF[yy] + pre * (INV_SQRT_2PI * jnp.exp(-0.5 * pre * pre))

            @pl.when(l == 0)
            def _():
                pass_on(1, 0)
                pass_on(1, 1)

            @pl.when((l == 0) & (zh == 1))
            def _():
                send_rest(1)

        fed = gather_scatter(YF, l, 1, feed, feed_window)
        unit, inv = standardize(Y1[...] + fed + row_of(l, 5))
        N2[l] = unit
        S2[l] = jnp.broadcast_to(inv, (64, 128))
        result = (unit * row_of(l, 1) + row_of(l, 3)).astype(BF16)

        @pl.when(l == 0)
        def _():
            XF[1, own_rows, :] = result

        spread_out(result, LO, lout, lo_s, lo_r, l)
        return carry

    lax.fori_loop(0, 2, forward_layer, 0)

    arrived(CT.at[1 - zl], in_r.at[1])
    GY[...] = CT[...].reshape(64, 1024).astype(F32)
    SM[...] = jnp.zeros_like(SM)
    SMN[...] = jnp.zeros_like(SMN)
    norm_pair = rc(SMN, SMC, sc_s, sc_r, sibling)
    norm_ring = [rc(SM1, SMY.at[y], sy_s.at[r], sy_r.at[r], yd(r)) for r in range(1, 4)]

    GX, QX, ZX = (GXA, GXF), (QXA, QXF), (ZXA, ZXF)

    def own_part(p, ref, who, *lead):
        base, size = PIECES[p]
        n = size // 4
        return ref.at[(*lead, pl.ds(pl.multiple_of(base + who * n, n), n))]

    def x_copy_of(l, p, b, r):
        src = own_part(p, G, lax.rem(x + r, 4), l, b)
        return rc(src, GX[p].at[l, b, r - 1], xr_s.at[l, p, b, r - 1], xr_r.at[l, p, b, r - 1], xd(r))

    def z_copy_of(l, p, b):
        k = lax.rem(2 * l + b + 4 - z, 4) - 1
        return rc(QX[p].at[l, b], ZX[p].at[k], gz_s.at[l, p, b], gz_r.at[p, k], dev(zh_=l, zl_=b))

    def g_copy_of(p, r):
        mine = own_part(p, gout, x)
        return rc(mine, mine, xg_s.at[p, r - 1], xg_r.at[p, r - 1], xd(r))

    def grad_x(l, p):
        for b in range(2):
            for r in (2, 1, 3):
                x_copy_of(l, p, b, r).start()

    def grad_z(l, p):
        n = PIECES[p][1] // 4
        for b in range(2):
            for r in (1, 3, 2):
                arrived(GX[p].at[l, b, r - 1], xr_r.at[l, p, b, r - 1])
            mine = own_part(p, G, x, l, b)

            @pl.loop(0, n // 32)
            def _(i, b=b, mine=mine):
                rows = pl.ds(pl.multiple_of(i * 32, 32), 32)
                QX[p][l, b, rows, :] = (
                    (mine[rows, :].astype(F32) + GX[p][l, b, 0, rows, :].astype(F32))
                    + (GX[p][l, b, 1, rows, :].astype(F32) + GX[p][l, b, 2, rows, :].astype(F32))
                ).astype(BF16)

            @pl.when((2 * l + b) != z)
            def _(b=b):
                z_copy_of(l, p, b).start()

    def grad_own(p):
        n = PIECES[p][1] // 4
        for k in range(3):
            arrived(ZX[p].at[k], gz_r.at[p, k])
        mine = own_part(p, gout, x)

        @pl.loop(0, n // 32)
        def _(i):
            rows = pl.ds(pl.multiple_of(i * 32, 32), 32)
            mine[rows, :] = (
                (QX[p][zh, zl, rows, :].astype(F32) + ZX[p][0, rows, :].astype(F32))
                + (ZX[p][1, rows, :].astype(F32) + ZX[p][2, rows, :].astype(F32))
            ).astype(BF16)

        for r in (2, 1, 3):
            g_copy_of(p, r).start()

    def grad_done(p):
        for r in (1, 3, 2):
            arrived(own_part(p, gout, lax.rem(x + 4 - r, 4)), xg_r.at[p, r - 1])

    def backward_layer(step, carry):
        l = 1 - step
        grad = GY[...]
        unit = N2[l]
        grad_second = standardize_back(grad, row_of(l, 1), unit, S2[l, :, 0:1])
        SMN[l, 1:2, :] = jnp.sum(grad * unit, axis=0, keepdims=True)
        SMN[l, 3:4, :] = jnp.sum(grad, axis=0, keepdims=True)
        SMN[l, 5:6, :] = jnp.sum(grad_second, axis=0, keepdims=True)
        GR[...] = grad_second
        GF[l, own_rows, :] = grad_second.astype(BF16)
        def feed_back(yy):
            rows = GF[l, lanes(yy), :]
            total = None
            for b in range(2):
                grad_pre = (nt(rows, W[l, b, 512:768, :]) * GD[l, yy, :, b * 256 : b * 256 + 256]).astype(BF16)
                HB[yy, :, pl.ds(b * 256, 256)] = grad_pre
                piece = nn(grad_pre, W[l, b, 256:512, :])
                total = piece if total is None else total + piece
            return total

        def feed_grads():
            @pl.loop(0, 4)
            def _(yy):
                grad_pre = HB[yy]
                GZT[:, lanes(yy)] = grad_pre.T
                SM[l, 6:7, 0:512] += jnp.sum(grad_pre.astype(F32), axis=0, keepdims=True)

            @pl.loop(0, 2)
            def _(b):
                rows = pl.ds(pl.multiple_of(b * 256, 256), 256)
                G[l, b, 256:512, :] = nn(GZT[rows, :], YF[l]).astype(BF16)
                G[l, b, 512:768, :] = nn(HT[l, rows, :], GF[l]).astype(BF16)

            grad_x(l, 1)

            @pl.when(l == 0)
            def _():
                grad_z(1, 1)
                grad_z(1, 0)

        grad_middle = GR[...] + gather_scatter(GF, l, 2, feed_back, feed_grads)
        unit = N1[l]
        grad_first = standardize_back(grad_middle, row_of(l, 0), unit, S1[l, :, 0:1])
        SMN[l, 0:1, :] = jnp.sum(grad_middle * unit, axis=0, keepdims=True)
        SMN[l, 2:3, :] = jnp.sum(grad_middle, axis=0, keepdims=True)
        SMN[l, 4:5, :] = jnp.sum(grad_first, axis=0, keepdims=True)
        GR[...] = grad_first
        GO[l, own_rows, :] = grad_first.astype(BF16)
        GKT[...] = jnp.zeros_like(GKT)
        GVT[...] = jnp.zeros_like(GVT)

        def attend_back(yy):
            cols = lanes(yy)
            grad_mixed = nt(GO[l, cols, :], out_weights(l)).astype(BF16)
            mixed_t = grad_mixed.T
            for h in range(2):
                base = h * 192
                half = mixed_t[h * 64 : h * 64 + 64, :]
                probs = PR[l, h, yy]
                grad_prob = nn(PB[l, :, base + 128 : base + 192], half)
                inner = jnp.sum(probs * grad_prob, axis=0, keepdims=True)
                grad_score = (probs * (grad_prob - inner)).astype(BF16)
                GPT[base : base + 64, cols] = (
                    nn(PT[l, base + 64 : base + 128, :], grad_score) * SCALE
                ).astype(BF16)
                GKT[h] += nt(PT[l, base : base + 64, cols], grad_score)
                GVT[h] += nt(half, probs.astype(BF16))

        @pl.when(l == 0)
        def _():
            norm_pair.start()

        o_copies = gather(GO, l, 3, attend_back)

        @pl.when(l == 0)
        def _():
            arrived(SMC, sc_r)
            SM1[...] = SMN[...] + SMC[...]
            SMY[y] = SM1[...]
            for cp in norm_ring:
                cp.start()


        for h in range(2):
            base = h * 192
            GPT[base + 64 : base + 128, :] = (GKT[h] * SCALE).astype(BF16)
            GPT[base + 128 : base + 192, :] = GVT[h].astype(BF16)

        def attend_grads():
            @pl.loop(0, 2)
            def _(b):
                G[l, b, 0:192, :] = nn(GPT[pl.ds(pl.multiple_of(b * 192, 64), 192), :], XF[l]).astype(BF16)
                G[l, b, 192:256, :] = nn(AT[l, pl.ds(pl.multiple_of(b * 64, 64), 64), :], GO[l]).astype(BF16)

            grad_x(l, 0)

        pl.when(l == 0)(attend_grads)

        def project_back(yy):
            grad_proj = GPT[:, lanes(yy)].T
            SM[l, 7:8, 0:384] += jnp.sum(grad_proj.astype(F32), axis=0, keepdims=True)
            return nn(grad_proj, qkv_weights(l))

        grad_input = (GR[...] + scatter(l, 3, project_back, lambda: pl.when(l == 1)(attend_grads), o_copies)).astype(BF16)
        GY[...] = grad_input.astype(F32)
        spread_out(grad_input, IG, igout, ig_s, ig_r, l)
        return carry

    lax.fori_loop(0, 2, backward_layer, 0)

    done = []

    def go(cp):
        cp.start()
        done.append(cp)

    for r in range(1, 4):
        arrived(SMY.at[lax.rem(y + 4 - r, 4)], sy_r.at[r])
    SM2[...] = ((SMY[0] + SMY[1]) + (SMY[2] + SMY[3])) + SM[...]
    SMZ[z] = SM2[zh]
    for k, where, lz in ((0, partner, zh), (1, cross, 1 - zh), (2, far, 1 - zh)):
        go(rc(SM2.at[lz], SMZ.at[z], sz_s.at[k], sz_r.at[k], where))
    grad_z(0, 1)
    grad_z(0, 0)
    grad_own(1)
    for k, zz in ((0, 2 * zh + 1 - zl), (1, 2 * (1 - zh) + 1 - zl), (2, 2 * (1 - zh) + zl)):
        arrived(SMZ.at[zz], sz_r.at[k])
    SM3[...] = (SMZ[0] + SMZ[1]) + (SMZ[2] + SMZ[3])
    SMX[x] = SM3[...]
    for r in range(1, 4):
        go(rc(SM3, SMX.at[x], sx_s.at[r], sx_r.at[r], xd(r)))
    grad_own(0)
    for r in range(1, 4):
        arrived(SMX.at[lax.rem(x + 4 - r, 4)], sx_r.at[r])
    total = (SMX[0] + SMX[1]) + (SMX[2] + SMX[3])
    first = zl == 0
    smout[...] = total
    smout[6:7, 0:256] = jnp.where(first, total[6:7, 0:256], total[6:7, 256:512])
    smout[7:8, 0:192] = jnp.where(first, total[7:8, 0:192], total[7:8, 192:384])
    spread_wait(LO, lout, lo_s, lo_r)
    spread_wait(IG, igout, ig_s, ig_r)
    grad_done(1)
    grad_done(0)

    x_copy.wait_send()
    c_copy.wait_send()
    for k in range(3):
        sv_copy(k).wait_send()
        for i in range(2):
            wz_copy(i, k).wait_send()
            wq_copy(i, k).wait_send()
    for l in range(2):
        for b in range(2):
            @pl.when((2 * l + b) != z)
            def _(l=l, b=b):
                for i in range(2):
                    for r in range(1, 4):
                        wx_copy(l, b, i, r).wait_send()
    for p in range(2):
        for l in range(2):
            for b in range(2):
                for r in range(1, 4):
                    x_copy_of(l, p, b, r).wait_send()

                @pl.when((2 * l + b) != z)
                def _(l=l, b=b, p=p):
                    z_copy_of(l, p, b).wait_send()
        for r in range(1, 4):
            g_copy_of(p, r).wait_send()
    for cp in done + [norm_pair] + norm_ring:
        cp.wait_send()


def run_kernel(*operands):
    vm = pltpu.VMEM
    dma = pltpu.SemaphoreType.DMA
    scratch = [
        vm((512, 128), F32),
        vm((8, 1024), F32),
        vm((2, 2, 768, 1024), BF16),
        vm((4, 8, 1024), F32),
        vm((2, 512, 1024), BF16),
        vm((2, 512, 1024), BF16),
        vm((2, 512, 1024), BF16),
        vm((2, 512, 1024), BF16),
        vm((2, 32, 1024), BF16),
        vm((2, 512, 384), BF16),
        vm((2, 384, 512), BF16),
        vm((2, 2, 4, 512, 128), F32),
        vm((2, 128, 512), BF16),
        vm((2, 512, 512), BF16),
        vm((2, 4, 128, 512), F32),
        vm((4, 128, 512), F32),
        vm((4, 128, 512), BF16),
        vm((512, 512), BF16),
        vm((384, 512), BF16),
        vm((2, 64, 512), F32),
        vm((2, 64, 512), F32),
        vm((2, 64, 1024), F32),
        vm((2, 64, 1024), F32),
        vm((2, 64, 128), F32),
        vm((2, 64, 128), F32),
        vm((64, 1024), F32),
        vm((64, 1024), F32),
        vm((64, 1024), F32),
        vm((64, 1024), F32),
        vm((4, 128, 1024), BF16),
        vm((4, 64, 1024), BF16),
        vm((4, 64, 1024), BF16),
        vm((4, 64, 1024), BF16),
        vm((2, 2, 768, 1024), BF16),
        vm((2, 2, 3, 64, 1024), BF16),
        vm((2, 2, 3, 128, 1024), BF16),
        vm((2, 2, 64, 1024), BF16),
        vm((2, 2, 128, 1024), BF16),
        vm((3, 64, 1024), BF16),
        vm((3, 128, 1024), BF16),
        vm((2, 2, 32, 1024), BF16),
        vm((2, 2, 32, 1024), BF16),
        vm((2, 8, 1024), F32),
        vm((2, 8, 1024), F32),
        vm((2, 8, 1024), F32),
        vm((2, 8, 1024), F32),
        vm((4, 2, 8, 1024), F32),
        vm((2, 8, 1024), F32),
        vm((4, 8, 1024), F32),
        vm((8, 1024), F32),
        vm((4, 8, 1024), F32),
        dma((2, 4, 8)),
        dma((2, 4, 8)),
        dma((2, 4, 4)),
        dma((2, 4, 4)),
        dma((2, 4, 4)),
        dma((2, 4, 4)),
        dma((2,)),
        dma((2,)),
        dma((3,)),
        dma((3,)),
        dma((2, 2)),
        dma((3, 2)),
        dma((2, 2, 2)),
        dma((3, 2)),
        dma((2, 2, 2)),
        dma((2, 2, 2, 3)),
        dma((2, 2, 2, 3)),
        dma((2, 2, 2, 3)),
        dma((2, 2, 2, 3)),
        dma((2, 2, 2)),
        dma((2, 3)),
        dma((2, 3)),
        dma((2, 3)),
        dma((2, 2)),
        dma((4,)),
        dma((2, 2)),
        dma((4,)),
        dma(()),
        dma(()),
        dma((4,)),
        dma((4,)),
        dma((3,)),
        dma((3,)),
        dma((4,)),
        dma((4,)),
    ]
    in_vmem = pl.BlockSpec(memory_space=pltpu.VMEM)
    hbm = pl.BlockSpec(memory_space=pl.ANY)
    return pl.pallas_call(
        kernel,
        out_shape=(
            jax.ShapeDtypeStruct((4, 32, 1024), BF16),
            jax.ShapeDtypeStruct((4, 32, 1024), BF16),
            jax.ShapeDtypeStruct((768, 1024), BF16),
            jax.ShapeDtypeStruct((8, 1024), F32),
        ),
        in_specs=[in_vmem] * 2 + [hbm] * 2 + [in_vmem, hbm] + [in_vmem] * 5 + [pl.BlockSpec(memory_space=pltpu.SMEM)],
        out_specs=(in_vmem,) * 4,
        scratch_shapes=scratch,
        compiler_params=pltpu.CompilerParams(
            collective_id=0, has_side_effects=True, vmem_limit_bytes=60 * 1024 * 1024
        ),
        cost_estimate=pl.CostEstimate(flops=10_000_000_000, bytes_accessed=10_000_000, transcendentals=3_000_000),
    )(*operands)


def place_kernel(
    lout_in, igout_in, gout_in, sm_in,
    out, grad_in, qkv, qv, w_out, up, up_bias, down, gains, shifts, bias,
    lout, igout, gout, sm, sems,
):
    pairs = ((gout_in, gout), (igout_in, igout), (lout_in, lout), (sm_in, sm))
    loads = [pltpu.make_async_copy(src, dst, sems.at[i]) for i, (src, dst) in enumerate(pairs)]
    for load in loads:
        load.start()
    for load in loads:
        load.wait()
    for m in range(2):
        for q in range(2):
            grad_in[0, m, :, q, :] = igout[2 * m + q].astype(F32)
    out[0] = jnp.transpose(lout[...].reshape(2, 2, 32, 1024), (0, 2, 1, 3))
    qkv[...] = gout[0:192, :].astype(F32)
    w_out[0] = gout[192:256, :].astype(F32)
    up[0] = gout[256:512, :].astype(F32).T
    down[0] = gout[512:768, :].astype(F32)
    gains[0] = sm[0:2, :]
    shifts[0] = sm[2:4, :]
    bias[0] = sm[4:6, :]
    up_bias[...] = sm[6:7, 0:256]
    qv[0, 0:1, :] = sm[7:8, 0:64]
    qv[0, 1:2, :] = sm[7:8, 128:192]


def place_outputs(lout, igout, gout, sm):
    vmem = pl.BlockSpec(memory_space=pltpu.VMEM)

    def f32(*shape):
        return jax.ShapeDtypeStruct(shape, F32)

    return pl.pallas_call(
        place_kernel,
        out_shape=(
            jax.ShapeDtypeStruct((1, 2, 32, 2, 1024), BF16), f32(1, 2, 32, 2, 1024), f32(192, 1024), f32(1, 2, 64),
            f32(1, 64, 1024), f32(1, 1024, 256), f32(1, 256), f32(1, 256, 1024),
            f32(1, 2, 1024), f32(1, 2, 1024), f32(1, 2, 1024),
        ),
        in_specs=[pl.BlockSpec(memory_space=pl.ANY)] * 4,
        out_specs=(vmem,) * 11,
        scratch_shapes=[
            pltpu.VMEM((4, 32, 1024), BF16),
            pltpu.VMEM((4, 32, 1024), BF16),
            pltpu.VMEM((768, 1024), BF16),
            pltpu.VMEM((8, 1024), F32),
            pltpu.SemaphoreType.DMA((4,)),
        ],
        compiler_params=pltpu.CompilerParams(vmem_limit_bytes=60 * 1024 * 1024),
        cost_estimate=pl.CostEstimate(flops=1_000_000, bytes_accessed=6_000_000, transcendentals=0),
    )(lout, igout, gout, sm)


def per_device(
    inputs, lengths, cotangent, w_qkv, b_qv, w_out, w_up, b_up, w_down, norm_gains, norm_shifts, out_bias
):
    zh = lax.axis_index("section")
    zl = lax.axis_index("tensor") // 8
    xs = jnp.transpose(lax.dynamic_index_in_dim(inputs, zh, 0, keepdims=False), (1, 0, 2))
    cs = jnp.transpose(lax.dynamic_index_in_dim(cotangent, zh, 0, keepdims=False), (1, 0, 2))
    qkv_rows = jnp.transpose(w_qkv[0], (1, 2, 0)).reshape(192, 1024)
    out, grad_in, qkv, qv, g_out, up, up_bias, down, gains, shifts, bias = place_outputs(
        *run_kernel(
            xs, cs, qkv_rows, w_out[0], w_up[0], w_down[0],
            norm_gains[0], norm_shifts[0], out_bias[0], b_up, b_qv[0], lengths,
        )
    )
    grad_qkv = jnp.transpose(qkv.reshape(3, 64, 1024), (2, 0, 1))[None]
    return (out, grad_in, grad_qkv, qv, g_out, up, up_bias, down, gains, shifts, bias)


def solution(mesh):
    in_specs = (
        P(None, "tensor", "dp", None),
        P(None, "dp"),
        P(None, "tensor", "dp", None),
        P("section", None, None, "tensor"),
        P("section", None, "tensor"),
        P("section", "tensor", None),
        P("section", None, "tensor"),
        P("section", "tensor"),
        P("section", "tensor", None),
        P("section", None, None),
        P("section", None, None),
        P("section", None, None),
    )
    out_specs = (
        P("section", None, "tensor", "dp", None),
        P("section", None, "tensor", "dp", None),
        P("section", None, None, "tensor"),
        P("section", None, "tensor"),
        P("section", "tensor", None),
        P("section", None, "tensor"),
        P("section", "tensor"),
        P("section", "tensor", None),
        P("section", None, None),
        P("section", None, None),
        P("section", None, None),
    )
    return jax.shard_map(per_device, mesh=mesh, in_specs=in_specs, out_specs=out_specs, check_vma=False)
```

```python
import jax
import jax.numpy as jnp
from jax import lax
from jax.experimental import pallas as pl
from jax.experimental.pallas import tpu as pltpu
from jax.sharding import PartitionSpec as P

EPSILON = 1e-12
MASKED = -1e30
F32 = jnp.float32
BF16 = jnp.bfloat16
MESH = pl.DeviceIdType.MESH
INV_SQRT2 = 0.7071067811865476
INV_SQRT_2PI = 0.3989422804014327
SCALE = 0.125

PIECES = ((0, 256), (256, 512))
ALONG_Z = ((0, 128), (256, 192))
QUARTERED = ((128, 128), (448, 320))


def nt(a, b):
    return lax.dot_general(a, b, (((1,), (1,)), ((), ())), preferred_element_type=F32)


def nn(a, b):
    return lax.dot_general(a, b, (((1,), (0,)), ((), ())), preferred_element_type=F32)


def standardize(rows):
    center = jnp.mean(rows, axis=-1, keepdims=True)
    centred = rows - center
    spread = jnp.mean(centred * centred, axis=-1, keepdims=True)
    inv = lax.rsqrt(spread + EPSILON)
    return centred * inv, inv


def standardize_back(grad_out, gain, unit, inv):
    scaled = grad_out * gain
    return inv * (
        scaled
        - jnp.mean(scaled, axis=-1, keepdims=True)
        - unit * jnp.mean(scaled * unit, axis=-1, keepdims=True)
    )


def kernel(
    xs, cs, qkv_in, out_in, up_in, down_in, gains_in, shifts_in, bias_in, b_up_in, b_qv_in, len_in,
    lout, igout, gout, smout,
    valid, sv,
    W, SW, XF, YF, GF, GO, CT, PB, PT, PR, AT, HT, GD, CDF, HB, GZT, GPT, GKT, GVT,
    N1, N2, S1, S2, Y1, GR, GY, OWN,
    PART, SIB, SUM, RIN, G, GXA, GXF, QXA, QXF, ZXA, ZXF,
    LO, IG, SM, SMN, SMC, SM1, SMY, SM2, SMZ, SM3, SMX,
    ag_s, ag_r, sb_s, sb_r, rs_s, rs_r, in_s, in_r, loc, sv_s, sv_r, wz_s, wz_r, wq_s, wq_r, wx_s, wx_r,
    xr_s, xr_r, xf_s, xf_r, xa_s, xa_r, gz_s, gz_r, xg_s, xg_r, lo_s, lo_r, ig_s, ig_r,
    sc_s, sc_r, sy_s, sy_r, sz_s, sz_r, sx_s, sx_r,
):
    zh = lax.axis_index("section")
    x = lax.axis_index("dp")
    t = lax.axis_index("tensor")
    zl = t // 8
    y = (t % 8) // 2
    c = t % 2
    d = t % 8
    z = 2 * zh + zl

    def dev(zh_=None, x_=None, zl_=None, y_=None, c_=None):
        zh_ = zh if zh_ is None else zh_
        x_ = x if x_ is None else x_
        zl_ = zl if zl_ is None else zl_
        y_ = y if y_ is None else y_
        c_ = c if c_ is None else c_
        return (zh_, x_, zl_ * 8 + y_ * 2 + c_)

    def yd(r):
        return dev(y_=lax.rem(y + r, 4))

    def xd(r):
        return dev(x_=lax.rem(x + r, 4))

    sibling = dev(c_=1 - c)
    partner = dev(zl_=1 - zl)
    cross = dev(zh_=1 - zh, zl_=1 - zl)
    far = dev(zh_=1 - zh)

    def rc(src, dst, ssem, rsem, where):
        return pltpu.make_async_remote_copy(
            src_ref=src, dst_ref=dst, send_sem=ssem, recv_sem=rsem, device_id=where, device_id_type=MESH
        )

    def arrived(dst, rsem):
        rc(dst, dst, rsem, rsem, sibling).wait_recv()

    barrier = pltpu.get_barrier_semaphore()
    greeted = [sibling, yd(1), yd(2), yd(3), xd(1), xd(2), xd(3), partner, cross, far]
    for other in greeted:
        pl.semaphore_signal(barrier, inc=1, device_id=other, device_id_type=MESH)
    pl.semaphore_wait(barrier, len(greeted))

    def slot(full, l, yy, cc):
        return full.at[l, pl.ds(pl.multiple_of(yy * 128 + cc * 64, 64), 64)]

    def ag_begin(full, l, k):
        mine = slot(full, l, y, c)
        copies = [rc(mine, mine, ag_s.at[l, k, i], ag_r.at[l, k, i], yd(i)) for i in (1, 3, 2)]
        copies.append(rc(mine, mine, ag_s.at[l, k, 4], ag_r.at[l, k, 4], sibling))
        for cp in copies:
            cp.start()
        return copies

    def from_ring(full, l, k, i, copies):
        got = slot(full, l, lax.rem(y + 4 - i, 4), c)
        arrived(got, ag_r.at[l, k, i])
        cp = rc(got, got, ag_s.at[l, k, 4 + i], ag_r.at[l, k, 4 + i], sibling)
        cp.start()
        copies.append(cp)

    def from_sibling(full, l, k, i):
        arrived(slot(full, l, lax.rem(y + 4 - i, 4), 1 - c), ag_r.at[l, k, 4 + i])

    def gather(full, l, k, use):
        copies = ag_begin(full, l, k)
        from_sibling(full, l, k, 0)
        use(y)
        from_ring(full, l, k, 1, copies)
        from_ring(full, l, k, 3, copies)
        from_sibling(full, l, k, 1)
        use(lax.rem(y + 3, 4))
        from_ring(full, l, k, 2, copies)
        from_sibling(full, l, k, 3)
        use(lax.rem(y + 1, 4))
        from_sibling(full, l, k, 2)
        use(lax.rem(y + 2, 4))
        return copies

    def make(l, k, r, chunk, copies):
        PART[r] = chunk(lax.rem(y + r, 4)).astype(BF16)
        theirs = PART.at[r, pl.ds(pl.multiple_of((1 - c) * 64, 64), 64)]
        cp = rc(theirs, SIB.at[r], sb_s.at[l, k, r], sb_r.at[l, k, r], sibling)
        cp.start()
        copies.append(cp)

    def both(l, k, r):
        arrived(SIB.at[r], sb_r.at[l, k, r])
        mine = PART[r, pl.ds(pl.multiple_of(c * 64, 64), 64), :]
        return mine.astype(F32) + SIB[r].astype(F32)

    def push(l, k, r, pushes):
        SUM[r] = both(l, k, r).astype(BF16)
        cp = rc(SUM.at[r], RIN.at[r], rs_s.at[l, k, r], rs_r.at[l, k, r], yd(r))
        cp.start()
        pushes.append(cp)

    def finish(l, k, copies, pushes):
        for cp in copies:
            cp.wait_send()
        for r in (1, 3, 2):
            arrived(RIN.at[r], rs_r.at[l, k, r])
        total = OWN[...] + ((RIN[1].astype(F32) + RIN[3].astype(F32)) + RIN[2].astype(F32))
        for cp in pushes:
            cp.wait_send()
        return total

    def scatter(l, k, chunk, window, copies, midway=lambda: None):
        pushes = []
        make(l, k, 2, chunk, copies)
        make(l, k, 1, chunk, copies)
        push(l, k, 2, pushes)
        make(l, k, 3, chunk, copies)
        push(l, k, 1, pushes)
        midway()
        make(l, k, 0, chunk, copies)
        push(l, k, 3, pushes)
        OWN[...] = both(l, k, 0)
        window()
        return finish(l, k, copies, pushes)

    def gather_scatter(full, l, k, chunk, window):
        mine = slot(full, l, y, c)
        pushes = []

        def to_ring(i):
            return rc(mine, mine, ag_s.at[l, k, i], ag_r.at[l, k, i], yd(i))

        copies = [rc(mine, mine, ag_s.at[l, k, 4], ag_r.at[l, k, 4], sibling), to_ring(1), to_ring(3)]
        for cp in copies:
            cp.start()
        from_sibling(full, l, k, 0)
        make(l, k, 0, chunk, copies)
        cp = to_ring(2)
        cp.start()
        copies.append(cp)
        from_ring(full, l, k, 1, copies)
        from_ring(full, l, k, 3, copies)
        from_sibling(full, l, k, 1)
        make(l, k, 3, chunk, copies)
        from_sibling(full, l, k, 3)
        make(l, k, 1, chunk, copies)
        push(l, k, 3, pushes)
        push(l, k, 1, pushes)
        from_ring(full, l, k, 2, copies)
        from_sibling(full, l, k, 2)
        make(l, k, 2, chunk, copies)
        push(l, k, 2, pushes)
        OWN[...] = both(l, k, 0)
        window()
        return finish(l, k, copies, pushes)

    others = (far, cross, partner)

    def sv_copy(k):
        return rc(sv, SW.at[z], sv_s.at[k], sv_r.at[zh, zl], others[k])

    def wz_copy(i, k):
        rows = W.at[zh, zl, pl.ds(*ALONG_Z[i])]
        return rc(rows, rows, wz_s.at[k, i], wz_r.at[zh, zl, i], others[k])

    def quarter(l, b, i, who):
        base, size = QUARTERED[i]
        n = size // 4
        return W.at[l, b, pl.ds(pl.multiple_of(base + who * n, 16), n)]

    def wq_copy(i, k):
        rows = quarter(zh, zl, i, x)
        return rc(rows, rows, wq_s.at[k, i], wq_r.at[zh, zl, i], others[k])

    def wx_copy(l, b, i, r):
        rows = quarter(l, b, i, x)
        return rc(rows, rows, wx_s.at[l, b, i, r - 1], wx_r.at[l, b, i, r - 1], xd(r))

    def send_quarter(i):
        for k in range(3):
            wq_copy(i, k).start()

    def send_rest(i):
        for k in range(3):
            wz_copy(i, k).start()

    def send_vectors():
        for k in range(3):
            sv_copy(k).start()

    def pass_on(l, i):
        for b in range(2):
            @pl.when((2 * l + b) != z)
            def _(b=b):
                arrived(quarter(l, b, i, x), wq_r.at[l, b, i])
                for r in (2, 1, 3):
                    wx_copy(l, b, i, r).start()

    def vectors_here(l):
        for b in range(2):
            @pl.when((2 * l + b) != z)
            def _(b=b):
                arrived(SW.at[2 * l + b], sv_r.at[l, b])

    def weights_here(l, i):
        for b in range(2):
            @pl.when((2 * l + b) != z)
            def _(b=b):
                arrived(W.at[l, b, pl.ds(*ALONG_Z[i])], wz_r.at[l, b, i])
                for r in (1, 3, 2):
                    arrived(quarter(l, b, i, lax.rem(x + 4 - r, 4)), wx_r.at[l, b, i, r - 1])

    mine_rows = pl.ds(pl.multiple_of(d * 64 + zl * 32, 32), 32)
    x_copy = rc(xs.at[1 - zl], XF.at[0, mine_rows], in_s.at[0], in_r.at[0], partner)
    x_copy.start()
    c_copy = rc(cs.at[1 - zl], CT.at[zl], in_s.at[1], in_r.at[1], partner)

    own_block = W.at[zh, zl]
    loads = [
        pltpu.make_async_copy(src, own_block.at[pl.ds(base, size)], loc.at[i])
        for i, (src, base, size) in enumerate(((qkv_in, 0, 192), (out_in, 192, 64), (down_in, 512, 256)))
    ]
    for load in loads:
        load.start()
    c_copy.start()
    XF[0, mine_rows, :] = xs[zl]
    CT[zl] = cs[zl]
    first = zl == 0
    sv[0:2, :] = gains_in[...]
    sv[2:4, :] = shifts_in[...]
    sv[4:6, :] = bias_in[...]
    sv[6:8, :] = jnp.zeros((2, 1024), F32)
    sv[6:7, 0:256] = jnp.where(first, b_up_in[...], 0.0)
    sv[6:7, 256:512] = jnp.where(first, 0.0, b_up_in[...])
    for i, at in ((0, 0), (1, 128)):
        sv[7:8, at : at + 64] = jnp.where(first, b_qv_in[i : i + 1, :], 0.0)
        sv[7:8, at + 192 : at + 256] = jnp.where(first, 0.0, b_qv_in[i : i + 1, :])
    SW[z] = sv[...]
    loads[0].wait()
    loads[1].wait()

    @pl.when(zh == 0)
    def _():
        send_vectors()
        send_quarter(0)
        send_rest(0)

    own_block[256:512, :] = up_in[...].T
    loads[2].wait()
    r_ = lax.broadcasted_iota(jnp.int32, (512, 128), 0)
    position = lax.rem(r_ // 32, 2) * 256 + (r_ // 64) * 32 + lax.rem(r_, 32)
    valid[...] = jnp.where(position < len_in[zh, zl], 1.0, 0.0)
    arrived(XF.at[0, pl.ds(pl.multiple_of(d * 64 + (1 - zl) * 32, 32), 32)], in_r.at[0])

    def spread_out(rows, buf, out, s_s, s_r, l):
        buf[l] = rows.reshape(2, 32, 1024)
        for b in range(2):
            @pl.when((2 * l + b) == z)
            def _(b=b):
                out[z] = buf[l, b]

            @pl.when((2 * l + b) != z)
            def _(b=b):
                rc(buf.at[l, b], out.at[z], s_s.at[l, b], s_r.at[z], dev(zh_=l, zl_=b)).start()

    def spread_wait(buf, out, s_s, s_r):
        for k in range(1, 4):
            zz = lax.rem(z + k, 4)
            arrived(out.at[zz], s_r.at[zz])
        for l in range(2):
            for b in range(2):
                @pl.when((2 * l + b) != z)
                def _(l=l, b=b):
                    rc(buf.at[l, b], buf.at[l, b], s_s.at[l, b], s_r.at[z], sibling).wait_send()

    def row_of(l, i):
        return SW[2 * l, pl.ds(i, 1), :]

    own_rows = pl.ds(pl.multiple_of(d * 64, 64), 64)

    def out_weights(l):
        return jnp.concatenate([W[l, 0, 192:256, :], W[l, 1, 192:256, :]], axis=0)

    def qkv_weights(l):
        return jnp.concatenate([W[l, 0, 0:192, :], W[l, 1, 0:192, :]], axis=0)

    def lanes(yy):
        return pl.ds(pl.multiple_of(yy * 128, 128), 128)

    def forward_layer(l, carry):
        seen = []

        def between(yy):
            seen.append(yy)
            if len(seen) == 2:
                @pl.when((l == 0) & (zh == 0))
                def _():
                    send_quarter(1)

                @pl.when(l == 0)
                def _():
                    pass_on(0, 0)

        x_copies = gather(XF, l, 0, between)

        @pl.when((l == 0) & (zh == 0))
        def _():
            send_rest(1)

        vectors_here(l)
        weights_here(l, 0)
        qv_bias = SW[2 * l, 7:8, 0:384] + SW[2 * l + 1, 7:8, 0:384]
        proj = (nt(XF[l], qkv_weights(l)) + qv_bias).astype(BF16)
        PB[l] = proj
        PT[l] = proj.T


        def attend(yy):
            cols = lanes(yy)
            for h in range(2):
                base = h * 192
                scores = nn(PB[l, :, base + 64 : base + 128], PT[l, base : base + 64, cols]) * SCALE
                scores = jnp.where(valid[...] > 0.5, scores, MASKED)
                terms = jnp.exp(scores - jnp.max(scores, axis=0, keepdims=True))
                probs = terms * (1.0 / jnp.sum(terms, axis=0, keepdims=True))
                PR[l, h, yy] = probs
                mixed = nn(PT[l, base + 128 : base + 192, :], probs.astype(BF16))
                AT[l, h * 64 : h * 64 + 64, cols] = mixed.astype(BF16)
            return nn(AT[l, :, cols].T, out_weights(l))

        def attend_midway():
            @pl.when(l == 0)
            def _():
                pass_on(0, 1)

        def attend_window():
            @pl.when((l == 0) & (zh == 1))
            def _():
                send_vectors()
                send_quarter(0)
                send_rest(0)
                send_quarter(1)

        attended = scatter(l, 0, attend, attend_window, x_copies, attend_midway)
        unit, inv = standardize(XF[l, own_rows, :].astype(F32) + attended + row_of(l, 4))
        N1[l] = unit
        S1[l] = jnp.broadcast_to(inv, (64, 128))
        middle = unit * row_of(l, 0) + row_of(l, 2)
        Y1[...] = middle
        YF[l, own_rows, :] = middle.astype(BF16)
        weights_here(l, 1)

        up_bias = SW[2 * l, 6:7, 0:512] + SW[2 * l + 1, 6:7, 0:512]

        def feed(yy):
            rows = YF[l, lanes(yy), :]
            total = None
            for b in range(2):
                pre = nt(rows, W[l, b, 256:512, :]) + up_bias[:, b * 256 : b * 256 + 256]
                cdf = 0.5 * (1.0 + lax.erf(pre * INV_SQRT2))
                hidden = (pre * cdf).astype(BF16)
                cols = pl.ds(b * 256, 256)
                GD[l, yy, :, cols] = pre
                CDF[yy, :, cols] = cdf
                HB[yy, :, cols] = hidden
                piece = nn(hidden, W[l, b, 512:768, :])
                total = piece if total is None else total + piece
            return total

        def feed_window():
            @pl.loop(0, 4)
            def _(yy):
                HT[l, :, lanes(yy)] = HB[yy].T
                pre = GD[l, yy]
                GD[l, yy] = CDF[yy] + pre * (INV_SQRT_2PI * jnp.exp(-0.5 * pre * pre))

            @pl.when(l == 0)
            def _():
                pass_on(1, 0)
                pass_on(1, 1)

            @pl.when((l == 0) & (zh == 1))
            def _():
                send_rest(1)

        fed = gather_scatter(YF, l, 1, feed, feed_window)
        unit, inv = standardize(Y1[...] + fed + row_of(l, 5))
        N2[l] = unit
        S2[l] = jnp.broadcast_to(inv, (64, 128))
        result = (unit * row_of(l, 1) + row_of(l, 3)).astype(BF16)

        @pl.when(l == 0)
        def _():
            XF[1, own_rows, :] = result

        spread_out(result, LO, lout, lo_s, lo_r, l)
        return carry

    lax.fori_loop(0, 2, forward_layer, 0)

    arrived(CT.at[1 - zl], in_r.at[1])
    GY[...] = CT[...].reshape(64, 1024).astype(F32)
    SM[...] = jnp.zeros_like(SM)
    SMN[...] = jnp.zeros_like(SMN)
    norm_pair = rc(SMN, SMC, sc_s, sc_r, sibling)
    norm_ring = [rc(SM1, SMY.at[y], sy_s.at[r], sy_r.at[r], yd(r)) for r in range(1, 4)]

    QX, ZX = (QXA, QXF), (ZXA, ZXF)

    def own_part(p, ref, who, *lead):
        base, size = PIECES[p]
        n = size // 4
        return ref.at[(*lead, pl.ds(pl.multiple_of(base + who * n, n), n))]

    def x_copy_of(l, b, r):
        src = own_part(0, G, lax.rem(x + r, 4), l, b)
        return rc(src, GXA.at[l, b, r - 1], xr_s.at[l, b, r - 1], xr_r.at[l, b, r - 1], xd(r))

    def half_of(ref, r, half, *lead):
        start = 256 + lax.rem(x + r, 4) * 128 + half * 64
        return ref.at[(*lead, pl.ds(pl.multiple_of(start, 64), 64))]

    RING = ((2, 0, 1), (2, 1, 3), (1, 1, 1), (3, 0, 3), (1, 0, 1), (3, 1, 3))

    def ring_copy(l, b, i):
        r, half, to = RING[i]
        return rc(half_of(G, r, half, l, b), GXF.at[l, b, i], xf_s.at[l, b, i], xf_r.at[l, b, i], xd(to))

    def ring_first(l):
        for i in range(4):
            for b in range(2):
                ring_copy(l, b, i).start()

    def ring_second(l):
        for i in range(2):
            for b in range(2):
                arrived(GXF.at[l, b, i], xf_r.at[l, b, i])
                r, half, _ = RING[4 + i]
                mine = half_of(G, r, half, l, b)
                mine[...] = (mine[...].astype(F32) + GXF[l, b, i].astype(F32)).astype(BF16)
                ring_copy(l, b, 4 + i).start()

    def z_copy_of(l, p, b):
        k = lax.rem(2 * l + b + 4 - z, 4) - 1
        return rc(QX[p].at[l, b], ZX[p].at[k], gz_s.at[l, p, b], gz_r.at[p, k], dev(zh_=l, zl_=b))

    def g_copy_of(r):
        mine = own_part(0, gout, x)
        return rc(mine, mine, xg_s.at[r - 1], xg_r.at[r - 1], xd(r))

    AROUND = ((0, 0, 1), (0, 1, 3), (0, 1, 1), (0, 0, 3), (3, 0, 1), (1, 1, 3))

    def around(i):
        r, half, to = AROUND[i]
        rows = half_of(gout, r, half)
        return rc(rows, rows, xa_s.at[i], xa_r.at[i], xd(to))

    def around_here(i):
        r, half, to = AROUND[i]
        arrived(half_of(gout, r + 4 - to, half), xa_r.at[i])

    def grad_x(l):
        for b in range(2):
            for r in (2, 1, 3):
                x_copy_of(l, b, r).start()

    def grad_z(l, p):
        for b in range(2):
            mine = own_part(p, G, x, l, b)
            if p == 0:
                for r in (1, 3, 2):
                    arrived(GXA.at[l, b, r - 1], xr_r.at[l, b, r - 1])
                got = ((0, 64, tuple(GXA.at[l, b, i] for i in range(3))),)
            else:
                for i in (2, 3, 4, 5):
                    arrived(GXF.at[l, b, i], xf_r.at[l, b, i])
                got = (
                    (0, 64, (GXF.at[l, b, 3], GXF.at[l, b, 4])),
                    (64, 64, (GXF.at[l, b, 2], GXF.at[l, b, 5])),
                )
            for base, size, terms in got:
                total = mine[base : base + size, :].astype(F32)
                for term in terms:
                    total = total + term[...].astype(F32)
                QX[p][l, b, base : base + size, :] = total.astype(BF16)

            @pl.when((2 * l + b) != z)
            def _(b=b):
                z_copy_of(l, p, b).start()

    def grad_own(p):
        n = PIECES[p][1] // 4
        for k in range(3):
            arrived(ZX[p].at[k], gz_r.at[p, k])
        mine = own_part(p, gout, x)

        @pl.loop(0, n // 32)
        def _(i):
            rows = pl.ds(pl.multiple_of(i * 32, 32), 32)
            mine[rows, :] = (
                (QX[p][zh, zl, rows, :].astype(F32) + ZX[p][0, rows, :].astype(F32))
                + (ZX[p][1, rows, :].astype(F32) + ZX[p][2, rows, :].astype(F32))
            ).astype(BF16)

        if p == 0:
            for r in (2, 1, 3):
                g_copy_of(r).start()
        else:
            for i in range(4):
                around(i).start()

    def grad_done():
        for i in (0, 1):
            around_here(i)
            around(4 + i).start()
        for i in (2, 3, 4, 5):
            around_here(i)
        for r in (1, 3, 2):
            arrived(own_part(0, gout, lax.rem(x + 4 - r, 4)), xg_r.at[r - 1])

    def backward_layer(step, carry):
        l = 1 - step
        grad = GY[...]
        unit = N2[l]
        grad_second = standardize_back(grad, row_of(l, 1), unit, S2[l, :, 0:1])
        SMN[l, 1:2, :] = jnp.sum(grad * unit, axis=0, keepdims=True)
        SMN[l, 3:4, :] = jnp.sum(grad, axis=0, keepdims=True)
        SMN[l, 5:6, :] = jnp.sum(grad_second, axis=0, keepdims=True)
        GR[...] = grad_second
        GF[l, own_rows, :] = grad_second.astype(BF16)
        def feed_back(yy):
            rows = GF[l, lanes(yy), :]
            total = None
            for b in range(2):
                grad_pre = (nt(rows, W[l, b, 512:768, :]) * GD[l, yy, :, b * 256 : b * 256 + 256]).astype(BF16)
                HB[yy, :, pl.ds(b * 256, 256)] = grad_pre
                piece = nn(grad_pre, W[l, b, 256:512, :])
                total = piece if total is None else total + piece
            return total

        def feed_grads():
            @pl.loop(0, 4)
            def _(yy):
                grad_pre = HB[yy]
                GZT[:, lanes(yy)] = grad_pre.T
                SM[l, 6:7, 0:512] += jnp.sum(grad_pre.astype(F32), axis=0, keepdims=True)

            @pl.loop(0, 2)
            def _(b):
                rows = pl.ds(pl.multiple_of(b * 256, 256), 256)
                G[l, b, 256:512, :] = nn(GZT[rows, :], YF[l]).astype(BF16)
                G[l, b, 512:768, :] = nn(HT[l, rows, :], GF[l]).astype(BF16)

            ring_first(l)

            @pl.when(l == 0)
            def _():
                grad_z(1, 1)
                grad_z(1, 0)

        grad_middle = GR[...] + gather_scatter(GF, l, 2, feed_back, feed_grads)
        unit = N1[l]
        grad_first = standardize_back(grad_middle, row_of(l, 0), unit, S1[l, :, 0:1])
        SMN[l, 0:1, :] = jnp.sum(grad_middle * unit, axis=0, keepdims=True)
        SMN[l, 2:3, :] = jnp.sum(grad_middle, axis=0, keepdims=True)
        SMN[l, 4:5, :] = jnp.sum(grad_first, axis=0, keepdims=True)
        GR[...] = grad_first
        GO[l, own_rows, :] = grad_first.astype(BF16)
        GKT[...] = jnp.zeros_like(GKT)
        GVT[...] = jnp.zeros_like(GVT)

        def attend_back(yy):
            cols = lanes(yy)
            grad_mixed = nt(GO[l, cols, :], out_weights(l)).astype(BF16)
            mixed_t = grad_mixed.T
            for h in range(2):
                base = h * 192
                half = mixed_t[h * 64 : h * 64 + 64, :]
                probs = PR[l, h, yy]
                grad_prob = nn(PB[l, :, base + 128 : base + 192], half)
                inner = jnp.sum(probs * grad_prob, axis=0, keepdims=True)
                grad_score = (probs * (grad_prob - inner)).astype(BF16)
                GPT[base : base + 64, cols] = (
                    nn(PT[l, base + 64 : base + 128, :], grad_score) * SCALE
                ).astype(BF16)
                GKT[h] += nt(PT[l, base : base + 64, cols], grad_score)
                GVT[h] += nt(half, probs.astype(BF16))

        @pl.when(l == 0)
        def _():
            norm_pair.start()

        o_copies = gather(GO, l, 3, attend_back)
        ring_second(l)

        @pl.when(l == 0)
        def _():
            arrived(SMC, sc_r)
            SM1[...] = SMN[...] + SMC[...]
            SMY[y] = SM1[...]
            for cp in norm_ring:
                cp.start()


        for h in range(2):
            base = h * 192
            GPT[base + 64 : base + 128, :] = (GKT[h] * SCALE).astype(BF16)
            GPT[base + 128 : base + 192, :] = GVT[h].astype(BF16)

        def attend_grads():
            @pl.loop(0, 2)
            def _(b):
                G[l, b, 0:192, :] = nn(GPT[pl.ds(pl.multiple_of(b * 192, 64), 192), :], XF[l]).astype(BF16)
                G[l, b, 192:256, :] = nn(AT[l, pl.ds(pl.multiple_of(b * 64, 64), 64), :], GO[l]).astype(BF16)

            grad_x(l)

        pl.when(l == 0)(attend_grads)

        def project_back(yy):
            grad_proj = GPT[:, lanes(yy)].T
            SM[l, 7:8, 0:384] += jnp.sum(grad_proj.astype(F32), axis=0, keepdims=True)
            return nn(grad_proj, qkv_weights(l))

        def project_window():
            pl.when(l == 1)(attend_grads)

            @pl.when(l == 0)
            def _():
                grad_z(0, 1)

        grad_input = (GR[...] + scatter(l, 3, project_back, project_window, o_copies)).astype(BF16)
        GY[...] = grad_input.astype(F32)
        spread_out(grad_input, IG, igout, ig_s, ig_r, l)
        return carry

    lax.fori_loop(0, 2, backward_layer, 0)

    done = []

    def go(cp):
        cp.start()
        done.append(cp)

    grad_z(0, 0)
    for r in range(1, 4):
        arrived(SMY.at[lax.rem(y + 4 - r, 4)], sy_r.at[r])
    SM2[...] = ((SMY[0] + SMY[1]) + (SMY[2] + SMY[3])) + SM[...]
    SMZ[z] = SM2[zh]
    for k, where, lz in ((0, partner, zh), (1, cross, 1 - zh), (2, far, 1 - zh)):
        go(rc(SM2.at[lz], SMZ.at[z], sz_s.at[k], sz_r.at[k], where))
    grad_own(1)
    for k, zz in ((0, 2 * zh + 1 - zl), (1, 2 * (1 - zh) + 1 - zl), (2, 2 * (1 - zh) + zl)):
        arrived(SMZ.at[zz], sz_r.at[k])
    SM3[...] = (SMZ[0] + SMZ[1]) + (SMZ[2] + SMZ[3])
    SMX[x] = SM3[...]
    for r in range(1, 4):
        go(rc(SM3, SMX.at[x], sx_s.at[r], sx_r.at[r], xd(r)))
    grad_own(0)
    for r in range(1, 4):
        arrived(SMX.at[lax.rem(x + 4 - r, 4)], sx_r.at[r])
    total = (SMX[0] + SMX[1]) + (SMX[2] + SMX[3])
    first = zl == 0
    smout[...] = total
    smout[6:7, 0:256] = jnp.where(first, total[6:7, 0:256], total[6:7, 256:512])
    smout[7:8, 0:192] = jnp.where(first, total[7:8, 0:192], total[7:8, 192:384])
    spread_wait(LO, lout, lo_s, lo_r)
    spread_wait(IG, igout, ig_s, ig_r)
    grad_done()

    x_copy.wait_send()
    c_copy.wait_send()
    for k in range(3):
        sv_copy(k).wait_send()
        for i in range(2):
            wz_copy(i, k).wait_send()
            wq_copy(i, k).wait_send()
    for l in range(2):
        for b in range(2):
            @pl.when((2 * l + b) != z)
            def _(l=l, b=b):
                for i in range(2):
                    for r in range(1, 4):
                        wx_copy(l, b, i, r).wait_send()
    for l in range(2):
        for b in range(2):
            for r in range(1, 4):
                x_copy_of(l, b, r).wait_send()
            for i in range(6):
                ring_copy(l, b, i).wait_send()

            @pl.when((2 * l + b) != z)
            def _(l=l, b=b):
                for p in range(2):
                    z_copy_of(l, p, b).wait_send()
    for r in range(1, 4):
        g_copy_of(r).wait_send()
    for i in range(6):
        around(i).wait_send()
    for cp in done + [norm_pair] + norm_ring:
        cp.wait_send()


def run_kernel(*operands):
    vm = pltpu.VMEM
    dma = pltpu.SemaphoreType.DMA
    scratch = [
        vm((512, 128), F32),
        vm((8, 1024), F32),
        vm((2, 2, 768, 1024), BF16),
        vm((4, 8, 1024), F32),
        vm((2, 512, 1024), BF16),
        vm((2, 512, 1024), BF16),
        vm((2, 512, 1024), BF16),
        vm((2, 512, 1024), BF16),
        vm((2, 32, 1024), BF16),
        vm((2, 512, 384), BF16),
        vm((2, 384, 512), BF16),
        vm((2, 2, 4, 512, 128), F32),
        vm((2, 128, 512), BF16),
        vm((2, 512, 512), BF16),
        vm((2, 4, 128, 512), F32),
        vm((4, 128, 512), F32),
        vm((4, 128, 512), BF16),
        vm((512, 512), BF16),
        vm((384, 512), BF16),
        vm((2, 64, 512), F32),
        vm((2, 64, 512), F32),
        vm((2, 64, 1024), F32),
        vm((2, 64, 1024), F32),
        vm((2, 64, 128), F32),
        vm((2, 64, 128), F32),
        vm((64, 1024), F32),
        vm((64, 1024), F32),
        vm((64, 1024), F32),
        vm((64, 1024), F32),
        vm((4, 128, 1024), BF16),
        vm((4, 64, 1024), BF16),
        vm((4, 64, 1024), BF16),
        vm((4, 64, 1024), BF16),
        vm((2, 2, 768, 1024), BF16),
        vm((2, 2, 3, 64, 1024), BF16),
        vm((2, 2, 6, 64, 1024), BF16),
        vm((2, 2, 64, 1024), BF16),
        vm((2, 2, 128, 1024), BF16),
        vm((3, 64, 1024), BF16),
        vm((3, 128, 1024), BF16),
        vm((2, 2, 32, 1024), BF16),
        vm((2, 2, 32, 1024), BF16),
        vm((2, 8, 1024), F32),
        vm((2, 8, 1024), F32),
        vm((2, 8, 1024), F32),
        vm((2, 8, 1024), F32),
        vm((4, 2, 8, 1024), F32),
        vm((2, 8, 1024), F32),
        vm((4, 8, 1024), F32),
        vm((8, 1024), F32),
        vm((4, 8, 1024), F32),
        dma((2, 4, 8)),
        dma((2, 4, 8)),
        dma((2, 4, 4)),
        dma((2, 4, 4)),
        dma((2, 4, 4)),
        dma((2, 4, 4)),
        dma((2,)),
        dma((2,)),
        dma((3,)),
        dma((3,)),
        dma((2, 2)),
        dma((3, 2)),
        dma((2, 2, 2)),
        dma((3, 2)),
        dma((2, 2, 2)),
        dma((2, 2, 2, 3)),
        dma((2, 2, 2, 3)),
        dma((2, 2, 3)),
        dma((2, 2, 3)),
        dma((2, 2, 6)),
        dma((2, 2, 6)),
        dma((6,)),
        dma((6,)),
        dma((2, 2, 2)),
        dma((2, 3)),
        dma((3,)),
        dma((3,)),
        dma((2, 2)),
        dma((4,)),
        dma((2, 2)),
        dma((4,)),
        dma(()),
        dma(()),
        dma((4,)),
        dma((4,)),
        dma((3,)),
        dma((3,)),
        dma((4,)),
        dma((4,)),
    ]
    in_vmem = pl.BlockSpec(memory_space=pltpu.VMEM)
    hbm = pl.BlockSpec(memory_space=pl.ANY)
    return pl.pallas_call(
        kernel,
        out_shape=(
            jax.ShapeDtypeStruct((4, 32, 1024), BF16),
            jax.ShapeDtypeStruct((4, 32, 1024), BF16),
            jax.ShapeDtypeStruct((768, 1024), BF16),
            jax.ShapeDtypeStruct((8, 1024), F32),
        ),
        in_specs=[in_vmem] * 2 + [hbm] * 2 + [in_vmem, hbm] + [in_vmem] * 5 + [pl.BlockSpec(memory_space=pltpu.SMEM)],
        out_specs=(in_vmem,) * 4,
        scratch_shapes=scratch,
        compiler_params=pltpu.CompilerParams(
            collective_id=0, has_side_effects=True, vmem_limit_bytes=60 * 1024 * 1024
        ),
        cost_estimate=pl.CostEstimate(flops=10_000_000_000, bytes_accessed=10_000_000, transcendentals=3_000_000),
    )(*operands)


def place_kernel(
    lout_in, igout_in, gout_in, sm_in,
    out, grad_in, qkv, qv, w_out, up, up_bias, down, gains, shifts, bias,
    lout, igout, gout, sm, sems,
):
    pairs = ((gout_in, gout), (igout_in, igout), (lout_in, lout), (sm_in, sm))
    loads = [pltpu.make_async_copy(src, dst, sems.at[i]) for i, (src, dst) in enumerate(pairs)]
    for load in loads:
        load.start()
    for load in loads:
        load.wait()
    for m in range(2):
        for q in range(2):
            grad_in[0, m, :, q, :] = igout[2 * m + q].astype(F32)
    out[0] = jnp.transpose(lout[...].reshape(2, 2, 32, 1024), (0, 2, 1, 3))
    qkv[...] = gout[0:192, :].astype(F32)
    w_out[0] = gout[192:256, :].astype(F32)
    up[0] = gout[256:512, :].astype(F32).T
    down[0] = gout[512:768, :].astype(F32)
    gains[0] = sm[0:2, :]
    shifts[0] = sm[2:4, :]
    bias[0] = sm[4:6, :]
    up_bias[...] = sm[6:7, 0:256]
    qv[0, 0:1, :] = sm[7:8, 0:64]
    qv[0, 1:2, :] = sm[7:8, 128:192]


def place_outputs(lout, igout, gout, sm):
    vmem = pl.BlockSpec(memory_space=pltpu.VMEM)

    def f32(*shape):
        return jax.ShapeDtypeStruct(shape, F32)

    return pl.pallas_call(
        place_kernel,
        out_shape=(
            jax.ShapeDtypeStruct((1, 2, 32, 2, 1024), BF16), f32(1, 2, 32, 2, 1024), f32(192, 1024), f32(1, 2, 64),
            f32(1, 64, 1024), f32(1, 1024, 256), f32(1, 256), f32(1, 256, 1024),
            f32(1, 2, 1024), f32(1, 2, 1024), f32(1, 2, 1024),
        ),
        in_specs=[pl.BlockSpec(memory_space=pl.ANY)] * 4,
        out_specs=(vmem,) * 11,
        scratch_shapes=[
            pltpu.VMEM((4, 32, 1024), BF16),
            pltpu.VMEM((4, 32, 1024), BF16),
            pltpu.VMEM((768, 1024), BF16),
            pltpu.VMEM((8, 1024), F32),
            pltpu.SemaphoreType.DMA((4,)),
        ],
        compiler_params=pltpu.CompilerParams(vmem_limit_bytes=60 * 1024 * 1024),
        cost_estimate=pl.CostEstimate(flops=1_000_000, bytes_accessed=6_000_000, transcendentals=0),
    )(lout, igout, gout, sm)


def per_device(
    inputs, lengths, cotangent, w_qkv, b_qv, w_out, w_up, b_up, w_down, norm_gains, norm_shifts, out_bias
):
    zh = lax.axis_index("section")
    zl = lax.axis_index("tensor") // 8
    xs = jnp.transpose(lax.dynamic_index_in_dim(inputs, zh, 0, keepdims=False), (1, 0, 2))
    cs = jnp.transpose(lax.dynamic_index_in_dim(cotangent, zh, 0, keepdims=False), (1, 0, 2))
    qkv_rows = jnp.transpose(w_qkv[0], (1, 2, 0)).reshape(192, 1024)
    out, grad_in, qkv, qv, g_out, up, up_bias, down, gains, shifts, bias = place_outputs(
        *run_kernel(
            xs, cs, qkv_rows, w_out[0], w_up[0], w_down[0],
            norm_gains[0], norm_shifts[0], out_bias[0], b_up, b_qv[0], lengths,
        )
    )
    grad_qkv = jnp.transpose(qkv.reshape(3, 64, 1024), (2, 0, 1))[None]
    return (out, grad_in, grad_qkv, qv, g_out, up, up_bias, down, gains, shifts, bias)


def solution(mesh):
    in_specs = (
        P(None, "tensor", "dp", None),
        P(None, "dp"),
        P(None, "tensor", "dp", None),
        P("section", None, None, "tensor"),
        P("section", None, "tensor"),
        P("section", "tensor", None),
        P("section", None, "tensor"),
        P("section", "tensor"),
        P("section", "tensor", None),
        P("section", None, None),
        P("section", None, None),
        P("section", None, None),
    )
    out_specs = (
        P("section", None, "tensor", "dp", None),
        P("section", None, "tensor", "dp", None),
        P("section", None, None, "tensor"),
        P("section", None, "tensor"),
        P("section", "tensor", None),
        P("section", None, "tensor"),
        P("section", "tensor"),
        P("section", "tensor", None),
        P("section", None, None),
        P("section", None, None),
        P("section", None, None),
    )
    return jax.shard_map(per_device, mesh=mesh, in_specs=in_specs, out_specs=out_specs, check_vma=False)
```

```python
import jax
import jax.numpy as jnp
from jax import lax
from jax.experimental import pallas as pl
from jax.experimental.pallas import tpu as pltpu
from jax.sharding import PartitionSpec as P

EPSILON = 1e-12
MASKED = -1e30
F32 = jnp.float32
BF16 = jnp.bfloat16
MESH = pl.DeviceIdType.MESH
INV_SQRT2 = 0.7071067811865476
INV_SQRT_2PI = 0.3989422804014327
SCALE = 0.125

PIECES = ((0, 256), (256, 512))
ALONG_Z = ((0, 128), (256, 192))
QUARTERED = ((128, 128), (448, 320))


def nt(a, b):
    return lax.dot_general(a, b, (((1,), (1,)), ((), ())), preferred_element_type=F32)


def nn(a, b):
    return lax.dot_general(a, b, (((1,), (0,)), ((), ())), preferred_element_type=F32)


def standardize(rows):
    center = jnp.mean(rows, axis=-1, keepdims=True)
    centred = rows - center
    spread = jnp.mean(centred * centred, axis=-1, keepdims=True)
    inv = lax.rsqrt(spread + EPSILON)
    return centred * inv, inv


def standardize_back(grad_out, gain, unit, inv):
    scaled = grad_out * gain
    return inv * (
        scaled
        - jnp.mean(scaled, axis=-1, keepdims=True)
        - unit * jnp.mean(scaled * unit, axis=-1, keepdims=True)
    )


def kernel(
    xs, cs, qkv_in, out_in, up_in, down_in, gains_in, shifts_in, bias_in, b_up_in, b_qv_in, len_in,
    lout, igout, gout, smout,
    valid, sv,
    W, SW, XF, YF, GF, GO, CT, PB, PT, PR, AT, HT, GD, CDF, HB, GZT, GPT, GKT, GVT,
    N1, N2, S1, S2, Y1, GR, GY, OWN,
    PART, SIB, SUM, RIN, G, GXA, GXF, QXA, QXF, ZXA, ZXF,
    LO, IG, SM, SMN, SMC, SM1, SMY, SM2, SMZ, SM3, SMX,
    ag_s, ag_r, sb_s, sb_r, rs_s, rs_r, in_s, in_r, loc, sv_s, sv_r, wz_s, wz_r, wq_s, wq_r, wx_s, wx_r,
    xr_s, xr_r, xf_s, xf_r, xa_s, xa_r, gz_s, gz_r, xg_s, xg_r, lo_s, lo_r, ig_s, ig_r,
    sc_s, sc_r, sy_s, sy_r, sz_s, sz_r, sx_s, sx_r,
):
    zh = lax.axis_index("section")
    x = lax.axis_index("dp")
    t = lax.axis_index("tensor")
    zl = t // 8
    y = (t % 8) // 2
    c = t % 2
    d = t % 8
    z = 2 * zh + zl

    def dev(zh_=None, x_=None, zl_=None, y_=None, c_=None):
        zh_ = zh if zh_ is None else zh_
        x_ = x if x_ is None else x_
        zl_ = zl if zl_ is None else zl_
        y_ = y if y_ is None else y_
        c_ = c if c_ is None else c_
        return (zh_, x_, zl_ * 8 + y_ * 2 + c_)

    def yd(r):
        return dev(y_=lax.rem(y + r, 4))

    def xd(r):
        return dev(x_=lax.rem(x + r, 4))

    sibling = dev(c_=1 - c)
    partner = dev(zl_=1 - zl)
    cross = dev(zh_=1 - zh, zl_=1 - zl)
    far = dev(zh_=1 - zh)

    def rc(src, dst, ssem, rsem, where):
        return pltpu.make_async_remote_copy(
            src_ref=src, dst_ref=dst, send_sem=ssem, recv_sem=rsem, device_id=where, device_id_type=MESH
        )

    def arrived(dst, rsem):
        rc(dst, dst, rsem, rsem, sibling).wait_recv()

    barrier = pltpu.get_barrier_semaphore()
    greeted = [sibling, yd(1), yd(2), yd(3), xd(1), xd(2), xd(3), partner, cross, far]
    for other in greeted:
        pl.semaphore_signal(barrier, inc=1, device_id=other, device_id_type=MESH)
    pl.semaphore_wait(barrier, len(greeted))

    def slot(full, l, yy, cc):
        return full.at[l, pl.ds(pl.multiple_of(yy * 128 + cc * 64, 64), 64)]

    def ag_begin(full, l, k):
        mine = slot(full, l, y, c)
        copies = [rc(mine, mine, ag_s.at[l, k, i], ag_r.at[l, k, i], yd(i)) for i in (1, 3, 2)]
        copies.append(rc(mine, mine, ag_s.at[l, k, 4], ag_r.at[l, k, 4], sibling))
        for cp in copies:
            cp.start()
        return copies

    def from_ring(full, l, k, i, copies):
        got = slot(full, l, lax.rem(y + 4 - i, 4), c)
        arrived(got, ag_r.at[l, k, i])
        cp = rc(got, got, ag_s.at[l, k, 4 + i], ag_r.at[l, k, 4 + i], sibling)
        cp.start()
        copies.append(cp)

    def from_sibling(full, l, k, i):
        arrived(slot(full, l, lax.rem(y + 4 - i, 4), 1 - c), ag_r.at[l, k, 4 + i])

    def gather(full, l, k, use):
        copies = ag_begin(full, l, k)
        from_sibling(full, l, k, 0)
        use(y)
        from_ring(full, l, k, 1, copies)
        from_ring(full, l, k, 3, copies)
        from_sibling(full, l, k, 1)
        use(lax.rem(y + 3, 4))
        from_ring(full, l, k, 2, copies)
        from_sibling(full, l, k, 3)
        use(lax.rem(y + 1, 4))
        from_sibling(full, l, k, 2)
        use(lax.rem(y + 2, 4))
        return copies

    def make(l, k, r, chunk, copies):
        PART[r] = chunk(lax.rem(y + r, 4)).astype(BF16)
        theirs = PART.at[r, pl.ds(pl.multiple_of((1 - c) * 64, 64), 64)]
        cp = rc(theirs, SIB.at[r], sb_s.at[l, k, r], sb_r.at[l, k, r], sibling)
        cp.start()
        copies.append(cp)

    def both(l, k, r):
        arrived(SIB.at[r], sb_r.at[l, k, r])
        mine = PART[r, pl.ds(pl.multiple_of(c * 64, 64), 64), :]
        return mine.astype(F32) + SIB[r].astype(F32)

    def push(l, k, r, pushes):
        SUM[r] = both(l, k, r).astype(BF16)
        cp = rc(SUM.at[r], RIN.at[r], rs_s.at[l, k, r], rs_r.at[l, k, r], yd(r))
        cp.start()
        pushes.append(cp)

    def finish(l, k, copies, pushes):
        for cp in copies:
            cp.wait_send()
        for r in (1, 3, 2):
            arrived(RIN.at[r], rs_r.at[l, k, r])
        total = OWN[...] + ((RIN[1].astype(F32) + RIN[3].astype(F32)) + RIN[2].astype(F32))
        for cp in pushes:
            cp.wait_send()
        return total

    def scatter(l, k, chunk, window, copies, midway=lambda: None):
        pushes = []
        make(l, k, 2, chunk, copies)
        make(l, k, 1, chunk, copies)
        push(l, k, 2, pushes)
        make(l, k, 3, chunk, copies)
        push(l, k, 1, pushes)
        midway()
        make(l, k, 0, chunk, copies)
        push(l, k, 3, pushes)
        OWN[...] = both(l, k, 0)
        window()
        return finish(l, k, copies, pushes)

    def gather_scatter(full, l, k, chunk, window):
        mine = slot(full, l, y, c)
        pushes = []

        def to_ring(i):
            return rc(mine, mine, ag_s.at[l, k, i], ag_r.at[l, k, i], yd(i))

        copies = [rc(mine, mine, ag_s.at[l, k, 4], ag_r.at[l, k, 4], sibling), to_ring(1), to_ring(3)]
        for cp in copies:
            cp.start()
        from_sibling(full, l, k, 0)
        make(l, k, 0, chunk, copies)
        cp = to_ring(2)
        cp.start()
        copies.append(cp)
        from_ring(full, l, k, 1, copies)
        from_ring(full, l, k, 3, copies)
        from_sibling(full, l, k, 1)
        make(l, k, 3, chunk, copies)
        from_sibling(full, l, k, 3)
        make(l, k, 1, chunk, copies)
        push(l, k, 3, pushes)
        push(l, k, 1, pushes)
        from_ring(full, l, k, 2, copies)
        from_sibling(full, l, k, 2)
        make(l, k, 2, chunk, copies)
        push(l, k, 2, pushes)
        OWN[...] = both(l, k, 0)
        window()
        return finish(l, k, copies, pushes)

    others = (far, cross, partner)

    def sv_copy(k):
        return rc(sv, SW.at[z], sv_s.at[k], sv_r.at[zh, zl], others[k])

    def wz_copy(i, k):
        rows = W.at[zh, zl, pl.ds(*ALONG_Z[i])]
        return rc(rows, rows, wz_s.at[k, i], wz_r.at[zh, zl, i], others[k])

    def quarter(l, b, i, who):
        base, size = QUARTERED[i]
        n = size // 4
        return W.at[l, b, pl.ds(pl.multiple_of(base + who * n, 16), n)]

    def wq_copy(i, k):
        rows = quarter(zh, zl, i, x)
        return rc(rows, rows, wq_s.at[k, i], wq_r.at[zh, zl, i], others[k])

    def wx_copy(l, b, i, r):
        rows = quarter(l, b, i, x)
        return rc(rows, rows, wx_s.at[l, b, i, r - 1], wx_r.at[l, b, i, r - 1], xd(r))

    def send_quarter(i):
        for k in range(3):
            wq_copy(i, k).start()

    def send_rest(i):
        for k in range(3):
            wz_copy(i, k).start()

    def send_vectors():
        for k in range(3):
            sv_copy(k).start()

    def pass_on(l, i):
        for b in range(2):
            @pl.when((2 * l + b) != z)
            def _(b=b):
                arrived(quarter(l, b, i, x), wq_r.at[l, b, i])
                for r in (2, 1, 3):
                    wx_copy(l, b, i, r).start()

    def vectors_here(l):
        for b in range(2):
            @pl.when((2 * l + b) != z)
            def _(b=b):
                arrived(SW.at[2 * l + b], sv_r.at[l, b])

    def weights_here(l, i):
        for b in range(2):
            @pl.when((2 * l + b) != z)
            def _(b=b):
                arrived(W.at[l, b, pl.ds(*ALONG_Z[i])], wz_r.at[l, b, i])
                for r in (1, 3, 2):
                    arrived(quarter(l, b, i, lax.rem(x + 4 - r, 4)), wx_r.at[l, b, i, r - 1])

    mine_rows = pl.ds(pl.multiple_of(d * 64 + zl * 32, 32), 32)
    x_copy = rc(xs.at[1 - zl], XF.at[0, mine_rows], in_s.at[0], in_r.at[0], partner)
    x_copy.start()
    c_copy = rc(cs.at[1 - zl], CT.at[zl], in_s.at[1], in_r.at[1], partner)

    own_block = W.at[zh, zl]
    loads = [
        pltpu.make_async_copy(src, own_block.at[pl.ds(base, size)], loc.at[i])
        for i, (src, base, size) in enumerate(((qkv_in, 0, 192), (out_in, 192, 64), (down_in, 512, 256)))
    ]
    for load in loads:
        load.start()
    c_copy.start()
    XF[0, mine_rows, :] = xs[zl]
    CT[zl] = cs[zl]
    first = zl == 0
    sv[0:2, :] = gains_in[...]
    sv[2:4, :] = shifts_in[...]
    sv[4:6, :] = bias_in[...]
    sv[6:8, :] = jnp.zeros((2, 1024), F32)
    sv[6:7, 0:256] = jnp.where(first, b_up_in[...], 0.0)
    sv[6:7, 256:512] = jnp.where(first, 0.0, b_up_in[...])
    for i, at in ((0, 0), (1, 128)):
        sv[7:8, at : at + 64] = jnp.where(first, b_qv_in[i : i + 1, :], 0.0)
        sv[7:8, at + 192 : at + 256] = jnp.where(first, 0.0, b_qv_in[i : i + 1, :])
    SW[z] = sv[...]
    loads[0].wait()
    loads[1].wait()

    @pl.when(zh == 0)
    def _():
        send_vectors()
        send_quarter(0)
        send_rest(0)

    own_block[256:512, :] = up_in[...].T
    loads[2].wait()
    r_ = lax.broadcasted_iota(jnp.int32, (512, 128), 0)
    position = lax.rem(r_ // 32, 2) * 256 + (r_ // 64) * 32 + lax.rem(r_, 32)
    valid[...] = jnp.where(position < len_in[zh, zl], 1.0, 0.0)
    arrived(XF.at[0, pl.ds(pl.multiple_of(d * 64 + (1 - zl) * 32, 32), 32)], in_r.at[0])

    def spread_out(rows, buf, out, s_s, s_r, l):
        buf[l] = rows.reshape(2, 32, 1024)
        for b in range(2):
            @pl.when((2 * l + b) == z)
            def _(b=b):
                out[z] = buf[l, b]

            @pl.when((2 * l + b) != z)
            def _(b=b):
                rc(buf.at[l, b], out.at[z], s_s.at[l, b], s_r.at[z], dev(zh_=l, zl_=b)).start()

    def spread_wait(buf, out, s_s, s_r):
        for k in range(1, 4):
            zz = lax.rem(z + k, 4)
            arrived(out.at[zz], s_r.at[zz])
        for l in range(2):
            for b in range(2):
                @pl.when((2 * l + b) != z)
                def _(l=l, b=b):
                    rc(buf.at[l, b], buf.at[l, b], s_s.at[l, b], s_r.at[z], sibling).wait_send()

    def row_of(l, i):
        return SW[2 * l, pl.ds(i, 1), :]

    own_rows = pl.ds(pl.multiple_of(d * 64, 64), 64)

    def out_weights(l):
        return jnp.concatenate([W[l, 0, 192:256, :], W[l, 1, 192:256, :]], axis=0)

    def qkv_weights(l):
        return jnp.concatenate([W[l, 0, 0:192, :], W[l, 1, 0:192, :]], axis=0)

    def lanes(yy):
        return pl.ds(pl.multiple_of(yy * 128, 128), 128)

    def forward_layer(l, carry):
        seen = []

        def between(yy):
            seen.append(yy)
            if len(seen) == 3:
                @pl.when((l == 0) & (zh == 0))
                def _():
                    send_quarter(1)

                @pl.when(l == 0)
                def _():
                    pass_on(0, 0)

        x_copies = gather(XF, l, 0, between)

        @pl.when((l == 0) & (zh == 0))
        def _():
            send_rest(1)

        vectors_here(l)
        weights_here(l, 0)
        qv_bias = SW[2 * l, 7:8, 0:384] + SW[2 * l + 1, 7:8, 0:384]
        proj = (nt(XF[l], qkv_weights(l)) + qv_bias).astype(BF16)
        PB[l] = proj
        PT[l] = proj.T


        def attend(yy):
            cols = lanes(yy)
            for h in range(2):
                base = h * 192
                scores = nn(PB[l, :, base + 64 : base + 128], PT[l, base : base + 64, cols]) * SCALE
                scores = jnp.where(valid[...] > 0.5, scores, MASKED)
                terms = jnp.exp(scores - jnp.max(scores, axis=0, keepdims=True))
                probs = terms * (1.0 / jnp.sum(terms, axis=0, keepdims=True))
                PR[l, h, yy] = probs
                mixed = nn(PT[l, base + 128 : base + 192, :], probs.astype(BF16))
                AT[l, h * 64 : h * 64 + 64, cols] = mixed.astype(BF16)
            return nn(AT[l, :, cols].T, out_weights(l))

        def attend_midway():
            @pl.when(l == 0)
            def _():
                pass_on(0, 1)

        def attend_window():
            @pl.when((l == 0) & (zh == 1))
            def _():
                send_vectors()
                send_quarter(0)
                send_rest(0)
                send_quarter(1)

        attended = scatter(l, 0, attend, attend_window, x_copies, attend_midway)
        unit, inv = standardize(XF[l, own_rows, :].astype(F32) + attended + row_of(l, 4))
        N1[l] = unit
        S1[l] = jnp.broadcast_to(inv, (64, 128))
        middle = unit * row_of(l, 0) + row_of(l, 2)
        Y1[...] = middle
        YF[l, own_rows, :] = middle.astype(BF16)
        weights_here(l, 1)

        up_bias = SW[2 * l, 6:7, 0:512] + SW[2 * l + 1, 6:7, 0:512]

        def feed(yy):
            rows = YF[l, lanes(yy), :]
            total = None
            for b in range(2):
                pre = nt(rows, W[l, b, 256:512, :]) + up_bias[:, b * 256 : b * 256 + 256]
                cdf = 0.5 * (1.0 + lax.erf(pre * INV_SQRT2))
                hidden = (pre * cdf).astype(BF16)
                cols = pl.ds(b * 256, 256)
                GD[l, yy, :, cols] = pre
                CDF[yy, :, cols] = cdf
                HB[yy, :, cols] = hidden
                piece = nn(hidden, W[l, b, 512:768, :])
                total = piece if total is None else total + piece
            return total

        def feed_window():
            @pl.loop(0, 4)
            def _(yy):
                HT[l, :, lanes(yy)] = HB[yy].T
                pre = GD[l, yy]
                GD[l, yy] = CDF[yy] + pre * (INV_SQRT_2PI * jnp.exp(-0.5 * pre * pre))

            @pl.when(l == 0)
            def _():
                pass_on(1, 0)
                pass_on(1, 1)

            @pl.when((l == 0) & (zh == 1))
            def _():
                send_rest(1)

        fed = gather_scatter(YF, l, 1, feed, feed_window)
        unit, inv = standardize(Y1[...] + fed + row_of(l, 5))
        N2[l] = unit
        S2[l] = jnp.broadcast_to(inv, (64, 128))
        result = (unit * row_of(l, 1) + row_of(l, 3)).astype(BF16)

        @pl.when(l == 0)
        def _():
            XF[1, own_rows, :] = result

        spread_out(result, LO, lout, lo_s, lo_r, l)
        return carry

    lax.fori_loop(0, 2, forward_layer, 0)

    arrived(CT.at[1 - zl], in_r.at[1])
    GY[...] = CT[...].reshape(64, 1024).astype(F32)
    SM[...] = jnp.zeros_like(SM)
    SMN[...] = jnp.zeros_like(SMN)
    norm_pair = rc(SMN, SMC, sc_s, sc_r, sibling)
    norm_ring = [rc(SM1, SMY.at[y], sy_s.at[r], sy_r.at[r], yd(r)) for r in range(1, 4)]

    QX, ZX = (QXA, QXF), (ZXA, ZXF)

    def own_part(p, ref, who, *lead):
        base, size = PIECES[p]
        n = size // 4
        return ref.at[(*lead, pl.ds(pl.multiple_of(base + who * n, n), n))]

    def x_copy_of(l, b, r):
        src = own_part(0, G, lax.rem(x + r, 4), l, b)
        return rc(src, GXA.at[l, b, r - 1], xr_s.at[l, b, r - 1], xr_r.at[l, b, r - 1], xd(r))

    def half_of(ref, r, half, *lead):
        start = 256 + lax.rem(x + r, 4) * 128 + half * 64
        return ref.at[(*lead, pl.ds(pl.multiple_of(start, 64), 64))]

    RING = ((2, 0, 1), (2, 1, 3), (1, 1, 1), (3, 0, 3), (1, 0, 1), (3, 1, 3))

    def ring_copy(l, b, i):
        r, half, to = RING[i]
        return rc(half_of(G, r, half, l, b), GXF.at[l, b, i], xf_s.at[l, b, i], xf_r.at[l, b, i], xd(to))

    def ring_first(l):
        for i in range(4):
            for b in range(2):
                ring_copy(l, b, i).start()

    def ring_second(l):
        for i in range(2):
            for b in range(2):
                arrived(GXF.at[l, b, i], xf_r.at[l, b, i])
                r, half, _ = RING[4 + i]
                mine = half_of(G, r, half, l, b)
                mine[...] = (mine[...].astype(F32) + GXF[l, b, i].astype(F32)).astype(BF16)
                ring_copy(l, b, 4 + i).start()

    def z_copy_of(l, p, b):
        k = lax.rem(2 * l + b + 4 - z, 4) - 1
        return rc(QX[p].at[l, b], ZX[p].at[k], gz_s.at[l, p, b], gz_r.at[p, k], dev(zh_=l, zl_=b))

    def g_copy_of(r):
        mine = own_part(0, gout, x)
        return rc(mine, mine, xg_s.at[r - 1], xg_r.at[r - 1], xd(r))

    AROUND = ((0, 0, 1), (0, 1, 3), (0, 1, 1), (0, 0, 3), (3, 0, 1), (1, 1, 3))

    def around(i):
        r, half, to = AROUND[i]
        rows = half_of(gout, r, half)
        return rc(rows, rows, xa_s.at[i], xa_r.at[i], xd(to))

    def around_here(i):
        r, half, to = AROUND[i]
        arrived(half_of(gout, r + 4 - to, half), xa_r.at[i])

    def grad_x(l):
        for b in range(2):
            for r in (2, 1, 3):
                x_copy_of(l, b, r).start()

    def grad_z(l, p):
        for b in range(2):
            mine = own_part(p, G, x, l, b)
            if p == 0:
                for r in (1, 3, 2):
                    arrived(GXA.at[l, b, r - 1], xr_r.at[l, b, r - 1])
                got = ((0, 64, tuple(GXA.at[l, b, i] for i in range(3))),)
            else:
                for i in (2, 3, 4, 5):
                    arrived(GXF.at[l, b, i], xf_r.at[l, b, i])
                got = (
                    (0, 64, (GXF.at[l, b, 3], GXF.at[l, b, 4])),
                    (64, 64, (GXF.at[l, b, 2], GXF.at[l, b, 5])),
                )
            for base, size, terms in got:
                total = mine[base : base + size, :].astype(F32)
                for term in terms:
                    total = total + term[...].astype(F32)
                QX[p][l, b, base : base + size, :] = total.astype(BF16)

            @pl.when((2 * l + b) != z)
            def _(b=b):
                z_copy_of(l, p, b).start()

    def grad_own(p):
        n = PIECES[p][1] // 4
        for k in range(3):
            arrived(ZX[p].at[k], gz_r.at[p, k])
        mine = own_part(p, gout, x)

        @pl.loop(0, n // 32)
        def _(i):
            rows = pl.ds(pl.multiple_of(i * 32, 32), 32)
            mine[rows, :] = (
                (QX[p][zh, zl, rows, :].astype(F32) + ZX[p][0, rows, :].astype(F32))
                + (ZX[p][1, rows, :].astype(F32) + ZX[p][2, rows, :].astype(F32))
            ).astype(BF16)

        if p == 0:
            for r in (2, 1, 3):
                g_copy_of(r).start()
        else:
            for i in range(4):
                around(i).start()

    def grad_done():
        for i in (0, 1):
            around_here(i)
            around(4 + i).start()
        for i in (2, 3, 4, 5):
            around_here(i)
        for r in (1, 3, 2):
            arrived(own_part(0, gout, lax.rem(x + 4 - r, 4)), xg_r.at[r - 1])

    def backward_layer(step, carry):
        l = 1 - step
        grad = GY[...]
        unit = N2[l]
        grad_second = standardize_back(grad, row_of(l, 1), unit, S2[l, :, 0:1])
        SMN[l, 1:2, :] = jnp.sum(grad * unit, axis=0, keepdims=True)
        SMN[l, 3:4, :] = jnp.sum(grad, axis=0, keepdims=True)
        SMN[l, 5:6, :] = jnp.sum(grad_second, axis=0, keepdims=True)
        GR[...] = grad_second
        GF[l, own_rows, :] = grad_second.astype(BF16)
        def feed_back(yy):
            rows = GF[l, lanes(yy), :]
            total = None
            for b in range(2):
                grad_pre = (nt(rows, W[l, b, 512:768, :]) * GD[l, yy, :, b * 256 : b * 256 + 256]).astype(BF16)
                HB[yy, :, pl.ds(b * 256, 256)] = grad_pre
                piece = nn(grad_pre, W[l, b, 256:512, :])
                total = piece if total is None else total + piece
            return total

        def feed_grads():
            @pl.loop(0, 4)
            def _(yy):
                grad_pre = HB[yy]
                GZT[:, lanes(yy)] = grad_pre.T
                SM[l, 6:7, 0:512] += jnp.sum(grad_pre.astype(F32), axis=0, keepdims=True)

            @pl.loop(0, 2)
            def _(b):
                rows = pl.ds(pl.multiple_of(b * 256, 256), 256)
                G[l, b, 256:512, :] = nn(GZT[rows, :], YF[l]).astype(BF16)
                G[l, b, 512:768, :] = nn(HT[l, rows, :], GF[l]).astype(BF16)

            ring_first(l)

            @pl.when(l == 0)
            def _():
                grad_z(1, 1)
                grad_z(1, 0)

        grad_middle = GR[...] + gather_scatter(GF, l, 2, feed_back, feed_grads)
        unit = N1[l]
        grad_first = standardize_back(grad_middle, row_of(l, 0), unit, S1[l, :, 0:1])
        SMN[l, 0:1, :] = jnp.sum(grad_middle * unit, axis=0, keepdims=True)
        SMN[l, 2:3, :] = jnp.sum(grad_middle, axis=0, keepdims=True)
        SMN[l, 4:5, :] = jnp.sum(grad_first, axis=0, keepdims=True)
        GR[...] = grad_first
        GO[l, own_rows, :] = grad_first.astype(BF16)
        GKT[...] = jnp.zeros_like(GKT)
        GVT[...] = jnp.zeros_like(GVT)

        def attend_back(yy):
            cols = lanes(yy)
            grad_mixed = nt(GO[l, cols, :], out_weights(l)).astype(BF16)
            mixed_t = grad_mixed.T
            for h in range(2):
                base = h * 192
                half = mixed_t[h * 64 : h * 64 + 64, :]
                probs = PR[l, h, yy]
                grad_prob = nn(PB[l, :, base + 128 : base + 192], half)
                inner = jnp.sum(probs * grad_prob, axis=0, keepdims=True)
                grad_score = (probs * (grad_prob - inner)).astype(BF16)
                GPT[base : base + 64, cols] = (
                    nn(PT[l, base + 64 : base + 128, :], grad_score) * SCALE
                ).astype(BF16)
                GKT[h] += nt(PT[l, base : base + 64, cols], grad_score)
                GVT[h] += nt(half, probs.astype(BF16))

        @pl.when(l == 0)
        def _():
            norm_pair.start()

        o_copies = gather(GO, l, 3, attend_back)
        ring_second(l)

        @pl.when(l == 0)
        def _():
            arrived(SMC, sc_r)
            SM1[...] = SMN[...] + SMC[...]
            SMY[y] = SM1[...]
            for cp in norm_ring:
                cp.start()


        for h in range(2):
            base = h * 192
            GPT[base + 64 : base + 128, :] = (GKT[h] * SCALE).astype(BF16)
            GPT[base + 128 : base + 192, :] = GVT[h].astype(BF16)

        def attend_grads():
            @pl.loop(0, 2)
            def _(b):
                G[l, b, 0:192, :] = nn(GPT[pl.ds(pl.multiple_of(b * 192, 64), 192), :], XF[l]).astype(BF16)
                G[l, b, 192:256, :] = nn(AT[l, pl.ds(pl.multiple_of(b * 64, 64), 64), :], GO[l]).astype(BF16)

            grad_x(l)

        pl.when(l == 0)(attend_grads)

        def project_back(yy):
            grad_proj = GPT[:, lanes(yy)].T
            SM[l, 7:8, 0:384] += jnp.sum(grad_proj.astype(F32), axis=0, keepdims=True)
            return nn(grad_proj, qkv_weights(l))

        def project_window():
            pl.when(l == 1)(attend_grads)

            @pl.when(l == 0)
            def _():
                grad_z(0, 1)

        grad_input = (GR[...] + scatter(l, 3, project_back, project_window, o_copies)).astype(BF16)
        GY[...] = grad_input.astype(F32)
        spread_out(grad_input, IG, igout, ig_s, ig_r, l)
        return carry

    lax.fori_loop(0, 2, backward_layer, 0)

    done = []

    def go(cp):
        cp.start()
        done.append(cp)

    grad_z(0, 0)
    for r in range(1, 4):
        arrived(SMY.at[lax.rem(y + 4 - r, 4)], sy_r.at[r])
    SM2[...] = ((SMY[0] + SMY[1]) + (SMY[2] + SMY[3])) + SM[...]
    SMZ[z] = SM2[zh]
    for k, where, lz in ((0, partner, zh), (1, cross, 1 - zh), (2, far, 1 - zh)):
        go(rc(SM2.at[lz], SMZ.at[z], sz_s.at[k], sz_r.at[k], where))
    grad_own(1)
    for k, zz in ((0, 2 * zh + 1 - zl), (1, 2 * (1 - zh) + 1 - zl), (2, 2 * (1 - zh) + zl)):
        arrived(SMZ.at[zz], sz_r.at[k])
    SM3[...] = (SMZ[0] + SMZ[1]) + (SMZ[2] + SMZ[3])
    SMX[x] = SM3[...]
    for r in range(1, 4):
        go(rc(SM3, SMX.at[x], sx_s.at[r], sx_r.at[r], xd(r)))
    grad_own(0)
    for r in range(1, 4):
        arrived(SMX.at[lax.rem(x + 4 - r, 4)], sx_r.at[r])
    total = (SMX[0] + SMX[1]) + (SMX[2] + SMX[3])
    first = zl == 0
    smout[...] = total
    smout[6:7, 0:256] = jnp.where(first, total[6:7, 0:256], total[6:7, 256:512])
    smout[7:8, 0:192] = jnp.where(first, total[7:8, 0:192], total[7:8, 192:384])
    spread_wait(LO, lout, lo_s, lo_r)
    spread_wait(IG, igout, ig_s, ig_r)
    grad_done()

    x_copy.wait_send()
    c_copy.wait_send()
    for k in range(3):
        sv_copy(k).wait_send()
        for i in range(2):
            wz_copy(i, k).wait_send()
            wq_copy(i, k).wait_send()
    for l in range(2):
        for b in range(2):
            @pl.when((2 * l + b) != z)
            def _(l=l, b=b):
                for i in range(2):
                    for r in range(1, 4):
                        wx_copy(l, b, i, r).wait_send()
    for l in range(2):
        for b in range(2):
            for r in range(1, 4):
                x_copy_of(l, b, r).wait_send()
            for i in range(6):
                ring_copy(l, b, i).wait_send()

            @pl.when((2 * l + b) != z)
            def _(l=l, b=b):
                for p in range(2):
                    z_copy_of(l, p, b).wait_send()
    for r in range(1, 4):
        g_copy_of(r).wait_send()
    for i in range(6):
        around(i).wait_send()
    for cp in done + [norm_pair] + norm_ring:
        cp.wait_send()


def run_kernel(*operands):
    vm = pltpu.VMEM
    dma = pltpu.SemaphoreType.DMA
    scratch = [
        vm((512, 128), F32),
        vm((8, 1024), F32),
        vm((2, 2, 768, 1024), BF16),
        vm((4, 8, 1024), F32),
        vm((2, 512, 1024), BF16),
        vm((2, 512, 1024), BF16),
        vm((2, 512, 1024), BF16),
        vm((2, 512, 1024), BF16),
        vm((2, 32, 1024), BF16),
        vm((2, 512, 384), BF16),
        vm((2, 384, 512), BF16),
        vm((2, 2, 4, 512, 128), F32),
        vm((2, 128, 512), BF16),
        vm((2, 512, 512), BF16),
        vm((2, 4, 128, 512), F32),
        vm((4, 128, 512), F32),
        vm((4, 128, 512), BF16),
        vm((512, 512), BF16),
        vm((384, 512), BF16),
        vm((2, 64, 512), F32),
        vm((2, 64, 512), F32),
        vm((2, 64, 1024), F32),
        vm((2, 64, 1024), F32),
        vm((2, 64, 128), F32),
        vm((2, 64, 128), F32),
        vm((64, 1024), F32),
        vm((64, 1024), F32),
        vm((64, 1024), F32),
        vm((64, 1024), F32),
        vm((4, 128, 1024), BF16),
        vm((4, 64, 1024), BF16),
        vm((4, 64, 1024), BF16),
        vm((4, 64, 1024), BF16),
        vm((2, 2, 768, 1024), BF16),
        vm((2, 2, 3, 64, 1024), BF16),
        vm((2, 2, 6, 64, 1024), BF16),
        vm((2, 2, 64, 1024), BF16),
        vm((2, 2, 128, 1024), BF16),
        vm((3, 64, 1024), BF16),
        vm((3, 128, 1024), BF16),
        vm((2, 2, 32, 1024), BF16),
        vm((2, 2, 32, 1024), BF16),
        vm((2, 8, 1024), F32),
        vm((2, 8, 1024), F32),
        vm((2, 8, 1024), F32),
        vm((2, 8, 1024), F32),
        vm((4, 2, 8, 1024), F32),
        vm((2, 8, 1024), F32),
        vm((4, 8, 1024), F32),
        vm((8, 1024), F32),
        vm((4, 8, 1024), F32),
        dma((2, 4, 8)),
        dma((2, 4, 8)),
        dma((2, 4, 4)),
        dma((2, 4, 4)),
        dma((2, 4, 4)),
        dma((2, 4, 4)),
        dma((2,)),
        dma((2,)),
        dma((3,)),
        dma((3,)),
        dma((2, 2)),
        dma((3, 2)),
        dma((2, 2, 2)),
        dma((3, 2)),
        dma((2, 2, 2)),
        dma((2, 2, 2, 3)),
        dma((2, 2, 2, 3)),
        dma((2, 2, 3)),
        dma((2, 2, 3)),
        dma((2, 2, 6)),
        dma((2, 2, 6)),
        dma((6,)),
        dma((6,)),
        dma((2, 2, 2)),
        dma((2, 3)),
        dma((3,)),
        dma((3,)),
        dma((2, 2)),
        dma((4,)),
        dma((2, 2)),
        dma((4,)),
        dma(()),
        dma(()),
        dma((4,)),
        dma((4,)),
        dma((3,)),
        dma((3,)),
        dma((4,)),
        dma((4,)),
    ]
    in_vmem = pl.BlockSpec(memory_space=pltpu.VMEM)
    hbm = pl.BlockSpec(memory_space=pl.ANY)
    return pl.pallas_call(
        kernel,
        out_shape=(
            jax.ShapeDtypeStruct((4, 32, 1024), BF16),
            jax.ShapeDtypeStruct((4, 32, 1024), BF16),
            jax.ShapeDtypeStruct((768, 1024), BF16),
            jax.ShapeDtypeStruct((8, 1024), F32),
        ),
        in_specs=[in_vmem] * 2 + [hbm] * 2 + [in_vmem, hbm] + [in_vmem] * 5 + [pl.BlockSpec(memory_space=pltpu.SMEM)],
        out_specs=(in_vmem,) * 4,
        scratch_shapes=scratch,
        compiler_params=pltpu.CompilerParams(
            collective_id=0, has_side_effects=True, vmem_limit_bytes=60 * 1024 * 1024
        ),
        cost_estimate=pl.CostEstimate(flops=10_000_000_000, bytes_accessed=10_000_000, transcendentals=3_000_000),
    )(*operands)


def place_kernel(
    lout_in, igout_in, gout_in, sm_in,
    out, grad_in, qkv, qv, w_out, up, up_bias, down, gains, shifts, bias,
    lout, igout, gout, sm, sems,
):
    pairs = ((gout_in, gout), (igout_in, igout), (lout_in, lout), (sm_in, sm))
    loads = [pltpu.make_async_copy(src, dst, sems.at[i]) for i, (src, dst) in enumerate(pairs)]
    for load in loads:
        load.start()
    for load in loads:
        load.wait()
    for m in range(2):
        for q in range(2):
            grad_in[0, m, :, q, :] = igout[2 * m + q].astype(F32)
    out[0] = jnp.transpose(lout[...].reshape(2, 2, 32, 1024), (0, 2, 1, 3))
    qkv[...] = gout[0:192, :].astype(F32)
    w_out[0] = gout[192:256, :].astype(F32)
    up[0] = gout[256:512, :].astype(F32).T
    down[0] = gout[512:768, :].astype(F32)
    gains[0] = sm[0:2, :]
    shifts[0] = sm[2:4, :]
    bias[0] = sm[4:6, :]
    up_bias[...] = sm[6:7, 0:256]
    qv[0, 0:1, :] = sm[7:8, 0:64]
    qv[0, 1:2, :] = sm[7:8, 128:192]


def place_outputs(lout, igout, gout, sm):
    vmem = pl.BlockSpec(memory_space=pltpu.VMEM)

    def f32(*shape):
        return jax.ShapeDtypeStruct(shape, F32)

    return pl.pallas_call(
        place_kernel,
        out_shape=(
            jax.ShapeDtypeStruct((1, 2, 32, 2, 1024), BF16), f32(1, 2, 32, 2, 1024), f32(192, 1024), f32(1, 2, 64),
            f32(1, 64, 1024), f32(1, 1024, 256), f32(1, 256), f32(1, 256, 1024),
            f32(1, 2, 1024), f32(1, 2, 1024), f32(1, 2, 1024),
        ),
        in_specs=[pl.BlockSpec(memory_space=pl.ANY)] * 4,
        out_specs=(vmem,) * 11,
        scratch_shapes=[
            pltpu.VMEM((4, 32, 1024), BF16),
            pltpu.VMEM((4, 32, 1024), BF16),
            pltpu.VMEM((768, 1024), BF16),
            pltpu.VMEM((8, 1024), F32),
            pltpu.SemaphoreType.DMA((4,)),
        ],
        compiler_params=pltpu.CompilerParams(vmem_limit_bytes=60 * 1024 * 1024),
        cost_estimate=pl.CostEstimate(flops=1_000_000, bytes_accessed=6_000_000, transcendentals=0),
    )(lout, igout, gout, sm)


def per_device(
    inputs, lengths, cotangent, w_qkv, b_qv, w_out, w_up, b_up, w_down, norm_gains, norm_shifts, out_bias
):
    zh = lax.axis_index("section")
    zl = lax.axis_index("tensor") // 8
    xs = jnp.transpose(lax.dynamic_index_in_dim(inputs, zh, 0, keepdims=False), (1, 0, 2))
    cs = jnp.transpose(lax.dynamic_index_in_dim(cotangent, zh, 0, keepdims=False), (1, 0, 2))
    qkv_rows = jnp.transpose(w_qkv[0], (1, 2, 0)).reshape(192, 1024)
    out, grad_in, qkv, qv, g_out, up, up_bias, down, gains, shifts, bias = place_outputs(
        *run_kernel(
            xs, cs, qkv_rows, w_out[0], w_up[0], w_down[0],
            norm_gains[0], norm_shifts[0], out_bias[0], b_up, b_qv[0], lengths,
        )
    )
    grad_qkv = jnp.transpose(qkv.reshape(3, 64, 1024), (2, 0, 1))[None]
    return (out, grad_in, grad_qkv, qv, g_out, up, up_bias, down, gains, shifts, bias)


def solution(mesh):
    in_specs = (
        P(None, "tensor", "dp", None),
        P(None, "dp"),
        P(None, "tensor", "dp", None),
        P("section", None, None, "tensor"),
        P("section", None, "tensor"),
        P("section", "tensor", None),
        P("section", None, "tensor"),
        P("section", "tensor"),
        P("section", "tensor", None),
        P("section", None, None),
        P("section", None, None),
        P("section", None, None),
    )
    out_specs = (
        P("section", None, "tensor", "dp", None),
        P("section", None, "tensor", "dp", None),
        P("section", None, None, "tensor"),
        P("section", None, "tensor"),
        P("section", "tensor", None),
        P("section", None, "tensor"),
        P("section", "tensor"),
        P("section", "tensor", None),
        P("section", None, None),
        P("section", None, None),
        P("section", None, None),
    )
    return jax.shard_map(per_device, mesh=mesh, in_specs=in_specs, out_specs=out_specs, check_vma=False)
```
